32 devices in a mesh: dp: 8 (over z, x), tensor: 4 (over y, core).
Axes of the slice: x: 2, y: 2, z: 4, core: 2. Of those that a mesh axis runs over, the one named last changes fastest.
Arguments:
- tokens: bfloat16 [16384, 768], P(('dp', 'tensor')), may hold values from -6 to 6
- seg_lengths: int32 [8, 13], P('dp'), may hold values from 32 to 1024, as said below
- parents: int32 [8, 13], P('dp'), may hold values from 0 to 4, as said below
- qkv_latent: float32 [768, 3, 768], P(None, None, 'tensor'), may hold values from -0.3125 to 0.3125
- qv_bias: bfloat16 [2, 768], P(None, 'tensor'), may hold values from -3 to 3
- out_latent: float32 [768, 768], P('tensor'), may hold values from -1.75 to 1.75
- out_bias: bfloat16 [768], replicated, may hold values from -3 to 3
- norm1_gain: bfloat16 [768], replicated, may hold values from 0.5 to 1.5
- norm1_shift: bfloat16 [768], replicated, may hold values from -3 to 3
- up_latent: float32 [768, 3072], P(None, 'tensor'), may hold values from -0.21875 to 0.21875
- up_bias: bfloat16 [3072], P('tensor'), may hold values from -3 to 3
- down_latent: float32 [3072, 768], P('tensor'), may hold values from -0.109375 to 0.109375
- down_bias: bfloat16 [768], replicated, may hold values from -3 to 3
- norm2_gain: bfloat16 [768], replicated, may hold values from 0.5 to 1.5
- norm2_shift: bfloat16 [768], replicated, may hold values from -3 to 3
- teacher_qkv: bfloat16 [768, 3, 768], P(None, None, 'tensor'), may hold values from -0.3125 to 0.3125
- teacher_qv_bias: bfloat16 [2, 768], P(None, 'tensor'), may hold values from -3 to 3
- teacher_out: bfloat16 [768, 768], P('tensor'), may hold values from -1.75 to 1.75
- teacher_out_bias: bfloat16 [768], replicated, may hold values from -3 to 3
- teacher_norm1_gain: bfloat16 [768], replicated, may hold values from 0.5 to 1.5
- teacher_norm1_shift: bfloat16 [768], replicated, may hold values from -3 to 3
- teacher_up: bfloat16 [768, 3072], P(None, 'tensor'), may hold values from -0.21875 to 0.21875
- teacher_up_bias: bfloat16 [3072], P('tensor'), may hold values from -3 to 3
- teacher_down: bfloat16 [3072, 768], P('tensor'), may hold values from -0.109375 to 0.109375
- teacher_down_bias: bfloat16 [768], replicated, may hold values from -3 to 3
- teacher_norm2_gain: bfloat16 [768], replicated, may hold values from 0.5 to 1.5
- teacher_norm2_shift: bfloat16 [768], replicated, may hold values from -3 to 3
Outputs:
- output: bfloat16 [16384, 768], P(('dp', 'tensor'))
- loss: float32 [8], P('dp')
- input_grad: float32 [16384, 768], P(('dp', 'tensor'))
- qkv_latent_grad: float32 [768, 3, 768], P(None, None, 'tensor')
- qv_bias_grad: float32 [2, 768], P(None, 'tensor')
- out_latent_grad: float32 [768, 768], P('tensor')
- out_bias_grad: float32 [768], replicated
- norm1_gain_grad: float32 [768], replicated
- norm1_shift_grad: float32 [768], replicated
- up_latent_grad: float32 [768, 3072], P(None, 'tensor')
- up_bias_grad: float32 [3072], P('tensor')
- down_latent_grad: float32 [3072, 768], P('tensor')
- down_bias_grad: float32 [768], replicated
- norm2_gain_grad: float32 [768], replicated
- norm2_shift_grad: float32 [768], replicated
The draws below stay inside these ranges and needn't reach their ends.
Inputs may be any that keep to these rules, and one draw needn't show every extreme that they name: `seg_lengths`: segments of a tree lie in order: segment 0 is the trunk with exactly 1024 tokens, then 4 branches whose lengths taken in pairs sum to 256, then 4 * 2 leaves whose lengths taken in pairs sum to 128; the lengths of a tree sum to 2048. `parents`: the trunk's and every branch's parent is 0; every leaf's parent is a branch, and each branch is the parent of exactly 2 leaves.
All inputs are finite; a program needn't handle non-finite values.
Results may differ from the reference program's by a relative error of at most 0.014.
The reference program's roundings to bfloat16 on the way count: a program that leaves them out, or rounds other values in their place, can miss the bound.
Values may be sent and summed in bfloat16 or wider, within the bound.
A program may use at most 128 MiB of HBM per device.

```python
import jax
import jax.numpy as jnp
from jax import lax

D = 768
HEADS = 12
HEAD_DIM = 64
FF = 3072
TRUNK = 1024
BRANCHES = 4
BRANCH = 128
KIDS = 2
LEAF = 64
TREE = 2048
TREES = 8
TOKENS = 16384
BLOCK = 512


def draw_seg_lengths(key, part):
    key_branch, key_leaf = jax.random.split(key)
    branch_half = BRANCH // 2
    leaf_half = LEAF // 2
    branch_sizes = jax.random.randint(key_branch, (TREES, BRANCHES // 2), BRANCH - branch_half, BRANCH + branch_half + 1)
    leaf_sizes = jax.random.randint(key_leaf, (TREES, BRANCHES * KIDS // 2), LEAF - leaf_half, LEAF + leaf_half + 1)
    trunk_sizes = jnp.full((TREES, 1), TRUNK, jnp.int32)
    joined = jnp.concatenate([trunk_sizes, branch_sizes, 2 * BRANCH - branch_sizes, leaf_sizes, 2 * LEAF - leaf_sizes], axis=1)
    return joined.astype(jnp.int32)


def draw_parents(key, part):
    tree_keys = jax.random.split(key, TREES)
    orders = jax.vmap(lambda tree_key: jax.random.permutation(tree_key, BRANCHES * KIDS))(tree_keys)
    leaf_parents = (1 + orders % BRANCHES).astype(jnp.int32)
    upper = jnp.zeros((TREES, 1 + BRANCHES), jnp.int32)
    return jnp.concatenate([upper, leaf_parents], axis=1)


def block_scale(stream_key, dims, cuts, low, top_value):
    def one(dim, parts):
        steps = jax.random.uniform(jax.random.fold_in(jax.random.fold_in(stream_key, 6), dim), (parts,), jnp.float32, low / len(cuts), top_value / len(cuts))
        return jnp.repeat(jnp.exp(steps), dims[dim] // parts).reshape((-1,) + (1,) * (len(dims) - dim - 1))

    loudness = one(*cuts[0])
    for cut in cuts[1:]:
        loudness = loudness * one(*cut)
    return loudness


def noise(stream_key, extent, deviation, limit, cuts=(), kind=jnp.bfloat16):
    drawn = deviation * jax.random.normal(stream_key, extent, jnp.float32)
    if cuts:
        drawn = drawn * block_scale(stream_key, extent, cuts, -0.22, 0.18)
    return jnp.clip(drawn, -limit, limit).astype(kind)


def setup_inputs(seed: int = 0) -> dict:
    splits = jax.random.split(jax.random.key(seed), 28)
    tokens = noise(splits[0], (TOKENS, D), 1.0, 6.0, ((0, 32),))
    seg_lengths = draw_seg_lengths(jax.random.fold_in(splits[27], 71), 0)
    parents = draw_parents(jax.random.fold_in(splits[27], 71), 0)
    qkv_latent = noise(splits[3], (D, 3, D), (D // 2) ** -0.5, 0.3125, ((2, 4),), jnp.float32)
    qv_bias = noise(splits[4], (2, D), 0.5, 3.0, ((1, 4),))
    out_latent = noise(splits[5], (D, D), (D // 64) ** -0.5, 1.75, ((0, 4),), jnp.float32)
    out_bias = noise(splits[6], (D,), 0.5, 3.0)
    norm1_gain = jnp.clip(1.0 + 0.1 * jax.random.normal(splits[7], (D,), jnp.float32), 0.5, 1.5).astype(jnp.bfloat16)
    norm1_shift = noise(splits[8], (D,), 0.5, 3.0)
    up_latent = noise(splits[9], (D, FF), D ** -0.5, 0.21875, ((1, 4),), jnp.float32)
    up_bias = noise(splits[10], (FF,), 0.5, 3.0, ((0, 4),))
    down_latent = noise(splits[11], (FF, D), FF ** -0.5, 0.109375, ((0, 4),), jnp.float32)
    down_bias = noise(splits[12], (D,), 0.5, 3.0)
    norm2_gain = jnp.clip(1.0 + 0.1 * jax.random.normal(splits[13], (D,), jnp.float32), 0.5, 1.5).astype(jnp.bfloat16)
    norm2_shift = noise(splits[14], (D,), 0.5, 3.0)
    teacher_qkv = noise(splits[15], (D, 3, D), (D // 2) ** -0.5, 0.3125, ((2, 4),))
    teacher_qv_bias = noise(splits[16], (2, D), 0.5, 3.0, ((1, 4),))
    teacher_out = noise(splits[17], (D, D), (D // 64) ** -0.5, 1.75, ((0, 4),))
    teacher_out_bias = noise(splits[18], (D,), 0.5, 3.0)
    teacher_norm1_gain = jnp.clip(1.0 + 0.1 * jax.random.normal(splits[19], (D,), jnp.float32), 0.5, 1.5).astype(jnp.bfloat16)
    teacher_norm1_shift = noise(splits[20], (D,), 0.5, 3.0)
    teacher_up = noise(splits[21], (D, FF), D ** -0.5, 0.21875, ((1, 4),))
    teacher_up_bias = noise(splits[22], (FF,), 0.5, 3.0, ((0, 4),))
    teacher_down = noise(splits[23], (FF, D), FF ** -0.5, 0.109375, ((0, 4),))
    teacher_down_bias = noise(splits[24], (D,), 0.5, 3.0)
    teacher_norm2_gain = jnp.clip(1.0 + 0.1 * jax.random.normal(splits[25], (D,), jnp.float32), 0.5, 1.5).astype(jnp.bfloat16)
    teacher_norm2_shift = noise(splits[26], (D,), 0.5, 3.0)
    return {"tokens": tokens, "seg_lengths": seg_lengths, "parents": parents, "qkv_latent": qkv_latent, "qv_bias": qv_bias, "out_latent": out_latent, "out_bias": out_bias, "norm1_gain": norm1_gain, "norm1_shift": norm1_shift, "up_latent": up_latent, "up_bias": up_bias, "down_latent": down_latent, "down_bias": down_bias, "norm2_gain": norm2_gain, "norm2_shift": norm2_shift, "teacher_qkv": teacher_qkv, "teacher_qv_bias": teacher_qv_bias, "teacher_out": teacher_out, "teacher_out_bias": teacher_out_bias, "teacher_norm1_gain": teacher_norm1_gain, "teacher_norm1_shift": teacher_norm1_shift, "teacher_up": teacher_up, "teacher_up_bias": teacher_up_bias, "teacher_down": teacher_down, "teacher_down_bias": teacher_down_bias, "teacher_norm2_gain": teacher_norm2_gain, "teacher_norm2_shift": teacher_norm2_shift}


CLIP_RANGE = 3.0
NORM_EPSILON = 1e-05
MASKED_SCORE = -1e+30
HIGHEST = lax.Precision.HIGHEST

@jax.custom_vjp
def low(v):
    return lax.optimization_barrier(v.astype(jnp.bfloat16)).astype(jnp.float32)

@jax.custom_vjp
def low_back(v):
    return v

def low_keep(v):
    return (low(v), None)

def low_pass(kept, grad):
    return (grad,)

def back_keep(v):
    return (v, None)

def back_low(kept, grad):
    return (low(grad),)
low.defvjp(low_keep, low_pass)
low_back.defvjp(back_keep, back_low)

def clip_act(values):
    return CLIP_RANGE * jnp.tanh(values / CLIP_RANGE)

def layer_norm(hidden, gain, shift):
    row_mean = lax.optimization_barrier(jnp.mean(hidden, axis=-1, keepdims=True))
    centred = hidden - row_mean
    variance = lax.optimization_barrier(jnp.mean(centred * centred, axis=-1, keepdims=True))
    return centred * lax.rsqrt(variance + NORM_EPSILON) * gain + shift

def token_links(lengths, parent):
    seg_ends = jnp.cumsum(lengths).astype(jnp.int32)
    starts = (seg_ends - lengths).astype(jnp.int32)
    positions = jnp.arange(TREE, dtype=jnp.int32)
    seg_ids = lax.optimization_barrier(jnp.sum((positions[:, None] >= starts[None, :]).astype(jnp.int32), axis=1)).astype(jnp.int32) - 1
    grand_parent = parent[parent]
    return (seg_ids, parent[seg_ids], grand_parent[seg_ids])

def path_mask(row_links, col_links):
    row_seg, row_one, row_two = row_links
    col_seg, col_one, col_two = col_links
    allowed = (col_seg[None, :] == row_seg[:, None]) | (col_seg[None, :] == row_one[:, None])
    allowed = allowed | (col_seg[None, :] == row_two[:, None]) | (col_one[None, :] == row_seg[:, None])
    return allowed | (col_two[None, :] == row_seg[:, None])

def attend(queries, key_rows, values, links):
    blocks = TREE // BLOCK
    query_blocks = queries.reshape(blocks, BLOCK, HEADS, HEAD_DIM)
    row_parts = tuple((element.reshape(blocks, BLOCK) for element in links))

    @jax.checkpoint
    def one_block(inputs):
        query_block, row_seg, row_one, row_two = inputs
        scores = low_back(jnp.einsum('qhd,khd->hqk', query_block, key_rows, precision=HIGHEST) * 0.125)
        allowed = path_mask((row_seg, row_one, row_two), links)
        scores = jnp.where(allowed[None], scores, MASKED_SCORE)
        weights = jax.nn.softmax(scores, axis=-1)
        return jnp.einsum('hqk,khd->qhd', low(weights), values, precision=HIGHEST)
    context = lax.map(one_block, (query_blocks,) + row_parts)
    return context.reshape(TREE, HEADS * HEAD_DIM)

def split_heads(array):
    return array.reshape(TREE, HEADS, HEAD_DIM)

def student(tokens, params, links):
    qkv_weight, qv_bias, out_weight, out_bias, gain_one, shift_one, up_weight, up_bias, down_weight, down_bias, gain_two, shift_two = params
    inputs = low(clip_act(tokens))
    projected = jnp.einsum('td,dcf->tcf', inputs, low(qkv_weight), precision=HIGHEST)
    queries = low(low_back(projected[:, 0] + qv_bias[0]))
    key_rows = low(low_back(projected[:, 1]))
    values = low(low_back(projected[:, 2] + qv_bias[1]))
    context = low_back(attend(split_heads(queries), split_heads(key_rows), split_heads(values), links))
    attention = low_back(jnp.dot(low(clip_act(context)), low(out_weight), precision=HIGHEST) + out_bias)
    normed_one = layer_norm(tokens + attention, gain_one, shift_one)
    upward = low_back(jnp.dot(low(clip_act(normed_one)), low(up_weight), precision=HIGHEST) + up_bias)
    hidden = low(clip_act(jax.nn.gelu(upward, approximate=False)))
    forward = low_back(jnp.dot(hidden, low(down_weight), precision=HIGHEST) + down_bias)
    return layer_norm(normed_one + forward, gain_two, shift_two)

def teacher(tokens, params, links):
    qkv_weight, qv_bias, out_weight, out_bias, gain_one, shift_one, up_weight, up_bias, down_weight, down_bias, gain_two, shift_two = params
    projected = jnp.einsum('td,dcf->tcf', tokens, qkv_weight, precision=HIGHEST)
    queries = low(projected[:, 0] + qv_bias[0])
    key_rows = low(projected[:, 1])
    values = low(projected[:, 2] + qv_bias[1])
    context = attend(split_heads(queries), split_heads(key_rows), split_heads(values), links)
    attention = jnp.dot(low(context), out_weight, precision=HIGHEST) + out_bias
    normed_one = layer_norm(tokens + attention, gain_one, shift_one)
    upward = jnp.dot(low(normed_one), up_weight, precision=HIGHEST) + up_bias
    hidden = low(jax.nn.gelu(upward, approximate=False))
    forward = jnp.dot(hidden, down_weight, precision=HIGHEST) + down_bias
    return layer_norm(normed_one + forward, gain_two, shift_two)

def binary(latent):
    return lax.optimization_barrier(jnp.mean(jnp.abs(latent), axis=0)) * jnp.sign(latent)

def widen(array):
    return array.astype(jnp.float32)

def reference(tokens, seg_lengths, parents, qkv_latent, qv_bias, out_latent, out_bias, norm1_gain, norm1_shift, up_latent, up_bias, down_latent, down_bias, norm2_gain, norm2_shift, teacher_qkv, teacher_qv_bias, teacher_out, teacher_out_bias, teacher_norm1_gain, teacher_norm1_shift, teacher_up, teacher_up_bias, teacher_down, teacher_down_bias, teacher_norm2_gain, teacher_norm2_shift):
    params = (binary(qkv_latent), widen(qv_bias), binary(out_latent), widen(out_bias), widen(norm1_gain), widen(norm1_shift), binary(up_latent), widen(up_bias), binary(down_latent), widen(down_bias), widen(norm2_gain), widen(norm2_shift))
    teacher_params = tuple((widen(array) for array in (teacher_qkv, teacher_qv_bias, teacher_out, teacher_out_bias, teacher_norm1_gain, teacher_norm1_shift, teacher_up, teacher_up_bias, teacher_down, teacher_down_bias, teacher_norm2_gain, teacher_norm2_shift)))
    trees = widen(tokens).reshape(TREES, TREE, D)

    def per_tree(totals, inputs):
        tree_tokens, lengths, parent = inputs
        links = token_links(lengths, parent)

        def both_layers(source, weights):
            return (student(source, weights, links), teacher(source, teacher_params, links))
        (output, target), pull_back = jax.vjp(both_layers, tree_tokens, params)
        mismatch = output - target
        input_grad, weight_grads = pull_back((mismatch, jnp.zeros_like(target)))
        totals = jax.tree.map(jnp.add, totals, weight_grads)
        return (totals, (output.astype(jnp.bfloat16), jnp.mean(mismatch * mismatch), input_grad))
    zero_grads = jax.tree.map(jnp.zeros_like, params)
    gradients, (outputs, losses, input_grads) = lax.scan(per_tree, zero_grads, (trees, seg_lengths, parents))
    return (outputs.reshape(TOKENS, D), losses, input_grads.reshape(TOKENS, D), gradients[0], gradients[1], gradients[2], gradients[3], gradients[4], gradients[5], gradients[6], gradients[7], gradients[8], gradients[9], gradients[10], gradients[11])
```

```python
import functools

import jax
import jax.numpy as jnp
from jax import lax
from jax.experimental import pallas as pl
from jax.experimental.pallas import tpu as pltpu
from jax.sharding import PartitionSpec as P

HEAD_DIM = 64
LANES = 128
CLIP_RANGE = 3.0
NORM_EPSILON = 1e-05
MASKED_SCORE = -1e30
SEG_LANE = HEAD_DIM
ROW_TERM = HEAD_DIM + 16
Q_BLOCK = 256
BF16, F32 = jnp.bfloat16, jnp.float32
ROWS_ROWS = (((0,), (0,)), ((), ()))
COLS_COLS = (((1,), (1,)), ((), ()))


def clip_act(values):
    return CLIP_RANGE * jnp.tanh(values / CLIP_RANGE)


def clip_slope(values):
    level = jnp.tanh(values / CLIP_RANGE)
    return 1.0 - level * level


def gelu_slope(upward):
    normal_cdf = 0.5 * (1.0 + lax.erf(upward * 0.7071067811865476))
    density = jnp.exp(-0.5 * upward * upward) * 0.3989422804014327
    return normal_cdf + upward * density


def norm_forward(hidden, gain, shift):
    row_mean = jnp.mean(hidden, axis=-1, keepdims=True)
    centred = hidden - row_mean
    inv_std = lax.rsqrt(jnp.mean(centred * centred, axis=-1, keepdims=True) + NORM_EPSILON)
    normed = centred * inv_std
    return (normed * gain + shift, normed, inv_std)


def norm_backward(grad_out, normed, inv_std, gain):
    grad_normed = grad_out * gain
    centre = jnp.mean(grad_normed, axis=-1, keepdims=True)
    inner_sum = jnp.mean(grad_normed * normed, axis=-1, keepdims=True)
    grad_in = inv_std * (grad_normed - centre - normed * inner_sum)
    return (grad_in, jnp.sum(grad_out * normed, axis=0), jnp.sum(grad_out, axis=0))


def dot(left, right):
    return jnp.dot(left, right, preferred_element_type=F32)


def dot_rows(left, right):
    return lax.dot_general(left, right, ROWS_ROWS, preferred_element_type=F32)


def dot_cols(left, right):
    return lax.dot_general(left, right, COLS_COLS, preferred_element_type=F32)


def swap(array, bit):
    size = lax.axis_size("tensor")
    return lax.ppermute(array, "tensor", [(i, i ^ bit) for i in range(size)])


def gather_blocks(own):
    far = swap(own, 2)
    near = swap(own, 1)
    return [own, near, far, swap(far, 1)]


def exchange_blocks(blocks):
    far = swap(jnp.stack([blocks[2], blocks[3]]), 2)
    near = swap(jnp.stack([blocks[1], far[1]]), 1)
    return [blocks[0], near[0], far[0], near[1]]


def reduce_blocks(blocks):
    near = swap(jnp.stack([blocks[1], blocks[3]]).astype(BF16), 1).astype(F32)
    far = swap((blocks[2] + near[1]).astype(BF16), 2).astype(F32)
    return blocks[0] + near[0] + far


def sum_small(array):
    array = array + swap(array, 1)
    return array + swap(array, 2)


def lookup(indices, lookup_table):
    labels = jnp.arange(lookup_table.shape[0], dtype=jnp.int32)
    picked = jnp.where(indices[:, None] == labels[None, :], lookup_table[None, :], 0)
    return jnp.sum(picked, axis=1)


def segment_features(lengths, parent, positions):
    count = lengths.shape[0]
    labels = jnp.arange(count, dtype=jnp.int32)
    starts = jnp.sum(jnp.where(labels[None, :] < labels[:, None], lengths[None, :], 0), axis=1)
    seg_ids = jnp.sum((positions[:, None] >= starts[None, :]).astype(jnp.int32), axis=1) - 1
    grand_parent = lookup(parent, parent)
    one, two = parent, grand_parent
    row, col = labels[:, None], labels[None, :]
    allowed = (col == row) | (col == one[:, None]) | (col == two[:, None])
    allowed = allowed | (one[None, :] == row) | (two[None, :] == row)
    blocked = (~allowed).astype(F32)
    onehot = (seg_ids[:, None] == labels[None, :]).astype(F32)
    query_part = onehot * MASKED_SCORE
    key_part = dot(onehot.astype(BF16), blocked.astype(BF16))
    rows = positions.shape[0]
    pad = jnp.zeros((rows, 16 - count), F32)
    left = jnp.zeros((rows, HEAD_DIM), F32)
    right = jnp.zeros((rows, LANES - HEAD_DIM - 16), F32)
    ones = jnp.ones((rows, 3), F32)
    none = jnp.zeros((rows, LANES - HEAD_DIM - 19), F32)
    return jnp.concatenate(
        [
            left, query_part, pad, right,
            left, key_part, pad, ones, none,
            left, pad * 0.0, jnp.zeros((rows, count), F32), ones, none,
        ],
        axis=1,
    ).astype(BF16)


def split_three(values, rounded=lambda part: part.astype(BF16).astype(F32)):
    first = rounded(values)
    second = rounded(values - first)
    return first, second, rounded(values - first - second)


def to_bf16_grid(values):
    return lax.reduce_precision(values, exponent_bits=8, mantissa_bits=7)


def forward_kernel(x_ref, w_ref, b_ref, f_ref, qkv_ref, ctx_ref, keys, vals_t, *, keep):
    rows = x_ref.shape[0]
    proj = dot(x_ref[...], w_ref[0])
    proj = (proj + b_ref[0]).astype(BF16) + f_ref[...]
    queries = proj[:, :LANES]
    qkv_ref[...] = proj
    keys[...] = proj[:, LANES : 2 * LANES]
    vals_t[...] = proj[:, 2 * LANES :].T
    scores = []
    for start in range(0, rows, Q_BLOCK):
        scores.append(dot_cols(keys[...], queries[start : start + Q_BLOCK]))
    for index, block in enumerate(scores):
        part = slice(index * Q_BLOCK, (index + 1) * Q_BLOCK)
        peak = jnp.max(block, axis=0, keepdims=True)
        raised = jnp.exp(block - peak)
        total = jnp.sum(raised, axis=0, keepdims=True)
        weights = (raised * (1.0 / total)).astype(BF16)
        context = dot(vals_t[...], weights)
        ctx_ref[0, part, :] = context[:HEAD_DIM].T
        if keep:
            first, second, third = split_three(-(peak + jnp.log(total)))
            lane = lax.broadcasted_iota(jnp.int32, (LANES, Q_BLOCK), 0)
            spread = jnp.where(lane == ROW_TERM, first, 0.0)
            spread = jnp.where(lane == ROW_TERM + 1, second, spread)
            spread = jnp.where(lane == ROW_TERM + 2, third, spread)
            qkv_ref[part, :LANES] = queries[part] + spread.T.astype(BF16)


def attend_forward(source, weight, bias, features, keep):
    rows, width = source.shape
    heads = weight.shape[0]
    cols = 3 * LANES
    return pl.pallas_call(
        functools.partial(forward_kernel, keep=keep),
        grid=(heads,),
        in_specs=[
            pl.BlockSpec((rows, width), lambda h: (0, 0)),
            pl.BlockSpec((1, width, cols), lambda h: (h, 0, 0)),
            pl.BlockSpec((1, 1, cols), lambda h: (h, 0, 0)),
            pl.BlockSpec((rows, cols), lambda h: (0, 0)),
        ],
        out_specs=[
            pl.BlockSpec((rows, cols), lambda h: (0, h)),
            pl.BlockSpec((1, rows, HEAD_DIM), lambda h: (h, 0, 0)),
        ],
        out_shape=[
            jax.ShapeDtypeStruct((rows, heads * cols), BF16),
            jax.ShapeDtypeStruct((heads, rows, HEAD_DIM), F32),
        ],
        scratch_shapes=[pltpu.VMEM((rows, LANES), BF16), pltpu.VMEM((LANES, rows), BF16)],
        compiler_params=pltpu.CompilerParams(vmem_limit_bytes=56 * 2**20),
        cost_estimate=pl.CostEstimate(
            flops=16 * heads * rows * rows * HEAD_DIM,
            bytes_accessed=2 * rows * (width + 2 * heads * cols),
            transcendentals=heads * rows * rows,
        ),
        name="attend_forward",
    )(source, weight, bias, features)


def backward_kernel(qkv_ref, g_ref, dq_ref, dk_ref, dv_ref, keys_t, *, key_block):
    rows = g_ref.shape[0]
    queries = qkv_ref[:, :LANES]
    grads = g_ref[...]
    keys_t[...] = qkv_ref[:, LANES : 2 * LANES].T
    total = None
    for start in range(0, rows, key_block):
        part = slice(start, start + key_block)
        weights = jnp.exp(dot_cols(qkv_ref[part, LANES : 2 * LANES], queries))
        grad_weights = dot_cols(qkv_ref[part, 2 * LANES :], grads)
        grad_scores = (weights * grad_weights).astype(BF16)
        step = dot(keys_t[:, part], grad_scores)
        total = step if total is None else total + step
        dk_ref[0, part, :] = dot(grad_scores, queries)[:, :HEAD_DIM]
        dv_ref[0, part, :] = dot(weights.astype(BF16), grads)[:, :HEAD_DIM]
    dq_ref[0] = total[:HEAD_DIM].T * 0.125


def attend_backward(qkv, grads):
    rows = qkv.shape[0]
    cols = 3 * LANES
    heads = qkv.shape[1] // cols
    one_head = jax.ShapeDtypeStruct((heads, rows, HEAD_DIM), F32)
    head_spec = pl.BlockSpec((1, rows, HEAD_DIM), lambda h: (h, 0, 0))
    return pl.pallas_call(
        functools.partial(backward_kernel, key_block=256),
        grid=(heads,),
        in_specs=[
            pl.BlockSpec((rows, cols), lambda h: (0, h)),
            pl.BlockSpec((rows, LANES), lambda h: (0, h)),
        ],
        out_specs=[head_spec] * 3,
        out_shape=[one_head] * 3,
        scratch_shapes=[pltpu.VMEM((LANES, rows), BF16)],
        compiler_params=pltpu.CompilerParams(vmem_limit_bytes=56 * 2**20),
        cost_estimate=pl.CostEstimate(
            flops=40 * heads * rows * rows * HEAD_DIM,
            bytes_accessed=2 * rows * heads * (cols + 7 * LANES),
            transcendentals=heads * rows * rows,
        ),
        name="attend_backward",
    )(qkv, grads)


def padded_heads(weight, bias):
    width, _, cols = weight.shape
    heads = cols // HEAD_DIM
    scale = jnp.array([0.125, 1.0, 1.0], F32)
    weight = weight.reshape(width, 3, heads, HEAD_DIM).transpose(2, 0, 1, 3)
    weight = weight * scale[None, None, :, None].astype(weight.dtype)
    weight = jnp.pad(weight, ((0, 0), (0, 0), (0, 0), (0, LANES - HEAD_DIM)))
    full = jnp.stack([bias[0] * 0.125, jnp.zeros_like(bias[0]), bias[1]]).astype(F32)
    full = full.reshape(3, heads, HEAD_DIM).transpose(1, 0, 2)
    full = jnp.pad(full, ((0, 0), (0, 0), (0, LANES - HEAD_DIM)))
    return (
        weight.reshape(heads, width, 3 * LANES).astype(BF16),
        full.reshape(heads, 1, 3 * LANES),
    )


def join_heads(parts):
    heads, rows, width = parts.shape
    return parts.transpose(1, 0, 2).reshape(rows, heads * width)


def reduce_dp(array):
    share = lax.psum_scatter(array.astype(BF16), "dp", scatter_dimension=0, tiled=True)
    return lax.all_gather(share, "dp", axis=0, tiled=True).astype(F32)


def body(
    tokens,
    seg_lengths,
    parents,
    qkv_latent,
    qv_bias,
    out_latent,
    out_bias,
    norm1_gain,
    norm1_shift,
    up_latent,
    up_bias,
    down_latent,
    down_bias,
    norm2_gain,
    norm2_shift,
    teacher_qkv,
    teacher_qv_bias,
    teacher_out,
    teacher_out_bias,
    teacher_norm1_gain,
    teacher_norm1_shift,
    teacher_up,
    teacher_up_bias,
    teacher_down,
    teacher_down_bias,
    teacher_norm2_gain,
    teacher_norm2_shift,
):
    own_rows, model_width = tokens.shape
    group = lax.axis_size("tensor")
    me = lax.axis_index("tensor")
    all_rows = own_rows * group
    local_cols = qkv_latent.shape[2]
    local_heads = local_cols // HEAD_DIM
    hidden_all = up_latent.shape[1] * group
    x_all = jnp.concatenate(gather_blocks(tokens))
    sums = sum_small(
        jnp.stack([jnp.sum(jnp.abs(out_latent), axis=0), jnp.sum(jnp.abs(down_latent), axis=0)])
    )
    w_qkv = (jnp.mean(jnp.abs(qkv_latent), axis=0) * jnp.sign(qkv_latent)).astype(BF16)
    w_out = (sums[0] / model_width * jnp.sign(out_latent)).astype(BF16)
    w_up = (jnp.mean(jnp.abs(up_latent), axis=0) * jnp.sign(up_latent)).astype(BF16)
    w_down = (sums[1] / hidden_all * jnp.sign(down_latent)).astype(BF16)
    block_rows = jnp.arange(own_rows, dtype=jnp.int32)
    positions = jnp.concatenate([(me ^ j) * own_rows + block_rows for j in range(group)])
    features = segment_features(seg_lengths[0], parents[0], positions)
    x_own = tokens.astype(F32)
    x_in_all = clip_act(x_all.astype(F32)).astype(BF16)

    qkv, context = attend_forward(
        x_in_all, *padded_heads(w_qkv, qv_bias), features, True
    )
    _, t_context = attend_forward(
        x_all, *padded_heads(teacher_qkv, teacher_qv_bias), features, False
    )
    context = join_heads(context)
    attn_in = clip_act(context).astype(BF16)
    t_attn_in = join_heads(t_context).astype(BF16)

    def own_rows_all_heads(array):
        return jnp.concatenate(exchange_blocks(list(array.reshape(group, own_rows, -1))), axis=1)

    w_out_all = jnp.concatenate(gather_blocks(w_out))
    t_weights = jnp.concatenate(
        [teacher_up, teacher_down, teacher_out, jnp.tile(teacher_up_bias[None], (16, 1))]
    )
    t_blocks = gather_blocks(t_weights)
    hid = teacher_up.shape[1]
    t_up = [block[:model_width] for block in t_blocks]
    t_down = [block[model_width : model_width + hid] for block in t_blocks]
    t_out_all = jnp.concatenate(
        [block[model_width + hid : model_width + hid + local_cols] for block in t_blocks]
    )
    t_up_bias = [block[-1].astype(F32) for block in t_blocks]

    attn_in_own = own_rows_all_heads(attn_in)
    attn_own = dot(attn_in_own, w_out_all)
    gain_one = norm1_gain.astype(F32)
    gain_two = norm2_gain.astype(F32)
    y_one, normed_one, inv_one = norm_forward(
        x_own + attn_own + out_bias.astype(F32), gain_one, norm1_shift.astype(F32)
    )
    y_one_in = clip_act(y_one).astype(BF16)
    y_one_all = jnp.concatenate(gather_blocks(y_one_in))

    t_attn_own = dot(own_rows_all_heads(t_attn_in), t_out_all)
    t_y_one, _, _ = norm_forward(
        x_own + t_attn_own + teacher_out_bias.astype(F32),
        teacher_norm1_gain.astype(F32),
        teacher_norm1_shift.astype(F32),
    )
    t_y_one_in = t_y_one.astype(BF16)
    t_ffn_own = teacher_down_bias.astype(F32)
    for up, down, bias in zip(t_up, t_down, t_up_bias):
        t_hidden = jax.nn.gelu(dot(t_y_one_in, up) + bias, approximate=False).astype(BF16)
        t_ffn_own = t_ffn_own + dot(t_hidden, down)
    t_out_own, _, _ = norm_forward(
        t_y_one + t_ffn_own,
        teacher_norm2_gain.astype(F32),
        teacher_norm2_shift.astype(F32),
    )

    upward = dot(y_one_all, w_up) + up_bias.astype(F32)
    gelu_vals = jax.nn.gelu(upward, approximate=False)
    gelu_in = clip_act(gelu_vals).astype(BF16)
    ffn_part = dot(gelu_in, w_down)
    ffn_own = reduce_blocks(list(ffn_part.reshape(group, own_rows, -1)))
    out_own, normed_two, inv_two = norm_forward(
        y_one + ffn_own + down_bias.astype(F32), gain_two, norm2_shift.astype(F32)
    )
    mismatch = out_own - t_out_own
    loss_part = jnp.sum(mismatch * mismatch)
    grad_two, gain_two_grad, shift_two_grad = norm_backward(mismatch, normed_two, inv_two, gain_two)
    grad_ffn = grad_two.astype(BF16)
    down_bias_grad = jnp.sum(grad_ffn.astype(F32), axis=0)
    grad_ffn_all = jnp.concatenate(gather_blocks(grad_ffn))
    down_grad = dot_rows(gelu_in, grad_ffn_all)
    grad_gelu = dot_cols(grad_ffn_all, w_down)
    grad_up = (grad_gelu * clip_slope(gelu_vals) * gelu_slope(upward)).astype(BF16)
    up_bias_grad = jnp.sum(grad_up.astype(F32), axis=0)
    up_grad = dot_rows(y_one_all, grad_up)
    ffn_grads = reduce_dp(jnp.concatenate([up_grad, down_grad]))
    grad_y_in = reduce_blocks(list(dot_cols(grad_up, w_up).reshape(group, own_rows, -1)))
    grad_y_one = grad_two + grad_y_in * clip_slope(y_one)
    grad_h, gain_one_grad, shift_one_grad = norm_backward(grad_y_one, normed_one, inv_one, gain_one)
    grad_attn = grad_h.astype(BF16)
    out_bias_grad = jnp.sum(grad_attn.astype(F32), axis=0)
    out_grad = reduce_blocks(
        list(dot_rows(attn_in_own, grad_attn).reshape(group, local_cols, -1))
    )
    level = attn_in_own.astype(F32) / CLIP_RANGE
    grad_context = (dot_cols(grad_attn, w_out_all) * (1.0 - level * level)).astype(BF16)
    grad_context = jnp.concatenate(
        exchange_blocks([grad_context[:, j * local_cols : (j + 1) * local_cols] for j in range(group)])
    )
    grad_heads = grad_context.reshape(all_rows, local_heads, HEAD_DIM)
    inner = -jnp.sum(
        grad_heads.astype(F32) * context.reshape(all_rows, local_heads, HEAD_DIM),
        axis=-1,
        keepdims=True,
    )
    grad_wide = jnp.concatenate(
        [
            grad_heads,
            jnp.zeros((all_rows, local_heads, ROW_TERM - HEAD_DIM), BF16),
            *(part.astype(BF16) for part in split_three(inner, to_bf16_grid)),
            jnp.zeros((all_rows, local_heads, LANES - ROW_TERM - 3), BF16),
        ],
        axis=-1,
    ).reshape(all_rows, local_heads * LANES)
    grad_queries, grad_keys, grad_values = attend_backward(qkv, grad_wide)
    grad_proj = jnp.concatenate(
        [join_heads(grad_queries), join_heads(grad_keys), join_heads(grad_values)], axis=1
    ).astype(BF16)
    proj_bias_grad = jnp.sum(grad_proj.astype(F32), axis=0)
    qkv_grad = dot_rows(x_in_all, grad_proj)
    grad_x_in = reduce_blocks(
        list(
            dot_cols(grad_proj, w_qkv.reshape(model_width, -1)).reshape(group, own_rows, -1)
        )
    )
    input_grad = grad_h + grad_x_in * clip_slope(x_own)

    shared = jnp.stack(
        [
            out_bias_grad,
            gain_one_grad,
            shift_one_grad,
            down_bias_grad,
            gain_two_grad,
            shift_two_grad,
            jnp.full((model_width,), loss_part),
        ]
    )
    shared = sum_small(shared)
    tree_loss = shared[6, :1] / (all_rows * model_width)
    small = jnp.concatenate(
        [shared[:6].reshape(-1), up_bias_grad, proj_bias_grad]
    )
    small = lax.psum(small, "dp")
    shared, up_bias_grad, proj_bias_grad = (
        small[: 6 * model_width].reshape(6, model_width),
        small[6 * model_width : 6 * model_width + hid],
        small[6 * model_width + hid :].reshape(3, local_cols),
    )
    late = reduce_dp(
        jnp.concatenate([qkv_grad.reshape(-1, model_width), out_grad.astype(F32)])
    )
    qkv_rows = 3 * local_cols
    return (
        out_own.astype(BF16),
        tree_loss,
        input_grad,
        late[:qkv_rows].reshape(model_width, 3, local_cols),
        jnp.stack([proj_bias_grad[0], proj_bias_grad[2]]),
        late[qkv_rows:],
        shared[0],
        shared[1],
        shared[2],
        ffn_grads[:model_width],
        up_bias_grad,
        ffn_grads[model_width:],
        shared[3],
        shared[4],
        shared[5],
    )


def solution(mesh):
    rows, cols = ("dp", "tensor"), "tensor"
    vec = P()
    params = (
        P(None, None, cols),
        P(None, cols),
        P(cols, None),
        vec,
        vec,
        vec,
        P(None, cols),
        P(cols),
        P(cols, None),
        vec,
        vec,
        vec,
    )
    in_specs = (P(rows, None), P("dp", None), P("dp", None)) + params + params
    out_specs = (P(rows, None), P("dp"), P(rows, None)) + params
    return jax.shard_map(body, mesh=mesh, in_specs=in_specs, out_specs=out_specs, check_vma=False)
```

```python
import functools

import jax
import jax.numpy as jnp
from jax import lax
from jax.experimental import pallas as pl
from jax.experimental.pallas import tpu as pltpu
from jax.sharding import PartitionSpec as P

HEAD_DIM = 64
LANES = 128
CLIP_RANGE = 3.0
NORM_EPSILON = 1e-05
MASKED_SCORE = -1e30
SEG_LANE = HEAD_DIM
ROW_TERM = HEAD_DIM + 16
Q_BLOCK = 256
CHUNKS = 2
BF16, F32 = jnp.bfloat16, jnp.float32
ROWS_ROWS = (((0,), (0,)), ((), ()))
COLS_COLS = (((1,), (1,)), ((), ()))


def clip_act(values):
    return CLIP_RANGE * jnp.tanh(values / CLIP_RANGE)


def clip_slope(values):
    level = jnp.tanh(values / CLIP_RANGE)
    return 1.0 - level * level


def normal_parts(values):
    bell = jnp.exp(-0.5 * values * values)
    step = 1.0 / (1.0 + 0.23164188843 * jnp.abs(values))
    series = 0.5307027145 * step - 0.7265760135
    series = series * step + 0.7107068705
    series = series * step - 0.142248368
    series = series * step + 0.127414796
    tail = series * step * bell
    return jnp.where(values >= 0.0, 1.0 - tail, tail), bell


def norm_forward(hidden, gain, shift):
    row_mean = jnp.mean(hidden, axis=-1, keepdims=True)
    centred = hidden - row_mean
    inv_std = lax.rsqrt(jnp.mean(centred * centred, axis=-1, keepdims=True) + NORM_EPSILON)
    normed = centred * inv_std
    return (normed * gain + shift, normed, inv_std)


def norm_backward(grad_out, normed, inv_std, gain):
    grad_normed = grad_out * gain
    centre = jnp.mean(grad_normed, axis=-1, keepdims=True)
    inner_sum = jnp.mean(grad_normed * normed, axis=-1, keepdims=True)
    return inv_std * (grad_normed - centre - normed * inner_sum)


def dot(left, right):
    return jnp.dot(left, right, preferred_element_type=F32)


def dot_rows(left, right):
    return lax.dot_general(left, right, ROWS_ROWS, preferred_element_type=F32)


def dot_cols(left, right):
    return lax.dot_general(left, right, COLS_COLS, preferred_element_type=F32)


def swap(array, bit):
    size = lax.axis_size("tensor")
    return lax.ppermute(array, "tensor", [(i, i ^ bit) for i in range(size)])


def gather_blocks(own):
    far = swap(own, 2)
    near = swap(own, 1)
    return [own, near, far, swap(far, 1)]


def reduce_blocks(blocks):
    near = swap(jnp.stack([blocks[1], blocks[3]]).astype(BF16), 1).astype(F32)
    far = swap((blocks[2] + near[1]).astype(BF16), 2).astype(F32)
    return blocks[0] + near[0] + far


def sum_small(array):
    array = array + swap(array, 1)
    return array + swap(array, 2)


def lookup(indices, lookup_table):
    labels = jnp.arange(lookup_table.shape[0], dtype=jnp.int32)
    picked = jnp.where(indices[:, None] == labels[None, :], lookup_table[None, :], 0)
    return jnp.sum(picked, axis=1)


def segment_tables(lengths, parent):
    count = lengths.shape[0]
    labels = jnp.arange(count, dtype=jnp.int32)
    row, col = labels[:, None], labels[None, :]
    starts = jnp.sum(jnp.where(col < row, lengths[None, :], 0), axis=1)
    two = lookup(parent, parent)
    allowed = (col == row) | (col == parent[:, None]) | (col == two[:, None])
    allowed = allowed | (parent[None, :] == row) | (two[None, :] == row)
    after = LANES - SEG_LANE - count
    lanes = jnp.pad(jnp.stack([starts, starts + lengths]), ((0, 6), (SEG_LANE, after)))
    blocked = jnp.pad((~allowed).astype(BF16), ((SEG_LANE, after), (SEG_LANE, after)))
    return lanes, blocked


def split_three(values):
    first = values.astype(BF16).astype(F32)
    second = (values - first).astype(BF16).astype(F32)
    return first, second, values - first - second


def in_lane(shape, axis, terms):
    lane = lax.broadcasted_iota(jnp.int32, shape, axis)
    spread = jnp.zeros(shape, F32)
    for offset, term in enumerate(terms):
        spread = jnp.where(lane == ROW_TERM + offset, term, spread)
    return spread


def forward_kernel(base_ref, x0, x1, x2, x3, w_ref, b_ref, seg_ref, blocked_ref, *rest, student):
    if student:
        qkv_ref, ctx_ref, source, own, near, far, joined, query_part, key_part, keys, vals_t = rest
    else:
        sent, source, joined, query_part, key_part, keys, vals_t = rest
    blocks = (x0, x1, x2, x3)
    own_rows = x0.shape[0]
    rows = own_rows * len(blocks)
    head = pl.program_id(0)

    @pl.when(head == 0)
    def _():
        lane = lax.broadcasted_iota(jnp.int32, (own_rows, LANES), 1)
        for j, block in enumerate(blocks):
            part = slice(j * own_rows, (j + 1) * own_rows)
            if student:
                source[part, :] = clip_act(block[...].astype(F32)).astype(BF16)
            else:
                source[part, :] = block[...]
            place = lax.broadcasted_iota(jnp.int32, (own_rows, LANES), 0) + base_ref[j]
            inside = (place >= seg_ref[0:1, :]) & (place < seg_ref[1:2, :])
            query_part[part, :] = jnp.where(inside, MASKED_SCORE, 0.0).astype(BF16)
            links = dot(jnp.where(inside, 1.0, 0.0).astype(BF16), blocked_ref[...])
            ones = (lane >= ROW_TERM) & (lane < ROW_TERM + 3)
            key_part[part, :] = jnp.where(ones, 1.0, links).astype(BF16)

    proj = (dot(source[...], w_ref[0]) + b_ref[0]).astype(BF16)
    queries = proj[:, :LANES] + query_part[...]
    keys[...] = proj[:, LANES : 2 * LANES] + key_part[...]
    vals_t[...] = proj[:, 2 * LANES :].T
    if student:
        qkv_ref[:, LANES : 2 * LANES] = keys[...]
        lane = lax.broadcasted_iota(jnp.int32, (rows, LANES), 1)
        ones = jnp.where((lane >= ROW_TERM) & (lane < ROW_TERM + 3), 1.0, 0.0).astype(BF16)
        qkv_ref[:, 2 * LANES :] = proj[:, 2 * LANES :] + ones
    scores = []
    for start in range(0, rows, Q_BLOCK):
        scores.append(dot_cols(keys[...], queries[start : start + Q_BLOCK]))
    for index, block in enumerate(scores):
        part = slice(index * Q_BLOCK, (index + 1) * Q_BLOCK)
        peak = jnp.max(block, axis=0, keepdims=True)
        raised = jnp.exp(block - peak)
        total = jnp.sum(raised, axis=0, keepdims=True)
        weights = (raised * (1.0 / total)).astype(BF16)
        context = dot(vals_t[...], weights)[:HEAD_DIM].T
        joined[head, part, :] = context
        if student:
            ctx_ref[0, part, :] = context
            terms = split_three(-(peak + jnp.log(total)))
            spread = in_lane((LANES, Q_BLOCK), 0, terms)
            qkv_ref[part, :LANES] = queries[part] + spread.T.astype(BF16)

    @pl.when(head == pl.num_programs(0) - 1)
    def _():
        for j in range(len(blocks)):
            part = slice(j * own_rows, (j + 1) * own_rows)
            block = jnp.concatenate([joined[h, part, :] for h in range(joined.shape[0])], axis=1)
            if not student:
                sent[j] = block.astype(BF16)
            elif j < 2:
                (own, near)[j][...] = clip_act(block).astype(BF16)
            else:
                far[j - 2] = clip_act(block).astype(BF16)


def attend_forward(base, blocks, weight, bias, seg_lanes, blocked, student):
    own_rows, width = blocks[0].shape
    rows = own_rows * len(blocks)
    heads = weight.shape[0]
    cols = 3 * LANES
    head_cols = heads * HEAD_DIM
    whole = lambda *shape: pl.BlockSpec(shape, lambda h: (0,) * len(shape))
    array = jax.ShapeDtypeStruct
    if student:
        out_specs = [
            pl.BlockSpec((rows, cols), lambda h: (0, h)),
            pl.BlockSpec((1, rows, HEAD_DIM), lambda h: (h, 0, 0)),
            whole(rows, width),
            whole(own_rows, head_cols),
            whole(own_rows, head_cols),
            whole(2, own_rows, head_cols),
        ]
        out_shape = [
            array((rows, heads * cols), BF16),
            array((heads, rows, HEAD_DIM), F32),
            array((rows, width), BF16),
            array((own_rows, head_cols), BF16),
            array((own_rows, head_cols), BF16),
            array((2, own_rows, head_cols), BF16),
        ]
        scratch = []
    else:
        out_specs = [whole(len(blocks), own_rows, head_cols)]
        out_shape = [array((len(blocks), own_rows, head_cols), BF16)]
        scratch = [pltpu.VMEM((rows, width), BF16)]
    scratch += [
        pltpu.VMEM((heads, rows, HEAD_DIM), F32),
        pltpu.VMEM((rows, LANES), BF16),
        pltpu.VMEM((rows, LANES), BF16),
        pltpu.VMEM((rows, LANES), BF16),
        pltpu.VMEM((LANES, rows), BF16),
    ]
    return pl.pallas_call(
        functools.partial(forward_kernel, student=student),
        grid=(heads,),
        in_specs=[pl.BlockSpec(memory_space=pltpu.SMEM)]
        + [whole(own_rows, width)] * 4
        + [
            pl.BlockSpec((1, width, cols), lambda h: (h, 0, 0)),
            pl.BlockSpec((1, 1, cols), lambda h: (h, 0, 0)),
            whole(*seg_lanes.shape),
            whole(*blocked.shape),
        ],
        out_specs=out_specs,
        out_shape=out_shape,
        scratch_shapes=scratch,
        compiler_params=pltpu.CompilerParams(vmem_limit_bytes=58 * 2**20),
        cost_estimate=pl.CostEstimate(
            flops=16 * heads * rows * rows * HEAD_DIM,
            bytes_accessed=2 * rows * (width + 2 * heads * cols),
            transcendentals=heads * rows * rows,
        ),
        name="student_attention" if student else "teacher_attention",
    )(base, *blocks, weight, bias, seg_lanes, blocked)


def backward_kernel(
    qkv_ref, ctx_ref, x_ref, w_ref, g0, g1, g2, g3,
    wg_ref, bg_ref, own_ref, near_ref, far_ref,
    grads, packed, keys_t, total, *, key_block,
):
    blocks = (g0, g1, g2, g3)
    own_rows = g0.shape[0]
    rows = own_rows * len(blocks)
    heads = grads.shape[0]
    head = pl.program_id(0)

    @pl.when(head == 0)
    def _():
        for h in range(heads):
            for j, block in enumerate(blocks):
                part = slice(j * own_rows, (j + 1) * own_rows)
                one = block[:, h * HEAD_DIM : (h + 1) * HEAD_DIM].astype(F32)
                grads[h, part, :] = jnp.concatenate([one, jnp.zeros_like(one)], axis=1).astype(BF16)
        packed[...] = jnp.zeros_like(packed)

    queries = qkv_ref[:, :LANES]
    slopes = grads[head]
    inner = -jnp.sum(
        slopes[:, :HEAD_DIM].astype(F32) * ctx_ref[0], axis=1, keepdims=True
    )
    slopes = slopes + in_lane((rows, LANES), 1, split_three(inner)).astype(BF16)
    keys_t[...] = qkv_ref[:, LANES : 2 * LANES].T
    query_grad = None
    for start in range(0, rows, key_block):
        part = slice(start, start + key_block)
        weights = jnp.exp(dot_cols(qkv_ref[part, LANES : 2 * LANES], queries))
        grad_weights = dot_cols(qkv_ref[part, 2 * LANES :], slopes)
        grad_scores = (weights * grad_weights).astype(BF16)
        step = dot(keys_t[:, part], grad_scores)
        query_grad = step if query_grad is None else query_grad + step
        key_grad = dot(grad_scores, queries)[:, :HEAD_DIM]
        packed[part, LANES : LANES + HEAD_DIM] = key_grad.astype(BF16)
        value_grad = dot(weights.astype(BF16), slopes)[:, :HEAD_DIM]
        packed[part, 2 * LANES : 2 * LANES + HEAD_DIM] = value_grad.astype(BF16)
    packed[:, :HEAD_DIM] = query_grad[:HEAD_DIM].T.astype(BF16)
    bg_ref[0] = jnp.sum(packed[...].astype(F32), axis=0, keepdims=True)
    weight_grad = dot_rows(packed[...], x_ref[...])
    for c, factor in enumerate((0.125, 1.0, 1.0)):
        wg_ref[0, c * HEAD_DIM : (c + 1) * HEAD_DIM, :] = (
            weight_grad[c * LANES : c * LANES + HEAD_DIM] * factor
        ).astype(BF16)
    for j in range(len(blocks)):
        part = slice(j * own_rows, (j + 1) * own_rows)
        step = dot_cols(packed[part, :], w_ref[0])
        total[part, :] = jnp.where(head == 0, step, total[part, :] + step)

    @pl.when(head == pl.num_programs(0) - 1)
    def _():
        part = lambda j: slice(j * own_rows, (j + 1) * own_rows)
        own_ref[...] = total[part(0), :]
        far_ref[...] = total[part(2), :]
        near_ref[0] = total[part(1), :].astype(BF16)
        near_ref[1] = total[part(3), :].astype(BF16)


def attend_backward(qkv, context, source, weight, blocks):
    rows, width = source.shape
    own_rows, head_cols = blocks[0].shape
    cols = 3 * LANES
    heads = weight.shape[0]
    array = jax.ShapeDtypeStruct
    whole = lambda *shape: pl.BlockSpec(shape, lambda h: (0,) * len(shape))
    head_block = lambda *shape: pl.BlockSpec((1,) + shape, lambda h: (h, 0, 0))
    return pl.pallas_call(
        functools.partial(backward_kernel, key_block=256),
        grid=(heads,),
        in_specs=[
            pl.BlockSpec((rows, cols), lambda h: (0, h)),
            head_block(rows, HEAD_DIM),
            whole(rows, width),
            head_block(width, cols),
        ]
        + [whole(own_rows, head_cols)] * 4,
        out_specs=[
            head_block(3 * HEAD_DIM, width),
            head_block(1, cols),
            whole(own_rows, width),
            whole(2, own_rows, width),
            whole(own_rows, width),
        ],
        out_shape=[
            array((heads, 3 * HEAD_DIM, width), BF16),
            array((heads, 1, cols), F32),
            array((own_rows, width), F32),
            array((2, own_rows, width), BF16),
            array((own_rows, width), F32),
        ],
        scratch_shapes=[
            pltpu.VMEM((heads, rows, LANES), BF16),
            pltpu.VMEM((rows, cols), BF16),
            pltpu.VMEM((LANES, rows), BF16),
            pltpu.VMEM((rows, width), F32),
        ],
        compiler_params=pltpu.CompilerParams(vmem_limit_bytes=58 * 2**20),
        cost_estimate=pl.CostEstimate(
            flops=40 * heads * rows * rows * HEAD_DIM,
            bytes_accessed=2 * rows * heads * (cols + 7 * LANES),
            transcendentals=heads * rows * rows,
        ),
        name="attention_backward",
    )(qkv, context, source, weight, *blocks)


(OUT_BIAS, GAIN_1, SHIFT_1, DOWN_BIAS, GAIN_2, SHIFT_2, UP_BIAS) = range(7)
T_VECTORS = 7
LOSS_ROW, UP_ROW = 6, 7


def middle_kernel(
    x_ref, ca0, ca1, ca23, ca3, tc_ref, w_out, tw_out, w_up, w_down, vec,
    pack_own, pack_near, pack_a, pack_b, pack_c, pack_d,
    out_ref, gh_ref, ffn_ref, outg_ref, g0_ref, g1_ref, g2_ref, g3_ref, small_ref,
    tc1, tc2, tcf, tc3, y_all, g_all, slope, hid, gu_all, t_out, first, normed, two, inv,
    part0, part2, send1, send2, send3, near0, near2, far0, gs, gr, packs,
    send_sem, recv_sem, pack_sem,
):
    me = lax.axis_index("tensor")
    near_id = me + 1 - 2 * lax.rem(me, 2)
    far_id = lax.rem(me + 2, 4)
    own_rows, width = x_ref.shape
    hidden = w_down.shape[0]
    head_cols = ca0.shape[1]
    size = own_rows // CHUNKS
    chunks = [slice(c * size, (c + 1) * size) for c in range(CHUNKS)]
    tiles = [slice(n, n + 256) for n in range(0, hidden, 256)]
    group = lambda j: slice(j * head_cols, (j + 1) * head_cols)
    row = lambda index: vec[index : index + 1, :]

    barrier = pltpu.get_barrier_semaphore()
    for other in (near_id, far_id):
        pl.semaphore_signal(
            barrier, inc=1, device_id={"tensor": other}, device_id_type=pl.DeviceIdType.MESH
        )
    pl.semaphore_wait(barrier, 2)

    count = [0]
    started = []

    def put(source, target, device):
        index = count[0]
        count[0] += 1
        copy = pltpu.make_async_remote_copy(
            src_ref=source,
            dst_ref=target,
            send_sem=send_sem.at[index],
            recv_sem=recv_sem.at[index],
            device_id={"tensor": device},
            device_id_type=pl.DeviceIdType.MESH,
        )
        copy.start()
        started.append(copy)
        return copy

    t_far = put(tc_ref.at[2], tc2, far_id)
    t_pass = put(tc_ref.at[3], tcf, far_id)
    t_near = put(tc_ref.at[1], tc1, near_id)

    pack_refs = [pack_own.at[0], pack_own.at[1], pack_near.at[0], pack_near.at[1]]
    pack_refs += [pack_a, pack_b, pack_c, pack_d]

    def load_pack(index):
        slot = index % 2
        return pltpu.make_async_copy(pack_refs[index], packs.at[slot], pack_sem.at[slot])

    load_pack(0).start()
    small_ref[...] = jnp.zeros_like(small_ref)

    def add_small(index, values):
        small_ref[index : index + 1, :] += jnp.sum(values, axis=0, keepdims=True)

    def share(own_block, where):
        return (
            put(own_block.at[0, where], own_block.at[1, where], near_id),
            put(own_block.at[0, where], own_block.at[2, where], far_id),
        )

    y_sent = []
    for rows in chunks:
        attn = dot(ca0[rows, :], w_out[group(0), :]) + dot(ca1[rows, :], w_out[group(1), :])
        attn += dot(ca23[0, rows, :], w_out[group(2), :]) + dot(ca3[rows, :], w_out[group(3), :])
        y_one, y_normed, y_inv = norm_forward(
            x_ref[rows, :].astype(F32) + attn + row(OUT_BIAS), row(GAIN_1), row(SHIFT_1)
        )
        first[rows, :] = y_one
        normed[rows, :] = y_normed
        inv[rows, :] = jnp.broadcast_to(y_inv, (size, LANES))
        y_all[0, rows, :] = clip_act(y_one).astype(BF16)
        y_sent.append(share(y_all, rows))

    def forward_block(j, rows):
        total = None
        for cols in tiles:
            upward = dot(y_all[j, rows, :], w_up[:, cols]) + row(UP_BIAS)[:, cols]
            cdf, bell = normal_parts(upward)
            level = jnp.tanh(upward * cdf * (1.0 / CLIP_RANGE))
            act = (CLIP_RANGE * level).astype(BF16)
            hid[j, rows, cols] = act
            slope[j, rows, cols] = (1.0 - level * level) * (
                cdf + upward * bell * 0.3989422804014327
            )
            step = dot(act, w_down[cols, :])
            total = step if total is None else total + step
        return total

    def backward_block(j, rows):
        total = None
        for cols in tiles:
            grad = dot_cols(g_all[j, rows, :], w_down[cols, :])
            grad = (grad * slope[j, rows, cols]).astype(BF16)
            gu_all[j, rows, cols] = grad
            small_ref[UP_ROW : UP_ROW + 1, cols] += jnp.sum(
                grad.astype(F32), axis=0, keepdims=True
            )
            step = dot_cols(grad, w_up[:, cols])
            total = step if total is None else total + step
        return total

    def near_blocks(work, sent):
        copies = []
        for rows in chunks:
            part0[rows, :] = work(0, rows)
        for rows, (near, _) in zip(chunks, sent):
            near.wait_recv()
            send1[rows, :] = work(1, rows).astype(BF16)
            copies.append(put(send1.at[rows], near0.at[rows], near_id))
        return copies

    def far_blocks(block, work, sent):
        copies = []
        for rows, (_, far) in zip(chunks, sent):
            far.wait_recv()
            passed = put(block.at[2, rows], block.at[3, rows], near_id)
            part2[rows, :] = work(2, rows)
            passed.wait_recv()
            send3[rows, :] = work(3, rows).astype(BF16)
            met = put(send3.at[rows], near2.at[rows], near_id)
            met.wait_recv()
            send2[rows, :] = (part2[rows, :] + near2[rows, :].astype(F32)).astype(BF16)
            copies.append(put(send2.at[rows], far0.at[rows], far_id))
        return copies

    def summed(rows, near, far):
        near.wait_recv()
        far.wait_recv()
        return part0[rows, :] + near0[rows, :].astype(F32) + far0[rows, :].astype(F32)

    y_near = near_blocks(forward_block, y_sent)

    t_pass.wait_recv()
    t_last = put(tcf, tc3, near_id)
    t_near.wait_recv()
    t_far.wait_recv()
    t_row = lambda index: row(T_VECTORS + index)
    t_attn = dot(tc_ref[0], tw_out[group(0), :]) + dot(tc1[...], tw_out[group(1), :])
    t_attn += dot(tc2[...], tw_out[group(2), :])
    t_last.wait_recv()
    t_attn += dot(tc3[...], tw_out[group(3), :])
    t_one, _, _ = norm_forward(x_ref[...].astype(F32) + t_attn + t_row(0), t_row(1), t_row(2))
    two[...] = t_one
    t_out[...] = t_one + t_row(3)
    half = hidden // 2
    t_in = t_one.astype(BF16)
    for index in range(len(pack_refs)):
        slot = index % 2
        if index + 1 < len(pack_refs):
            load_pack(index + 1).start()
        load_pack(index).wait()
        upward = dot_cols(t_in, packs[slot, :half, :])
        upward = upward + packs[slot, hidden : hidden + 1, :half].astype(F32)
        act = (upward * normal_parts(upward)[0]).astype(BF16)
        t_out[...] += dot(act, packs[slot, half:hidden, :])
    t_out[...] = norm_forward(t_out[...], t_row(4), t_row(5))[0]

    y_far = far_blocks(y_all, forward_block, y_sent)

    g_sent = []
    for copy in started:
        copy.wait_send()
    started.clear()
    for rows, near, far in zip(chunks, y_near, y_far):
        ffn = summed(rows, near, far)
        out, n_two, inv_two = norm_forward(
            first[rows, :] + ffn + row(DOWN_BIAS), row(GAIN_2), row(SHIFT_2)
        )
        out_ref[rows, :] = out.astype(BF16)
        gap = out - t_out[rows, :]
        add_small(LOSS_ROW, gap * gap)
        add_small(GAIN_2, gap * n_two)
        add_small(SHIFT_2, gap)
        grad_two = norm_backward(gap, n_two, inv_two, row(GAIN_2))
        two[rows, :] = grad_two
        grad_ffn = grad_two.astype(BF16)
        add_small(DOWN_BIAS, grad_ffn.astype(F32))
        g_all[0, rows, :] = grad_ffn
        g_sent.append(share(g_all, rows))

    g_near = near_blocks(backward_block, g_sent)
    g_far = far_blocks(g_all, backward_block, g_sent)
    flat = lambda block: block[...].reshape(4 * own_rows, block.shape[2])
    ffn_ref[:width, :] = dot_rows(flat(y_all), flat(gu_all)).astype(BF16)
    ffn_ref[width:, :] = dot_rows(flat(hid), flat(g_all)).astype(BF16)

    passes = []
    for c, (rows, near, far) in enumerate(zip(chunks, g_near, g_far)):
        y_one = first[rows, :]
        grad_one = two[rows, :] + summed(rows, near, far) * clip_slope(y_one)
        n_one = normed[rows, :]
        add_small(GAIN_1, grad_one * n_one)
        add_small(SHIFT_1, grad_one)
        grad_h = norm_backward(grad_one, n_one, inv[rows, :1], row(GAIN_1))
        gh_ref[rows, :] = grad_h
        grad_attn = grad_h.astype(BF16)
        add_small(OUT_BIAS, grad_attn.astype(F32))
        for j, ca in enumerate((ca0.at[rows], ca1.at[rows], ca23.at[0, rows], ca3.at[rows])):
            act = ca[...]
            level = act.astype(F32) * (1.0 / CLIP_RANGE)
            grad = dot_cols(grad_attn, w_out[group(j), :]) * (1.0 - level * level)
            gs[j, rows, :] = grad.astype(BF16)
            step = dot_rows(act, grad_attn)
            if c:
                step = step + part2[group(j), :]
            part2[group(j), :] = step
        passes.append(
            (
                put(gs.at[3, rows], gr.at[3, rows], far_id),
                put(gs.at[2, rows], gr.at[1, rows], far_id),
                put(gs.at[1, rows], gr.at[0, rows], near_id),
            )
        )
    g0_ref[...] = gs[0]
    for j in range(4):
        outg_ref[j] = part2[group(j), :].astype(BF16)
    lasts = []
    for rows, (passing, _, _) in zip(chunks, passes):
        passing.wait_recv()
        lasts.append(put(gr.at[3, rows], gr.at[2, rows], near_id))
    for rows, (_, far, near), last in zip(chunks, passes, lasts):
        near.wait_recv()
        g1_ref[rows, :] = gr[0, rows, :]
        far.wait_recv()
        g2_ref[rows, :] = gr[1, rows, :]
        last.wait_recv()
        g3_ref[rows, :] = gr[2, rows, :]
    for copy in started:
        copy.wait_send()


def middle(x_own, cas, tc, w_out, tw_out, w_up, w_down, vectors, packs):
    own_rows, width = x_own.shape
    hidden = w_down.shape[0]
    head_cols = cas[0].shape[1]
    array = jax.ShapeDtypeStruct
    vmem = pl.BlockSpec(memory_space=pltpu.VMEM)
    transfers = 4 + 4 * 3 * CHUNKS + 4 * CHUNKS
    square = lambda kind: pltpu.VMEM((own_rows, width), kind)
    four = lambda cols, kind: pltpu.VMEM((4, own_rows, cols), kind)
    return pl.pallas_call(
        middle_kernel,
        in_specs=[vmem] * 11 + [pl.BlockSpec(memory_space=pl.ANY)] * 6,
        out_specs=[vmem] * 9,
        out_shape=[
            array((own_rows, width), BF16),
            array((own_rows, width), F32),
            array((width + hidden, width), BF16),
            array((4, head_cols, width), BF16),
        ]
        + [array((own_rows, head_cols), BF16)] * 4
        + [array((8, width), F32)],
        scratch_shapes=[pltpu.VMEM((own_rows, head_cols), BF16)] * 4
        + [four(width, BF16), four(width, BF16), four(hidden, F32), four(hidden, BF16)]
        + [four(hidden, BF16)]
        + [square(F32)] * 4
        + [pltpu.VMEM((own_rows, LANES), F32)]
        + [square(F32), pltpu.VMEM((4 * max(own_rows // 4, head_cols), width), F32)]
        + [square(BF16)] * 6
        + [four(head_cols, BF16), four(head_cols, BF16)]
        + [
            pltpu.VMEM((2,) + packs[2].shape, BF16),
            pltpu.SemaphoreType.DMA((transfers,)),
            pltpu.SemaphoreType.DMA((transfers,)),
            pltpu.SemaphoreType.DMA((2,)),
        ],
        compiler_params=pltpu.CompilerParams(
            collective_id=3, has_side_effects=True, vmem_limit_bytes=62 * 2**20
        ),
        cost_estimate=pl.CostEstimate(
            flops=120 * own_rows * width * hidden, bytes_accessed=2**25, transcendentals=2**22
        ),
        name="middle",
    )(x_own, *cas, tc, w_out, tw_out, w_up, w_down, vectors, *packs)


def padded_heads(weight, bias):
    width, _, cols = weight.shape
    heads = cols // HEAD_DIM
    scale = jnp.array([0.125, 1.0, 1.0], F32)
    weight = weight.reshape(width, 3, heads, HEAD_DIM).transpose(2, 0, 1, 3)
    weight = weight * scale[None, None, :, None].astype(weight.dtype)
    weight = jnp.pad(weight, ((0, 0), (0, 0), (0, 0), (0, LANES - HEAD_DIM)))
    full = jnp.stack([bias[0] * 0.125, jnp.zeros_like(bias[0]), bias[1]]).astype(F32)
    full = full.reshape(3, heads, HEAD_DIM).transpose(1, 0, 2)
    full = jnp.pad(full, ((0, 0), (0, 0), (0, LANES - HEAD_DIM)))
    return (
        weight.reshape(heads, width, 3 * LANES).astype(BF16),
        full.reshape(heads, 1, 3 * LANES),
    )


def reduce_dp(array):
    share = lax.psum_scatter(array.astype(BF16), "dp", scatter_dimension=0, tiled=True)
    return lax.all_gather(share, "dp", axis=0, tiled=True).astype(F32)


def body(
    tokens,
    seg_lengths,
    parents,
    qkv_latent,
    qv_bias,
    out_latent,
    out_bias,
    norm1_gain,
    norm1_shift,
    up_latent,
    up_bias,
    down_latent,
    down_bias,
    norm2_gain,
    norm2_shift,
    teacher_qkv,
    teacher_qv_bias,
    teacher_out,
    teacher_out_bias,
    teacher_norm1_gain,
    teacher_norm1_shift,
    teacher_up,
    teacher_up_bias,
    teacher_down,
    teacher_down_bias,
    teacher_norm2_gain,
    teacher_norm2_shift,
):
    own_rows, model_width = tokens.shape
    group = lax.axis_size("tensor")
    me = lax.axis_index("tensor")
    all_rows = own_rows * group
    local_cols = qkv_latent.shape[2]
    local_heads = local_cols // HEAD_DIM
    hid = up_latent.shape[1]
    half = hid // 2
    near_x = swap(tokens, 1)
    far_x = swap(tokens, 2)
    blocks = [tokens, near_x, far_x, swap(far_x, 1)]
    sums = sum_small(
        jnp.stack([jnp.sum(jnp.abs(out_latent), axis=0), jnp.sum(jnp.abs(down_latent), axis=0)])
    )
    w_qkv = (jnp.mean(jnp.abs(qkv_latent), axis=0) * jnp.sign(qkv_latent)).astype(BF16)
    w_out = (sums[0] / model_width * jnp.sign(out_latent)).astype(BF16)
    w_up = (jnp.mean(jnp.abs(up_latent), axis=0) * jnp.sign(up_latent)).astype(BF16)
    w_down = (sums[1] / (hid * group) * jnp.sign(down_latent)).astype(BF16)
    seg_lanes, blocked = segment_tables(seg_lengths[0], parents[0])
    base = jnp.stack([(me ^ j) * own_rows for j in range(group)]).astype(jnp.int32)

    up_t = teacher_up.T
    bias_rows = jnp.pad(teacher_up_bias.reshape(2, 1, half), ((0, 0), (0, 15), (0, model_width - half)))
    pack = jnp.concatenate(
        [up_t.reshape(2, half, -1), teacher_down.reshape(2, half, -1), bias_rows], axis=1
    )
    pack, far_x = lax.optimization_barrier((pack, far_x))
    side = lax.rem(lax.axis_index("dp"), 2)
    far_a = swap(lax.dynamic_index_in_dim(pack, side, 0, keepdims=False), 2)
    far_b = lax.ppermute(far_a, "dp", [(i, i ^ 1) for i in range(lax.axis_size("dp"))])
    packs = [pack, swap(pack, 1), far_a, far_b, swap(far_a, 1), swap(far_b, 1)]
    outs = jnp.concatenate([w_out, teacher_out])
    outs = gather_blocks(outs)
    w_out_all = jnp.concatenate([block[:local_cols] for block in outs])
    t_out_all = jnp.concatenate([block[local_cols:] for block in outs])

    wide_qkv, wide_bias = padded_heads(w_qkv, qv_bias)
    qkv, context, x_in_all, ca_own, ca_near, ca_far = attend_forward(
        base, blocks, wide_qkv, wide_bias, seg_lanes, blocked, True
    )
    (t_context,) = attend_forward(
        base, blocks, *padded_heads(teacher_qkv, teacher_qv_bias), seg_lanes, blocked, False
    )
    ca_23 = swap(ca_far, 2)
    cas = [ca_own, swap(ca_near, 1), ca_23, swap(ca_23[1], 1)]
    vectors = [out_bias, norm1_gain, norm1_shift, down_bias, norm2_gain, norm2_shift, up_bias]
    vectors += [teacher_out_bias, teacher_norm1_gain, teacher_norm1_shift]
    vectors += [teacher_down_bias, teacher_norm2_gain, teacher_norm2_shift]
    vectors = jnp.pad(jnp.stack(vectors).astype(F32), ((0, 3), (0, 0)))
    out_own, grad_h, ffn_grads, out_grads, g0, g1, g2, g3, small = middle(
        tokens, cas, t_context, w_out_all, t_out_all, w_up, w_down, vectors, packs
    )
    ffn_share = lax.psum_scatter(ffn_grads, "dp", scatter_dimension=0, tiled=True)
    ffn_grads = lax.all_gather(ffn_share, "dp", axis=0, tiled=True).astype(F32)

    weight_grad, proj_bias_grad, gx_own, gx_near, gx_far = attend_backward(
        qkv, context, x_in_all, wide_qkv, [g0, g1, g2, g3]
    )
    out_grad = reduce_blocks([out_grads[j].astype(F32) for j in range(group)])
    gx_near = swap(gx_near, 1).astype(F32)
    gx_far = swap((gx_far + gx_near[1]).astype(BF16), 2).astype(F32)
    grad_x_in = gx_own + gx_near[0] + gx_far
    input_grad = grad_h + grad_x_in * clip_slope(tokens.astype(F32))

    shared = sum_small(small[:7])
    tree_loss = jnp.sum(shared[6])[None] / (all_rows * model_width)
    proj_bias_grad = proj_bias_grad.reshape(local_heads, 3, LANES)[:, :, :HEAD_DIM]
    proj_bias_grad = proj_bias_grad.transpose(1, 0, 2).reshape(3, local_cols)
    small = jnp.concatenate(
        [
            shared[:6].reshape(-1),
            small[7],
            proj_bias_grad[0] * 0.125,
            proj_bias_grad[2],
        ]
    )
    small = lax.psum(small, "dp")
    shared = small[: 6 * model_width].reshape(6, model_width)
    late = reduce_dp(
        jnp.concatenate([weight_grad.reshape(-1, model_width).astype(F32), out_grad])
    )
    qkv_rows = 3 * local_cols
    qkv_grad = late[:qkv_rows].reshape(local_heads, 3, HEAD_DIM, model_width)
    qkv_grad = qkv_grad.transpose(3, 1, 0, 2).reshape(model_width, 3, local_cols)
    return (
        out_own,
        tree_loss,
        input_grad,
        qkv_grad,
        small[6 * model_width + hid :].reshape(2, local_cols),
        late[qkv_rows:],
        shared[0],
        shared[1],
        shared[2],
        ffn_grads[:model_width],
        small[6 * model_width : 6 * model_width + hid],
        ffn_grads[model_width:],
        shared[3],
        shared[4],
        shared[5],
    )


def solution(mesh):
    rows, cols = ("dp", "tensor"), "tensor"
    vec = P()
    params = (
        P(None, None, cols),
        P(None, cols),
        P(cols, None),
        vec,
        vec,
        vec,
        P(None, cols),
        P(cols),
        P(cols, None),
        vec,
        vec,
        vec,
    )
    in_specs = (P(rows, None), P("dp", None), P("dp", None)) + params + params
    out_specs = (P(rows, None), P("dp"), P(rows, None)) + params
    return jax.shard_map(body, mesh=mesh, in_specs=in_specs, out_specs=out_specs, check_vma=False)
```

```python
import functools

import jax
import jax.numpy as jnp
from jax import lax
from jax.experimental import pallas as pl
from jax.experimental.pallas import tpu as pltpu
from jax.sharding import PartitionSpec as P

HEAD_DIM = 64
LANES = 128
CLIP_RANGE = 3.0
NORM_EPSILON = 1e-05
MASKED_SCORE = -1e30
SEG_LANE = HEAD_DIM
ROW_TERM = HEAD_DIM + 16
Q_BLOCK = 256
CHUNKS = 2
BF16, F32 = jnp.bfloat16, jnp.float32
ROWS_ROWS = (((0,), (0,)), ((), ()))
COLS_COLS = (((1,), (1,)), ((), ()))


def clip_act(values):
    return CLIP_RANGE * jnp.tanh(values / CLIP_RANGE)


def clip_slope(values):
    level = jnp.tanh(values / CLIP_RANGE)
    return 1.0 - level * level


def normal_parts(values):
    bell = jnp.exp(-0.5 * values * values)
    step = 1.0 / (1.0 + 0.23164188843 * jnp.abs(values))
    series = 0.5307027145 * step - 0.7265760135
    series = series * step + 0.7107068705
    series = series * step - 0.142248368
    series = series * step + 0.127414796
    tail = series * step * bell
    return jnp.where(values >= 0.0, 1.0 - tail, tail), bell


def norm_forward(hidden, gain, shift):
    row_mean = jnp.mean(hidden, axis=-1, keepdims=True)
    centred = hidden - row_mean
    inv_std = lax.rsqrt(jnp.mean(centred * centred, axis=-1, keepdims=True) + NORM_EPSILON)
    normed = centred * inv_std
    return (normed * gain + shift, normed, inv_std)


def norm_backward(grad_out, normed, inv_std, gain):
    grad_normed = grad_out * gain
    centre = jnp.mean(grad_normed, axis=-1, keepdims=True)
    inner_sum = jnp.mean(grad_normed * normed, axis=-1, keepdims=True)
    return inv_std * (grad_normed - centre - normed * inner_sum)


def dot(left, right):
    return jnp.dot(left, right, preferred_element_type=F32)


def dot_rows(left, right):
    return lax.dot_general(left, right, ROWS_ROWS, preferred_element_type=F32)


def dot_cols(left, right):
    return lax.dot_general(left, right, COLS_COLS, preferred_element_type=F32)


def swap(array, bit):
    size = lax.axis_size("tensor")
    return lax.ppermute(array, "tensor", [(i, i ^ bit) for i in range(size)])


def gather_blocks(own):
    far = swap(own, 2)
    near = swap(own, 1)
    return [own, near, far, swap(far, 1)]


def sum_small(array):
    array = array + swap(array, 1)
    return array + swap(array, 2)


def lookup(indices, lookup_table):
    labels = jnp.arange(lookup_table.shape[0], dtype=jnp.int32)
    picked = jnp.where(indices[:, None] == labels[None, :], lookup_table[None, :], 0)
    return jnp.sum(picked, axis=1)


def segment_tables(lengths, parent):
    count = lengths.shape[0]
    labels = jnp.arange(count, dtype=jnp.int32)
    row, col = labels[:, None], labels[None, :]
    starts = jnp.sum(jnp.where(col < row, lengths[None, :], 0), axis=1)
    two = lookup(parent, parent)
    allowed = (col == row) | (col == parent[:, None]) | (col == two[:, None])
    allowed = allowed | (parent[None, :] == row) | (two[None, :] == row)
    after = LANES - SEG_LANE - count
    lanes = jnp.pad(jnp.stack([starts, starts + lengths]), ((0, 6), (SEG_LANE, after)))
    blocked = jnp.pad((~allowed).astype(BF16), ((SEG_LANE, after), (SEG_LANE, after)))
    return lanes, blocked


def split_three(values):
    first = values.astype(BF16).astype(F32)
    second = (values - first).astype(BF16).astype(F32)
    return first, second, values - first - second


def in_lane(shape, axis, terms):
    lane = lax.broadcasted_iota(jnp.int32, shape, axis)
    spread = jnp.zeros(shape, F32)
    for offset, term in enumerate(terms):
        spread = jnp.where(lane == ROW_TERM + offset, term, spread)
    return spread


def forward_kernel(base_ref, x0, x1, x2, x3, w_ref, b_ref, seg_ref, blocked_ref, *rest, student):
    if student:
        qkv_ref, ctx_ref, source, own, near, far, joined, query_part, key_part, keys, vals_t = rest
    else:
        sent, source, joined, query_part, key_part, keys, vals_t = rest
    blocks = (x0, x1, x2, x3)
    own_rows = x0.shape[0]
    rows = own_rows * len(blocks)
    head = pl.program_id(0)

    @pl.when(head == 0)
    def _():
        lane = lax.broadcasted_iota(jnp.int32, (own_rows, LANES), 1)
        for j, block in enumerate(blocks):
            part = slice(j * own_rows, (j + 1) * own_rows)
            if student:
                source[part, :] = clip_act(block[...].astype(F32)).astype(BF16)
            else:
                source[part, :] = block[...]
            place = lax.broadcasted_iota(jnp.int32, (own_rows, LANES), 0) + base_ref[j]
            inside = (place >= seg_ref[0:1, :]) & (place < seg_ref[1:2, :])
            query_part[part, :] = jnp.where(inside, MASKED_SCORE, 0.0).astype(BF16)
            links = dot(jnp.where(inside, 1.0, 0.0).astype(BF16), blocked_ref[...])
            ones = (lane >= ROW_TERM) & (lane < ROW_TERM + 3)
            key_part[part, :] = jnp.where(ones, 1.0, links).astype(BF16)

    proj = (dot(source[...], w_ref[0]) + b_ref[0]).astype(BF16)
    queries = proj[:, :LANES] + query_part[...]
    keys[...] = proj[:, LANES : 2 * LANES] + key_part[...]
    vals_t[...] = proj[:, 2 * LANES :].T
    if student:
        qkv_ref[:, LANES : 2 * LANES] = keys[...]
        lane = lax.broadcasted_iota(jnp.int32, (rows, LANES), 1)
        ones = jnp.where((lane >= ROW_TERM) & (lane < ROW_TERM + 3), 1.0, 0.0).astype(BF16)
        qkv_ref[:, 2 * LANES :] = proj[:, 2 * LANES :] + ones
    scores = []
    for start in range(0, rows, Q_BLOCK):
        scores.append(dot_cols(keys[...], queries[start : start + Q_BLOCK]))
    for index, block in enumerate(scores):
        part = slice(index * Q_BLOCK, (index + 1) * Q_BLOCK)
        peak = jnp.max(block, axis=0, keepdims=True)
        raised = jnp.exp(block - peak)
        total = jnp.sum(raised, axis=0, keepdims=True)
        weights = (raised * (1.0 / total)).astype(BF16)
        context = dot(vals_t[...], weights)[:HEAD_DIM].T
        joined[head, part, :] = context
        if student:
            ctx_ref[0, part, :] = context
            terms = split_three(-(peak + jnp.log(total)))
            spread = in_lane((LANES, Q_BLOCK), 0, terms)
            qkv_ref[part, :LANES] = queries[part] + spread.T.astype(BF16)

    @pl.when(head == pl.num_programs(0) - 1)
    def _():
        for j in range(len(blocks)):
            part = slice(j * own_rows, (j + 1) * own_rows)
            block = jnp.concatenate([joined[h, part, :] for h in range(joined.shape[0])], axis=1)
            if not student:
                sent[j] = block.astype(BF16)
            elif j < 2:
                (own, near)[j][...] = clip_act(block).astype(BF16)
            else:
                far[j - 2] = clip_act(block).astype(BF16)


def attend_forward(base, blocks, weight, bias, seg_lanes, blocked, student):
    own_rows, width = blocks[0].shape
    rows = own_rows * len(blocks)
    heads = weight.shape[0]
    cols = 3 * LANES
    head_cols = heads * HEAD_DIM
    whole = lambda *shape: pl.BlockSpec(shape, lambda h: (0,) * len(shape))
    array = jax.ShapeDtypeStruct
    if student:
        out_specs = [
            pl.BlockSpec((rows, cols), lambda h: (0, h)),
            pl.BlockSpec((1, rows, HEAD_DIM), lambda h: (h, 0, 0)),
            whole(rows, width),
            whole(own_rows, head_cols),
            whole(own_rows, head_cols),
            whole(2, own_rows, head_cols),
        ]
        out_shape = [
            array((rows, heads * cols), BF16),
            array((heads, rows, HEAD_DIM), F32),
            array((rows, width), BF16),
            array((own_rows, head_cols), BF16),
            array((own_rows, head_cols), BF16),
            array((2, own_rows, head_cols), BF16),
        ]
        scratch = []
    else:
        out_specs = [whole(len(blocks), own_rows, head_cols)]
        out_shape = [array((len(blocks), own_rows, head_cols), BF16)]
        scratch = [pltpu.VMEM((rows, width), BF16)]
    scratch += [
        pltpu.VMEM((heads, rows, HEAD_DIM), F32),
        pltpu.VMEM((rows, LANES), BF16),
        pltpu.VMEM((rows, LANES), BF16),
        pltpu.VMEM((rows, LANES), BF16),
        pltpu.VMEM((LANES, rows), BF16),
    ]
    return pl.pallas_call(
        functools.partial(forward_kernel, student=student),
        grid=(heads,),
        in_specs=[pl.BlockSpec(memory_space=pltpu.SMEM)]
        + [whole(own_rows, width)] * 4
        + [
            pl.BlockSpec((1, width, cols), lambda h: (h, 0, 0)),
            pl.BlockSpec((1, 1, cols), lambda h: (h, 0, 0)),
            whole(*seg_lanes.shape),
            whole(*blocked.shape),
        ],
        out_specs=out_specs,
        out_shape=out_shape,
        scratch_shapes=scratch,
        compiler_params=pltpu.CompilerParams(vmem_limit_bytes=58 * 2**20),
        cost_estimate=pl.CostEstimate(
            flops=16 * heads * rows * rows * HEAD_DIM,
            bytes_accessed=2 * rows * (width + 2 * heads * cols),
            transcendentals=heads * rows * rows,
        ),
        name="student_attention" if student else "teacher_attention",
    )(base, *blocks, weight, bias, seg_lanes, blocked)


def in_pair(place, bit):
    digit = lax.rem(lax.div(place, bit), 2)
    return place + bit - 2 * bit * digit, digit


def halving_steps(partial, total, landing, rows, landing_row, order, place, copy_of, done=0, base=None):
    low, size = rows
    here = low if base is None else base
    steps, levels, used = [], [], landing_row
    for level, bit in enumerate(order):
        partner, digit = in_pair(place, bit)
        halved = size % 32 == 0
        count = size // 2 if halved else size
        low = pl.multiple_of(low + digit * count, 16) if halved else low
        if level >= done:
            give = pl.multiple_of(here + (1 - digit) * count, 16) if halved else here
            here = pl.multiple_of(here + digit * count, 16) if halved else here
            copy = copy_of(partial.at[pl.ds(give, count)], landing.at[pl.ds(used, count)], partner)
            last = level == len(order) - 1

            def add(used=used, here=here, count=count, out=total if last else partial, at=low if last else here):
                arrived = landing[used : used + count, :].astype(F32)
                mine = partial[pl.ds(here, count), :].astype(F32)
                out[pl.ds(at, count), :] = (mine + arrived).astype(out.dtype)

            steps.append((copy, add))
            used += count
        if halved:
            levels.append((count, low, partner))
        size = count
    for count, keep, partner in reversed(levels):
        where = total.at[pl.ds(keep, count)]
        steps.append((copy_of(where, where, partner), lambda: None))
    return steps, used


def run_step(plans, index):
    for steps in plans:
        if 0 < index <= len(steps):
            copy, after = steps[index - 1]
            copy().wait()
            after()
        if index < len(steps):
            steps[index][0]().start()


def split_rows(first, count):
    large = count * 2 // 3 // 64 * 64
    return ((first, large), (first + large, count - large))


def dp_bits():
    bits = [1 << i for i in range((lax.axis_size("dp") - 1).bit_length())]
    return bits, (bits[1:] + bits[:1])


def backward_kernel(
    qkv_ref, ctx_ref, x_ref, w_ref, g0, g1, g2, g3, ffn_ref, outg_ref, small_ref,
    ffn_out, late_out, small_out, gx_out, gxfar_out,
    grads, packed, keys_t, total, ffn_part, ffn, late_in, late, small, small_in, landing, small_land,
    out_near, out_near_land, out_far, out_far_land, gx_near, gx_near_land, gx_far, gx_far_land,
    send_sem, recv_sem, *, key_block,
):
    blocks = (g0, g1, g2, g3)
    own_rows = g0.shape[0]
    rows = own_rows * len(blocks)
    heads = grads.shape[0]
    head_cols = heads * HEAD_DIM
    head = pl.program_id(0)
    group = lax.axis_size("tensor")
    me, place = lax.axis_index("tensor"), lax.axis_index("dp")
    near_id = me + 1 - 2 * lax.rem(me, 2)
    far_id = lax.rem(me + 2, group)
    part = lambda j: slice(j * own_rows, (j + 1) * own_rows)
    bits, turned = dp_bits()

    count = [0]
    sends = []

    def copy_to(source, target, device):
        index = count[0]
        count[0] += 1

        def make():
            return pltpu.make_async_remote_copy(
                src_ref=source,
                dst_ref=target,
                send_sem=send_sem.at[index],
                recv_sem=recv_sem.at[index],
                device_id=device,
                device_id_type=pl.DeviceIdType.MESH,
            )

        sends.append(make)
        return make

    over_dp = lambda source, target, other: copy_to(source, target, {"dp": other})
    over_tensor = lambda source, target, other: copy_to(source, target, {"tensor": other})

    used = [0]

    def reduced(partial, target, first, size, done=0):
        plans, taken = [], 0
        for rows_of, order in zip(split_rows(first, size), (bits, turned)):
            steps, used[0] = halving_steps(
                partial, target, landing, rows_of, used[0], order, place, over_dp, done,
                taken if done else None,
            )
            plans.append(steps)
            taken += rows_of[1] // 2
        return plans

    width = x_ref.shape[1]
    ffn_plans = reduced(ffn_part, ffn, 0, ffn.shape[0], 1)
    early_plans = reduced(late_in, late, 0, 2 * head_cols)
    middle_plans = reduced(late_in, late, 2 * head_cols, head_cols)
    last_plans = reduced(late_in, late, 3 * head_cols, head_cols)
    small_steps = []
    for level, bit in enumerate(bits):
        partner, _ = in_pair(place, bit)
        small_steps.append(over_dp(small_in.at[level], small_land.at[level], partner))
    tensor_small = [
        over_tensor(small.at[0], small.at[1], near_id),
        over_tensor(small.at[2], small.at[3], far_id),
    ]
    out_steps = [
        over_tensor(out_near, out_near_land, near_id),
        over_tensor(out_far, out_far_land, far_id),
    ]
    gx_steps = [
        over_tensor(gx_near, gx_near_land, near_id),
        over_tensor(gx_far, gx_far_land, far_id),
    ]

    @pl.when(head == 0)
    def _():
        barrier = pltpu.get_barrier_semaphore()
        others = [{"tensor": near_id}, {"tensor": far_id}]
        others += [{"dp": in_pair(place, bit)[0]} for bit in bits]
        for other in others:
            pl.semaphore_signal(
                barrier, inc=1, device_id=other, device_id_type=pl.DeviceIdType.MESH
            )
        pl.semaphore_wait(barrier, len(others))
        ffn_part[...] = ffn_ref[...]
        run_step(ffn_plans, 0)
        out_near[0] = outg_ref[1]
        out_near[1] = outg_ref[3]
        out_steps[0]().start()
        small[0] = small_ref[...]
        tensor_small[0]().start()
        for h in range(heads):
            for j, block in enumerate(blocks):
                one = block[:, h * HEAD_DIM : (h + 1) * HEAD_DIM].astype(F32)
                grads[h, part(j), :] = jnp.concatenate(
                    [one, jnp.zeros_like(one)], axis=1
                ).astype(BF16)
        packed[...] = jnp.zeros_like(packed)

    queries = qkv_ref[:, :LANES]
    slopes = grads[head]
    inner = -jnp.sum(slopes[:, :HEAD_DIM].astype(F32) * ctx_ref[0], axis=1, keepdims=True)
    slopes = slopes + in_lane((rows, LANES), 1, split_three(inner)).astype(BF16)
    keys_t[...] = qkv_ref[:, LANES : 2 * LANES].T

    def over_keys(first, last, query_grad):
        for start in range(first, last, key_block):
            span = slice(start, start + key_block)
            weights = jnp.exp(dot_cols(qkv_ref[span, LANES : 2 * LANES], queries))
            grad_weights = dot_cols(qkv_ref[span, 2 * LANES :], slopes)
            grad_scores = (weights * grad_weights).astype(BF16)
            step = dot(keys_t[:, span], grad_scores)
            query_grad = step if query_grad is None else query_grad + step
            key_grad = dot(grad_scores, queries)[:, :HEAD_DIM]
            packed[span, LANES : LANES + HEAD_DIM] = key_grad.astype(BF16)
            value_grad = dot(weights.astype(BF16), slopes)[:, :HEAD_DIM]
            packed[span, 2 * LANES : 2 * LANES + HEAD_DIM] = value_grad.astype(BF16)
        return query_grad

    query_grad = over_keys(0, rows // 2, None)

    @pl.when(head == 0)
    def _():
        out_steps[0]().wait_recv()
        out_far[...] = (outg_ref[2].astype(F32) + out_near_land[1].astype(F32)).astype(BF16)
        out_steps[1]().start()
        tensor_small[0]().wait_recv()
        small[2] = small[0] + small[1]
        tensor_small[1]().start()

    @pl.when(head == 1)
    def _():
        run_step(ffn_plans, 2)
        run_step(early_plans, 1)

    @pl.when(head == 2)
    def _():
        run_step(ffn_plans, 4)
        run_step(early_plans, 3)
        run_step(middle_plans, 1)

    query_grad = over_keys(rows // 2, rows, query_grad)
    packed[:, :HEAD_DIM] = query_grad[:HEAD_DIM].T.astype(BF16)
    sums = jnp.sum(packed[...].astype(F32), axis=0, keepdims=True)
    small[4 + head, 0:1, : 3 * LANES] = sums
    weight_grad = dot_rows(packed[...], x_ref[...])
    slot = jnp.where(head == 0, 0, head_cols + head * head_cols)
    for c, factor in enumerate((0.125, 1.0, 1.0)):
        target = pl.multiple_of(slot + c * HEAD_DIM, HEAD_DIM)
        late_in[pl.ds(target, HEAD_DIM), :] = (
            weight_grad[c * LANES : c * LANES + HEAD_DIM] * factor
        ).astype(BF16)

    @pl.when(head == 0)
    def _():
        out_steps[1]().wait_recv()
        late_in[head_cols : 2 * head_cols, :] = (
            outg_ref[0].astype(F32)
            + out_near_land[0].astype(F32)
            + out_far_land[...].astype(F32)
        ).astype(BF16)
        tensor_small[1]().wait_recv()
        run_step(ffn_plans, 1)
        run_step(early_plans, 0)

    @pl.when(head == 1)
    def _():
        run_step(middle_plans, 0)
        run_step(ffn_plans, 3)
        run_step(early_plans, 2)

    @pl.when(head == 2)
    def _():
        run_step(last_plans, 0)
        small_in[0, :8, :] = small[2] + small[3]
        small_in[0, UP_ROW : UP_ROW + 1, :] = small_ref[UP_ROW : UP_ROW + 1, :]
        small_in[0, 8:, :] = jnp.zeros((8, width), F32)
        for h in range(heads):
            small_in[0, 8 + h : 9 + h, : 3 * LANES] = small[4 + h, 0:1, : 3 * LANES]
        small_steps[0]().start()

    for j in (1, 3, 2, 0):
        step = dot_cols(packed[part(j), :], w_ref[0])
        total[part(j), :] = jnp.where(head == 0, step, total[part(j), :] + step)

    @pl.when(head == heads - 1)
    def _():
        gx_near[0] = total[part(1), :].astype(BF16)
        gx_near[1] = total[part(3), :].astype(BF16)
        gx_steps[0]().start()
        run_step(ffn_plans, 5)
        run_step(early_plans, 4)
        run_step(middle_plans, 2)
        run_step(last_plans, 1)
        gx_steps[0]().wait_recv()
        gx_far[...] = (total[part(2), :] + gx_near_land[1].astype(F32)).astype(BF16)
        gx_steps[1]().start()
        gx_out[...] = total[part(0), :] + gx_near_land[0].astype(F32)
        for index in range(1, 2 * len(bits) + 1):
            if index > 1:
                run_step(last_plans, index)
            if index <= len(bits):
                small_steps[index - 1]().wait_recv()
                arrived = small_in[index - 1] + small_land[index - 1]
                if index < len(bits):
                    small_in[index] = arrived
                    small_steps[index]().start()
                else:
                    small_out[...] = arrived
            run_step(middle_plans, 2 + index)
            run_step(early_plans, 4 + index)
            run_step(ffn_plans, 5 + index)
        ffn_out[...] = ffn[...]
        late_out[...] = late[...]
        gx_steps[1]().wait_recv()
        gxfar_out[...] = gx_far_land[...]
        shared = small[2, LOSS_ROW : LOSS_ROW + 1, :] + small[3, LOSS_ROW : LOSS_ROW + 1, :]
        small_out[LOSS_ROW : LOSS_ROW + 1, :] = shared
        for copy in small_steps + tensor_small + out_steps + gx_steps:
            copy().wait_send()


def attend_backward(qkv, context, source, weight, blocks, ffn_grads, out_grads, small):
    rows, width = source.shape
    own_rows, head_cols = blocks[0].shape
    cols = 3 * LANES
    heads = weight.shape[0]
    levels = (lax.axis_size("dp") - 1).bit_length()
    ffn_rows, late_rows = 2 * ffn_grads.shape[0], (heads + 1) * head_cols
    landing = ffn_rows + late_rows + 8 * 48 * levels
    transfers = 2 * 4 * 2 * levels + levels + 6
    array = jax.ShapeDtypeStruct
    whole = lambda *shape: pl.BlockSpec(shape, lambda h: (0,) * len(shape))
    head_block = lambda *shape: pl.BlockSpec((1,) + shape, lambda h: (h, 0, 0))
    return pl.pallas_call(
        functools.partial(backward_kernel, key_block=256),
        grid=(heads,),
        in_specs=[
            pl.BlockSpec((rows, cols), lambda h: (0, h)),
            head_block(rows, HEAD_DIM),
            whole(rows, width),
            head_block(width, cols),
        ]
        + [whole(own_rows, head_cols)] * 4
        + [whole(*ffn_grads.shape), whole(*out_grads.shape), whole(*small.shape)],
        out_specs=[
            whole(ffn_rows, width),
            whole(late_rows, width),
            whole(16, width),
            whole(own_rows, width),
            whole(own_rows, width),
        ],
        out_shape=[
            array((ffn_rows, width), BF16),
            array((late_rows, width), BF16),
            array((16, width), F32),
            array((own_rows, width), F32),
            array((own_rows, width), BF16),
        ],
        scratch_shapes=[
            pltpu.VMEM((heads, rows, LANES), BF16),
            pltpu.VMEM((rows, cols), BF16),
            pltpu.VMEM((LANES, rows), BF16),
            pltpu.VMEM((rows, width), F32),
            pltpu.VMEM((ffn_rows // 2, width), BF16),
            pltpu.VMEM((ffn_rows, width), BF16),
            pltpu.VMEM((late_rows, width), BF16),
            pltpu.VMEM((late_rows, width), BF16),
            pltpu.VMEM((4 + heads, 8, width), F32),
            pltpu.VMEM((levels, 16, width), F32),
            pltpu.VMEM((landing, width), BF16),
            pltpu.VMEM((levels, 16, width), F32),
            pltpu.VMEM((2, head_cols, width), BF16),
            pltpu.VMEM((2, head_cols, width), BF16),
            pltpu.VMEM((head_cols, width), BF16),
            pltpu.VMEM((head_cols, width), BF16),
            pltpu.VMEM((2, own_rows, width), BF16),
            pltpu.VMEM((2, own_rows, width), BF16),
            pltpu.VMEM((own_rows, width), BF16),
            pltpu.VMEM((own_rows, width), BF16),
            pltpu.SemaphoreType.DMA((transfers,)),
            pltpu.SemaphoreType.DMA((transfers,)),
        ],
        compiler_params=pltpu.CompilerParams(
            collective_id=4, has_side_effects=True, vmem_limit_bytes=62 * 2**20
        ),
        cost_estimate=pl.CostEstimate(
            flops=60 * heads * rows * rows * HEAD_DIM,
            bytes_accessed=2 * rows * heads * (cols + 7 * LANES),
            transcendentals=heads * rows * rows,
        ),
        name="attention_backward",
    )(qkv, context, source, weight, *blocks, ffn_grads, out_grads, small)


(OUT_BIAS, GAIN_1, SHIFT_1, DOWN_BIAS, GAIN_2, SHIFT_2, UP_BIAS) = range(7)
T_VECTORS = 7
LOSS_ROW, UP_ROW = 6, 7


def middle_kernel(
    x_ref, ca0, ca1, ca23, ca3, tc_ref, w_out, tw_out, w_up, w_down, vec,
    pack_own, pack_near, pack_a, pack_b, pack_c, pack_d,
    out_ref, gh_ref, kept_ref, outg_ref, g0_ref, g1_ref, g2_ref, g3_ref, small_ref,
    tc1, tc2, tcf, tc3, y_all, g_all, slope, hid, gu_all, t_out, first, normed, two, inv,
    part0, part2, send1, send2, send3, near0, near2, far0, gs, gr, packs, ffn_ref, ffn_land,
    send_sem, recv_sem, pack_sem,
):
    me = lax.axis_index("tensor")
    near_id = me + 1 - 2 * lax.rem(me, 2)
    far_id = lax.rem(me + 2, 4)
    own_rows, width = x_ref.shape
    hidden = w_down.shape[0]
    head_cols = ca0.shape[1]
    size = own_rows // CHUNKS
    chunks = [slice(c * size, (c + 1) * size) for c in range(CHUNKS)]
    tiles = [slice(n, n + 256) for n in range(0, hidden, 256)]
    group = lambda j: slice(j * head_cols, (j + 1) * head_cols)
    row = lambda index: vec[index : index + 1, :]

    place = lax.axis_index("dp")
    first_bits = [order[0] for order in dp_bits()]
    others = [{"tensor": near_id}, {"tensor": far_id}]
    others += [{"dp": in_pair(place, bit)[0]} for bit in first_bits]
    barrier = pltpu.get_barrier_semaphore()
    for other in others:
        pl.semaphore_signal(barrier, inc=1, device_id=other, device_id_type=pl.DeviceIdType.MESH)
    pl.semaphore_wait(barrier, len(others))

    count = [0]
    started = []

    def put(source, target, device, axis="tensor"):
        index = count[0]
        count[0] += 1
        copy = pltpu.make_async_remote_copy(
            src_ref=source,
            dst_ref=target,
            send_sem=send_sem.at[index],
            recv_sem=recv_sem.at[index],
            device_id={axis: device},
            device_id_type=pl.DeviceIdType.MESH,
        )
        copy.start()
        started.append(copy)
        return copy

    t_far = put(tc_ref.at[2], tc2, far_id)
    t_pass = put(tc_ref.at[3], tcf, far_id)
    t_near = put(tc_ref.at[1], tc1, near_id)

    pack_refs = [pack_own.at[0], pack_own.at[1], pack_near.at[0], pack_near.at[1]]
    pack_refs += [pack_a, pack_b, pack_c, pack_d]

    def load_pack(index):
        slot = index % 2
        return pltpu.make_async_copy(pack_refs[index], packs.at[slot], pack_sem.at[slot])

    load_pack(0).start()
    small_ref[...] = jnp.zeros_like(small_ref)

    def add_small(index, values):
        small_ref[index : index + 1, :] += jnp.sum(values, axis=0, keepdims=True)

    def share(own_block, where):
        return (
            put(own_block.at[0, where], own_block.at[1, where], near_id),
            put(own_block.at[0, where], own_block.at[2, where], far_id),
        )

    y_sent = []
    for rows in chunks:
        attn = dot(ca0[rows, :], w_out[group(0), :]) + dot(ca1[rows, :], w_out[group(1), :])
        attn += dot(ca23[0, rows, :], w_out[group(2), :]) + dot(ca3[rows, :], w_out[group(3), :])
        y_one, y_normed, y_inv = norm_forward(
            x_ref[rows, :].astype(F32) + attn + row(OUT_BIAS), row(GAIN_1), row(SHIFT_1)
        )
        first[rows, :] = y_one
        normed[rows, :] = y_normed
        inv[rows, :] = jnp.broadcast_to(y_inv, (size, LANES))
        y_all[0, rows, :] = clip_act(y_one).astype(BF16)
        y_sent.append(share(y_all, rows))

    def forward_block(j, rows):
        total = None
        for cols in tiles:
            upward = dot(y_all[j, rows, :], w_up[:, cols]) + row(UP_BIAS)[:, cols]
            cdf, bell = normal_parts(upward)
            level = jnp.tanh(upward * cdf * (1.0 / CLIP_RANGE))
            act = (CLIP_RANGE * level).astype(BF16)
            hid[j, rows, cols] = act
            slope[j, rows, cols] = (1.0 - level * level) * (
                cdf + upward * bell * 0.3989422804014327
            )
            step = dot(act, w_down[cols, :])
            total = step if total is None else total + step
        return total

    def backward_block(j, rows):
        total = None
        for cols in tiles:
            grad = dot_cols(g_all[j, rows, :], w_down[cols, :])
            grad = (grad * slope[j, rows, cols]).astype(BF16)
            gu_all[j, rows, cols] = grad
            small_ref[UP_ROW : UP_ROW + 1, cols] += jnp.sum(
                grad.astype(F32), axis=0, keepdims=True
            )
            step = dot_cols(grad, w_up[:, cols])
            total = step if total is None else total + step
        return total

    def near_blocks(work, sent):
        copies = []
        for rows in chunks:
            part0[rows, :] = work(0, rows)
        for rows, (near, _) in zip(chunks, sent):
            near.wait_recv()
            send1[rows, :] = work(1, rows).astype(BF16)
            copies.append(put(send1.at[rows], near0.at[rows], near_id))
        return copies

    def far_blocks(block, work, sent):
        copies = []
        for rows, (_, far) in zip(chunks, sent):
            far.wait_recv()
            passed = put(block.at[2, rows], block.at[3, rows], near_id)
            part2[rows, :] = work(2, rows)
            passed.wait_recv()
            send3[rows, :] = work(3, rows).astype(BF16)
            met = put(send3.at[rows], near2.at[rows], near_id)
            met.wait_recv()
            send2[rows, :] = (part2[rows, :] + near2[rows, :].astype(F32)).astype(BF16)
            copies.append(put(send2.at[rows], far0.at[rows], far_id))
        return copies

    def summed(rows, near, far):
        near.wait_recv()
        far.wait_recv()
        return part0[rows, :] + near0[rows, :].astype(F32) + far0[rows, :].astype(F32)

    y_near = near_blocks(forward_block, y_sent)

    t_pass.wait_recv()
    t_last = put(tcf, tc3, near_id)
    t_near.wait_recv()
    t_far.wait_recv()
    t_row = lambda index: row(T_VECTORS + index)
    t_attn = dot(tc_ref[0], tw_out[group(0), :]) + dot(tc1[...], tw_out[group(1), :])
    t_attn += dot(tc2[...], tw_out[group(2), :])
    t_last.wait_recv()
    t_attn += dot(tc3[...], tw_out[group(3), :])
    t_one, _, _ = norm_forward(x_ref[...].astype(F32) + t_attn + t_row(0), t_row(1), t_row(2))
    two[...] = t_one
    t_out[...] = t_one + t_row(3)
    half = hidden // 2
    t_in = t_one.astype(BF16)
    for index in range(len(pack_refs)):
        slot = index % 2
        if index + 1 < len(pack_refs):
            load_pack(index + 1).start()
        load_pack(index).wait()
        upward = dot_cols(t_in, packs[slot, :half, :])
        upward = upward + packs[slot, hidden : hidden + 1, :half].astype(F32)
        act = (upward * normal_parts(upward)[0]).astype(BF16)
        t_out[...] += dot(act, packs[slot, half:hidden, :])
    t_out[...] = norm_forward(t_out[...], t_row(4), t_row(5))[0]

    y_far = far_blocks(y_all, forward_block, y_sent)

    g_sent = []
    for copy in started:
        copy.wait_send()
    started.clear()
    for rows, near, far in zip(chunks, y_near, y_far):
        ffn = summed(rows, near, far)
        out, n_two, inv_two = norm_forward(
            first[rows, :] + ffn + row(DOWN_BIAS), row(GAIN_2), row(SHIFT_2)
        )
        out_ref[rows, :] = out.astype(BF16)
        gap = out - t_out[rows, :]
        add_small(LOSS_ROW, gap * gap)
        add_small(GAIN_2, gap * n_two)
        add_small(SHIFT_2, gap)
        grad_two = norm_backward(gap, n_two, inv_two, row(GAIN_2))
        two[rows, :] = grad_two
        grad_ffn = grad_two.astype(BF16)
        add_small(DOWN_BIAS, grad_ffn.astype(F32))
        g_all[0, rows, :] = grad_ffn
        g_sent.append(share(g_all, rows))

    g_near = near_blocks(backward_block, g_sent)
    g_far = far_blocks(g_all, backward_block, g_sent)
    flat = lambda block: block[...].reshape(4 * own_rows, block.shape[2])
    ffn_ref[:width, :] = dot_rows(flat(y_all), flat(gu_all)).astype(BF16)
    ffn_ref[width:, :] = dot_rows(flat(hid), flat(g_all)).astype(BF16)
    halves, taken = [], 0
    for (low, size), bit in zip(split_rows(0, width + hidden), first_bits):
        partner, digit = in_pair(place, bit)
        size = size // 2
        give = ffn_ref.at[pl.ds(pl.multiple_of(low + (1 - digit) * size, 16), size)]
        keep = pl.multiple_of(low + digit * size, 16)
        land = slice(taken, taken + size)
        halves.append((put(give, ffn_land.at[land], partner, "dp"), keep, land))
        taken += size

    passes = []
    for c, (rows, near, far) in enumerate(zip(chunks, g_near, g_far)):
        y_one = first[rows, :]
        grad_one = two[rows, :] + summed(rows, near, far) * clip_slope(y_one)
        n_one = normed[rows, :]
        add_small(GAIN_1, grad_one * n_one)
        add_small(SHIFT_1, grad_one)
        grad_h = norm_backward(grad_one, n_one, inv[rows, :1], row(GAIN_1))
        gh_ref[rows, :] = grad_h
        grad_attn = grad_h.astype(BF16)
        add_small(OUT_BIAS, grad_attn.astype(F32))
        for j, ca in enumerate((ca0.at[rows], ca1.at[rows], ca23.at[0, rows], ca3.at[rows])):
            act = ca[...]
            level = act.astype(F32) * (1.0 / CLIP_RANGE)
            grad = dot_cols(grad_attn, w_out[group(j), :]) * (1.0 - level * level)
            gs[j, rows, :] = grad.astype(BF16)
            step = dot_rows(act, grad_attn)
            if c:
                step = step + part2[group(j), :]
            part2[group(j), :] = step
        passes.append(
            (
                put(gs.at[3, rows], gr.at[3, rows], far_id),
                put(gs.at[2, rows], gr.at[1, rows], far_id),
                put(gs.at[1, rows], gr.at[0, rows], near_id),
            )
        )
    g0_ref[...] = gs[0]
    for j in range(4):
        outg_ref[j] = part2[group(j), :].astype(BF16)
    lasts = []
    for rows, (passing, _, _) in zip(chunks, passes):
        passing.wait_recv()
        lasts.append(put(gr.at[3, rows], gr.at[2, rows], near_id))
    for rows, (_, far, near), last in zip(chunks, passes, lasts):
        near.wait_recv()
        g1_ref[rows, :] = gr[0, rows, :]
        far.wait_recv()
        g2_ref[rows, :] = gr[1, rows, :]
        last.wait_recv()
        g3_ref[rows, :] = gr[2, rows, :]
    for copy, keep, land in halves:
        copy.wait_recv()
        mine = ffn_ref[pl.ds(keep, land.stop - land.start), :].astype(F32)
        kept_ref[land, :] = (mine + ffn_land[land, :].astype(F32)).astype(BF16)
    for copy in started:
        copy.wait_send()


def middle(x_own, cas, tc, w_out, tw_out, w_up, w_down, vectors, packs):
    own_rows, width = x_own.shape
    hidden = w_down.shape[0]
    head_cols = cas[0].shape[1]
    array = jax.ShapeDtypeStruct
    vmem = pl.BlockSpec(memory_space=pltpu.VMEM)
    transfers = 4 + 4 * 3 * CHUNKS + 4 * CHUNKS + 2
    square = lambda kind: pltpu.VMEM((own_rows, width), kind)
    four = lambda cols, kind: pltpu.VMEM((4, own_rows, cols), kind)
    return pl.pallas_call(
        middle_kernel,
        in_specs=[vmem] * 11 + [pl.BlockSpec(memory_space=pl.ANY)] * 6,
        out_specs=[vmem] * 9,
        out_shape=[
            array((own_rows, width), BF16),
            array((own_rows, width), F32),
            array(((width + hidden) // 2, width), BF16),
            array((4, head_cols, width), BF16),
        ]
        + [array((own_rows, head_cols), BF16)] * 4
        + [array((8, width), F32)],
        scratch_shapes=[pltpu.VMEM((own_rows, head_cols), BF16)] * 4
        + [four(width, BF16), four(width, BF16), four(hidden, F32), four(hidden, BF16)]
        + [four(hidden, BF16)]
        + [square(F32)] * 4
        + [pltpu.VMEM((own_rows, LANES), F32)]
        + [square(F32), pltpu.VMEM((4 * max(own_rows // 4, head_cols), width), F32)]
        + [square(BF16)] * 6
        + [four(head_cols, BF16), four(head_cols, BF16)]
        + [
            pltpu.VMEM((2,) + packs[2].shape, BF16),
            pltpu.VMEM((width + hidden, width), BF16),
            pltpu.VMEM(((width + hidden) // 2, width), BF16),
            pltpu.SemaphoreType.DMA((transfers,)),
            pltpu.SemaphoreType.DMA((transfers,)),
            pltpu.SemaphoreType.DMA((2,)),
        ],
        compiler_params=pltpu.CompilerParams(
            collective_id=3, has_side_effects=True, vmem_limit_bytes=62 * 2**20
        ),
        cost_estimate=pl.CostEstimate(
            flops=120 * own_rows * width * hidden, bytes_accessed=2**25, transcendentals=2**22
        ),
        name="middle",
    )(x_own, *cas, tc, w_out, tw_out, w_up, w_down, vectors, *packs)


def padded_heads(weight, bias):
    width, _, cols = weight.shape
    heads = cols // HEAD_DIM
    scale = jnp.array([0.125, 1.0, 1.0], F32)
    weight = weight.reshape(width, 3, heads, HEAD_DIM).transpose(2, 0, 1, 3)
    weight = weight * scale[None, None, :, None].astype(weight.dtype)
    weight = jnp.pad(weight, ((0, 0), (0, 0), (0, 0), (0, LANES - HEAD_DIM)))
    full = jnp.stack([bias[0] * 0.125, jnp.zeros_like(bias[0]), bias[1]]).astype(F32)
    full = full.reshape(3, heads, HEAD_DIM).transpose(1, 0, 2)
    full = jnp.pad(full, ((0, 0), (0, 0), (0, LANES - HEAD_DIM)))
    return (
        weight.reshape(heads, width, 3 * LANES).astype(BF16),
        full.reshape(heads, 1, 3 * LANES),
    )


def body(
    tokens,
    seg_lengths,
    parents,
    qkv_latent,
    qv_bias,
    out_latent,
    out_bias,
    norm1_gain,
    norm1_shift,
    up_latent,
    up_bias,
    down_latent,
    down_bias,
    norm2_gain,
    norm2_shift,
    teacher_qkv,
    teacher_qv_bias,
    teacher_out,
    teacher_out_bias,
    teacher_norm1_gain,
    teacher_norm1_shift,
    teacher_up,
    teacher_up_bias,
    teacher_down,
    teacher_down_bias,
    teacher_norm2_gain,
    teacher_norm2_shift,
):
    own_rows, model_width = tokens.shape
    group = lax.axis_size("tensor")
    me = lax.axis_index("tensor")
    all_rows = own_rows * group
    local_cols = qkv_latent.shape[2]
    local_heads = local_cols // HEAD_DIM
    hid = up_latent.shape[1]
    half = hid // 2
    near_x = swap(tokens, 1)
    far_x = swap(tokens, 2)
    blocks = [tokens, near_x, far_x, swap(far_x, 1)]
    sums = sum_small(
        jnp.stack([jnp.sum(jnp.abs(out_latent), axis=0), jnp.sum(jnp.abs(down_latent), axis=0)])
    )
    w_qkv = (jnp.mean(jnp.abs(qkv_latent), axis=0) * jnp.sign(qkv_latent)).astype(BF16)
    w_out = (sums[0] / model_width * jnp.sign(out_latent)).astype(BF16)
    w_up = (jnp.mean(jnp.abs(up_latent), axis=0) * jnp.sign(up_latent)).astype(BF16)
    w_down = (sums[1] / (hid * group) * jnp.sign(down_latent)).astype(BF16)
    seg_lanes, blocked = segment_tables(seg_lengths[0], parents[0])
    base = jnp.stack([(me ^ j) * own_rows for j in range(group)]).astype(jnp.int32)

    up_t = teacher_up.T
    bias_rows = jnp.pad(teacher_up_bias.reshape(2, 1, half), ((0, 0), (0, 15), (0, model_width - half)))
    pack = jnp.concatenate(
        [up_t.reshape(2, half, -1), teacher_down.reshape(2, half, -1), bias_rows], axis=1
    )
    pack, far_x = lax.optimization_barrier((pack, far_x))
    side = lax.rem(lax.axis_index("dp"), 2)
    far_a = swap(lax.dynamic_index_in_dim(pack, side, 0, keepdims=False), 2)
    far_b = lax.ppermute(far_a, "dp", [(i, i ^ 1) for i in range(lax.axis_size("dp"))])
    packs = [pack, swap(pack, 1), far_a, far_b, swap(far_a, 1), swap(far_b, 1)]
    outs = jnp.concatenate([w_out, teacher_out])
    outs = gather_blocks(outs)
    w_out_all = jnp.concatenate([block[:local_cols] for block in outs])
    t_out_all = jnp.concatenate([block[local_cols:] for block in outs])

    wide_qkv, wide_bias = padded_heads(w_qkv, qv_bias)
    qkv, context, x_in_all, ca_own, ca_near, ca_far = attend_forward(
        base, blocks, wide_qkv, wide_bias, seg_lanes, blocked, True
    )
    (t_context,) = attend_forward(
        base, blocks, *padded_heads(teacher_qkv, teacher_qv_bias), seg_lanes, blocked, False
    )
    ca_23 = swap(ca_far, 2)
    cas = [ca_own, swap(ca_near, 1), ca_23, swap(ca_23[1], 1)]
    vectors = [out_bias, norm1_gain, norm1_shift, down_bias, norm2_gain, norm2_shift, up_bias]
    vectors += [teacher_out_bias, teacher_norm1_gain, teacher_norm1_shift]
    vectors += [teacher_down_bias, teacher_norm2_gain, teacher_norm2_shift]
    vectors = jnp.pad(jnp.stack(vectors).astype(F32), ((0, 3), (0, 0)))
    out_own, grad_h, ffn_grads, out_grads, g0, g1, g2, g3, small = middle(
        tokens, cas, t_context, w_out_all, t_out_all, w_up, w_down, vectors, packs
    )
    ffn_grads, late, small, gx_own, gx_far = attend_backward(
        qkv, context, x_in_all, wide_qkv, [g0, g1, g2, g3], ffn_grads, out_grads, small
    )
    grad_x_in = gx_own + gx_far.astype(F32)
    input_grad = grad_h + grad_x_in * clip_slope(tokens.astype(F32))
    ffn_grads = ffn_grads.astype(F32)
    tree_loss = jnp.sum(small[LOSS_ROW])[None] / (all_rows * model_width)
    proj_bias_grad = small[8 : 8 + local_heads, : 3 * LANES].reshape(local_heads, 3, LANES)
    proj_bias_grad = proj_bias_grad[:, :, :HEAD_DIM].transpose(1, 0, 2).reshape(3, local_cols)
    proj_bias_grad = jnp.stack([proj_bias_grad[0] * 0.125, proj_bias_grad[2]])
    late = late.astype(F32)
    qkv_grad = jnp.concatenate([late[:local_cols], late[2 * local_cols :]])
    qkv_grad = qkv_grad.reshape(local_heads, 3, HEAD_DIM, model_width)
    qkv_grad = qkv_grad.transpose(3, 1, 0, 2).reshape(model_width, 3, local_cols)
    return (
        out_own,
        tree_loss,
        input_grad,
        qkv_grad,
        proj_bias_grad,
        late[local_cols : 2 * local_cols],
        small[0],
        small[1],
        small[2],
        ffn_grads[:model_width],
        small[7],
        ffn_grads[model_width:],
        small[3],
        small[4],
        small[5],
    )


def solution(mesh):
    rows, cols = ("dp", "tensor"), "tensor"
    vec = P()
    params = (
        P(None, None, cols),
        P(None, cols),
        P(cols, None),
        vec,
        vec,
        vec,
        P(None, cols),
        P(cols),
        P(cols, None),
        vec,
        vec,
        vec,
    )
    in_specs = (P(rows, None), P("dp", None), P("dp", None)) + params + params
    out_specs = (P(rows, None), P("dp"), P(rows, None)) + params
    return jax.shard_map(body, mesh=mesh, in_specs=in_specs, out_specs=out_specs, check_vma=False)
```

```python
import functools

import jax
import jax.numpy as jnp
from jax import lax
from jax.experimental import pallas as pl
from jax.experimental.pallas import tpu as pltpu
from jax.sharding import PartitionSpec as P

HEAD_DIM = 64
LANES = 128
CLIP_RANGE = 3.0
NORM_EPSILON = 1e-05
MASKED_SCORE = -1e30
SEG_LANE = HEAD_DIM
ROW_TERM = HEAD_DIM + 16
Q_BLOCK = 256
PACK_PAD = 32
CHUNKS = 2
BF16, F32 = jnp.bfloat16, jnp.float32
ROWS_ROWS = (((0,), (0,)), ((), ()))
COLS_COLS = (((1,), (1,)), ((), ()))


def clip_act(values):
    return CLIP_RANGE * jnp.tanh(values / CLIP_RANGE)


def clip_slope(values):
    level = jnp.tanh(values / CLIP_RANGE)
    return 1.0 - level * level


def normal_parts(values):
    bell = jnp.exp(-0.5 * values * values)
    step = 1.0 / (1.0 + 0.23164188843 * jnp.abs(values))
    series = 0.5307027145 * step - 0.7265760135
    series = series * step + 0.7107068705
    series = series * step - 0.142248368
    series = series * step + 0.127414796
    tail = series * step * bell
    return jnp.where(values >= 0.0, 1.0 - tail, tail), bell


def norm_forward(hidden, gain, shift):
    row_mean = jnp.mean(hidden, axis=-1, keepdims=True)
    centred = hidden - row_mean
    inv_std = lax.rsqrt(jnp.mean(centred * centred, axis=-1, keepdims=True) + NORM_EPSILON)
    normed = centred * inv_std
    return (normed * gain + shift, normed, inv_std)


def norm_backward(grad_out, normed, inv_std, gain):
    grad_normed = grad_out * gain
    centre = jnp.mean(grad_normed, axis=-1, keepdims=True)
    inner_sum = jnp.mean(grad_normed * normed, axis=-1, keepdims=True)
    return inv_std * (grad_normed - centre - normed * inner_sum)


def dot(left, right):
    return jnp.dot(left, right, preferred_element_type=F32)


def dot_rows(left, right):
    return lax.dot_general(left, right, ROWS_ROWS, preferred_element_type=F32)


def dot_cols(left, right):
    return lax.dot_general(left, right, COLS_COLS, preferred_element_type=F32)


def swap(array, bit):
    size = lax.axis_size("tensor")
    return lax.ppermute(array, "tensor", [(i, i ^ bit) for i in range(size)])


def lookup(indices, lookup_table):
    labels = jnp.arange(lookup_table.shape[0], dtype=jnp.int32)
    picked = jnp.where(indices[:, None] == labels[None, :], lookup_table[None, :], 0)
    return jnp.sum(picked, axis=1)


def segment_tables(lengths, parent):
    count = lengths.shape[0]
    labels = jnp.arange(count, dtype=jnp.int32)
    row, col = labels[:, None], labels[None, :]
    starts = jnp.sum(jnp.where(col < row, lengths[None, :], 0), axis=1)
    two = lookup(parent, parent)
    allowed = (col == row) | (col == parent[:, None]) | (col == two[:, None])
    allowed = allowed | (parent[None, :] == row) | (two[None, :] == row)
    after = LANES - SEG_LANE - count
    lanes = jnp.pad(jnp.stack([starts, starts + lengths]), ((0, 6), (SEG_LANE, after)))
    blocked = jnp.pad((~allowed).astype(BF16), ((SEG_LANE, after), (SEG_LANE, after)))
    return lanes, blocked


def split_three(values):
    first = values.astype(BF16).astype(F32)
    second = (values - first).astype(BF16).astype(F32)
    return first, second, values - first - second


def sign_of(values):
    return jnp.where(values > 0.0, 1.0, jnp.where(values < 0.0, -1.0, 0.0))


def prepare_kernel(
    out_ref, t_out_ref, up_ref, down_ref, t_up_ref, t_down_ref, t_bias_ref, *rest
):
    *vectors, outs_ref, w_up_ref, s_down_ref, pack_ref, sums_ref, vec_ref = rest
    vec_ref[...] = jnp.zeros_like(vec_ref)
    for index, vector in enumerate(vectors):
        vec_ref[index : index + 1, :] = vector[...].astype(F32).reshape(1, -1)
    hidden, width = down_ref.shape
    half = hidden // 2
    rows = out_ref.shape[0]
    total = lambda ref: jnp.sum(jnp.abs(ref[...]), axis=0, keepdims=True)
    sums_ref[...] = jnp.zeros_like(sums_ref)
    sums_ref[0:1, :] = total(out_ref)
    sums_ref[1:2, :] = total(down_ref)
    outs_ref[:rows, :] = sign_of(out_ref[...]).astype(BF16)
    outs_ref[rows:, :] = t_out_ref[...]
    w_up_ref[...] = (total(up_ref) * (1.0 / width) * sign_of(up_ref[...])).astype(BF16)
    s_down_ref[...] = sign_of(down_ref[...]).astype(BF16)
    up_t = t_up_ref[...].T
    pack_ref[:, hidden:, :] = jnp.zeros((2, PACK_PAD, width), BF16)
    for side in range(2):
        cols = slice(side * half, (side + 1) * half)
        pack_ref[side, :half, :] = up_t[cols]
        pack_ref[side, half:hidden, :] = t_down_ref[cols, :]
        bias = t_bias_ref[cols].astype(F32).reshape(1, -1)
        pack_ref[side, hidden : hidden + 1, :half] = bias.astype(BF16)


def prepare(latents, vectors):
    array = jax.ShapeDtypeStruct
    out_latent, _, up_latent, down_latent, *_ = latents
    hidden, width = down_latent.shape
    return pl.pallas_call(
        prepare_kernel,
        out_shape=[
            array((2 * out_latent.shape[0], width), BF16),
            array(up_latent.shape, BF16),
            array(down_latent.shape, BF16),
            array((2, hidden + PACK_PAD, width), BF16),
            array((8, width), F32),
            array((16, width), F32),
        ],
        compiler_params=pltpu.CompilerParams(vmem_limit_bytes=58 * 2**20),
        name="prepare",
    )(*latents, *vectors)


def in_lane(shape, axis, terms):
    lane = lax.broadcasted_iota(jnp.int32, shape, axis)
    spread = jnp.zeros(shape, F32)
    for offset, term in enumerate(terms):
        spread = jnp.where(lane == ROW_TERM + offset, term, spread)
    return spread


def make_copies(send_sem, recv_sem):
    count = [0]

    def copy_to(source, target, axis, device):
        index = count[0]
        count[0] += 1

        def make():
            return pltpu.make_async_remote_copy(
                src_ref=source,
                dst_ref=target,
                send_sem=send_sem.at[index],
                recv_sem=recv_sem.at[index],
                device_id={axis: device},
                device_id_type=pl.DeviceIdType.MESH,
            )

        return make

    return copy_to


def greet(others):
    barrier = pltpu.get_barrier_semaphore()
    for other in others:
        pl.semaphore_signal(barrier, inc=1, device_id=other, device_id_type=pl.DeviceIdType.MESH)
    pl.semaphore_wait(barrier, len(others))


def neighbours():
    me = lax.axis_index("tensor")
    return me + 1 - 2 * lax.rem(me, 2), lax.rem(me + 2, lax.axis_size("tensor"))


def forward_kernel(base_ref, x0, x1, x2, x3, w_ref, b_ref, seg_ref, blocked_ref, *rest, student):
    if student:
        pack_ref, outs, sums_ref, *rest = rest
        q_ref, k_ref, v_ref, ctx_ref, source, own, near, far, *rest = rest
        sums_out, pack_near, piece_a, outs1, outs2, sums, *rest = rest
    else:
        ca_near, ca_far, outs2, piece_a, *rest = rest
        sent, ca1, ca2, ca_pass, ca3, outs3, next_a, piece_b, piece_c, source, *rest = rest
    joined, queries, keys, vals_t, send_sem, recv_sem = rest
    blocks = (x0, x1, x2, x3)
    own_rows = x0.shape[0]
    rows = own_rows * len(blocks)
    heads = joined.shape[0]
    head = pl.program_id(0)
    near_id, far_id = neighbours()
    place = lax.axis_index("dp")
    copy_to = make_copies(send_sem, recv_sem)
    side_id, side = in_pair(place, 1)
    next_id, level = in_pair(place, 2)
    others = [{"tensor": near_id}, {"tensor": far_id}, {"dp": side_id}]
    if not student:
        others.append({"dp": next_id})
    if student:
        size = piece_a.shape[0]
        quarter = pack_ref.at[side, pl.ds(pl.multiple_of(level * size, 16), size)]
        half = outs.shape[0] // 2
        rows_of = pl.ds(pl.multiple_of(side * half, 16), half)
        outs_far = copy_to(outs.at[rows_of], outs2.at[rows_of], "tensor", far_id)
        pack_far = copy_to(quarter, piece_a, "tensor", far_id)
        sum_near = copy_to(sums.at[0], sums.at[1], "tensor", near_id)
        sum_far = copy_to(sums.at[2], sums.at[3], "tensor", far_id)
        stages = [
            (
                [],
                [
                    sum_near,
                    outs_far,
                    copy_to(outs, outs1, "tensor", near_id),
                    copy_to(pack_ref, pack_near, "tensor", near_id),
                ],
            ),
            ([outs_far], [pack_far, copy_to(outs2.at[rows_of], outs2.at[rows_of], "dp", side_id)]),
            ([], []),
        ]
    else:
        passing = copy_to(ca_far.at[1], ca_pass, "tensor", far_id)
        stages = [
            (
                [],
                [
                    passing,
                    copy_to(ca_far.at[0], ca2, "tensor", far_id),
                    copy_to(ca_near, ca1, "tensor", near_id),
                    copy_to(outs2, outs3, "tensor", near_id),
                    copy_to(piece_a, next_a, "dp", next_id),
                    copy_to(piece_a, piece_c, "tensor", near_id),
                    copy_to(piece_a, piece_b, "dp", side_id),
                ],
            ),
            ([], []),
            ([passing], [copy_to(ca_pass, ca3, "tensor", near_id)]),
        ]

    def run_stage(index):
        before, copies = stages[index]
        for copy in before:
            copy().wait_recv()
        for copy in copies:
            copy().start()

    @pl.when(head == 0)
    def _():
        if student:
            sums[0] = sums_ref[...]
        greet(others)
        run_stage(0)
        lane = lax.broadcasted_iota(jnp.int32, (own_rows, LANES), 1)
        ones = (lane >= ROW_TERM) & (lane < ROW_TERM + 3)
        for j, block in enumerate(blocks):
            part = slice(j * own_rows, (j + 1) * own_rows)
            if student:
                source[part, :] = clip_act(block[...].astype(F32)).astype(BF16)
            else:
                source[part, :] = block[...]
            spot = lax.broadcasted_iota(jnp.int32, (own_rows, LANES), 0) + base_ref[j]
            inside = (spot >= seg_ref[0:1, :]) & (spot < seg_ref[1:2, :])
            links = dot(jnp.where(inside, 1.0, 0.0).astype(BF16), blocked_ref[...])
            extras = (
                jnp.where(inside, MASKED_SCORE, 0.0).astype(BF16),
                jnp.where(ones, 1.0, links).astype(BF16),
                jnp.where(ones, 1.0, 0.0).astype(BF16),
            )
            for c, (scale, extra) in enumerate(zip((0.125, 1.0, 1.0), extras)):
                proj = dot(source[part, :], w_ref[c]) + b_ref[c : c + 1, :]
                proj = proj.astype(BF16)
                for h in range(heads):
                    one = proj[:, h * HEAD_DIM : (h + 1) * HEAD_DIM] * scale
                    wide = jnp.concatenate([one, jnp.zeros_like(one)], axis=1) + extra
                    if c == 0:
                        queries[h, part, :] = wide
                    elif c == 1:
                        keys[h, part, :] = wide
                    else:
                        vals_t[h, :, part] = wide.T
                        if student:
                            v_ref[h, part, :] = wide

    if student:
        k_ref[0] = keys[head]

    scores = {}
    for index in range(rows // Q_BLOCK):
        if index % (rows // Q_BLOCK // 2) == 0:
            if index:

                @pl.when(head == 0)
                def _():
                    run_stage(1)

                @pl.when(head == 1)
                def _():
                    run_stage(2)
                    if student:
                        sum_near().wait_recv()
                        sums[2] = sums[0] + sums[1]
                        sum_far().start()

            for later in range(index, index + rows // Q_BLOCK // 2):
                start = later * Q_BLOCK
                scores[later] = dot_cols(keys[head], queries[head, start : start + Q_BLOCK, :])
        block = scores[index]
        part = slice(index * Q_BLOCK, (index + 1) * Q_BLOCK)
        peak = jnp.max(block, axis=0, keepdims=True)
        raised = jnp.exp(block - peak)
        total = jnp.sum(raised, axis=0, keepdims=True)
        weights = (raised * (1.0 / total)).astype(BF16)
        context = dot(vals_t[head], weights)[:HEAD_DIM].T
        joined[head, part, :] = context
        if student:
            ctx_ref[0, part, :] = context
            terms = split_three(-(peak + jnp.log(total)))
            spread = in_lane((LANES, Q_BLOCK), 0, terms)
            q_ref[0, part, :] = queries[head, part, :] + spread.T.astype(BF16)

    @pl.when(head == heads - 1)
    def _():
        for j in range(len(blocks)):
            part = slice(j * own_rows, (j + 1) * own_rows)
            block = jnp.concatenate([joined[h, part, :] for h in range(heads)], axis=1)
            if not student:
                sent[j] = block.astype(BF16)
            elif j < 2:
                (own, near)[j][...] = clip_act(block).astype(BF16)
            else:
                far[j - 2] = clip_act(block).astype(BF16)
        waited = [copy for before, _ in stages for copy in before]
        if student:
            sum_far().wait_recv()
            sums_out[...] = sums[2] + sums[3]
            sum_far().wait_send()
            waited.append(sum_near)
        for _, copies in stages:
            for copy in copies:
                copy().wait_send()
                if copy not in waited:
                    copy().wait_recv()


def attend_forward(base, blocks, weight, bias, seg_lanes, blocked, moved, student):
    own_rows, width = blocks[0].shape
    rows = own_rows * len(blocks)
    head_cols = weight.shape[2]
    heads = head_cols // HEAD_DIM
    whole = lambda *shape: pl.BlockSpec(shape, lambda h: (0,) * len(shape))
    anywhere = pl.BlockSpec(memory_space=pl.ANY)
    array = jax.ShapeDtypeStruct
    per_head = lambda cols: pl.BlockSpec((1, rows, cols), lambda h: (h, 0, 0))
    if student:
        pack, out_weights, sums = moved
        piece = (pack.shape[1] // 2, width)
        outs = [
            (per_head(LANES), array((heads, rows, LANES), BF16)),
            (per_head(LANES), array((heads, rows, LANES), BF16)),
            (whole(heads, rows, LANES), array((heads, rows, LANES), BF16)),
            (per_head(HEAD_DIM), array((heads, rows, HEAD_DIM), F32)),
            (whole(rows, width), array((rows, width), BF16)),
            (whole(own_rows, head_cols), array((own_rows, head_cols), BF16)),
            (whole(own_rows, head_cols), array((own_rows, head_cols), BF16)),
            (whole(2, own_rows, head_cols), array((2, own_rows, head_cols), BF16)),
            (whole(*sums.shape), array(sums.shape, F32)),
            (anywhere, array(pack.shape, BF16)),
        ]
        outs += [(anywhere, array(piece, BF16))]
        outs += [(anywhere, array(out_weights.shape, BF16))] * 2
        scratch, transfers = [pltpu.VMEM((4,) + sums.shape, F32)], 7
    else:
        ca_near, ca_far, out_weights, piece = moved
        outs = [(whole(len(blocks), own_rows, head_cols), array((len(blocks), own_rows, head_cols), BF16))]
        outs += [(anywhere, array(ca_near.shape, BF16))] * 4
        outs += [(anywhere, array(out_weights.shape, BF16))]
        outs += [(anywhere, array(piece.shape, BF16))] * 3
        scratch, transfers = [pltpu.VMEM((rows, width), BF16)], 8
    scratch += [
        pltpu.VMEM((heads, rows, HEAD_DIM), F32),
        pltpu.VMEM((heads, rows, LANES), BF16),
        pltpu.VMEM((heads, rows, LANES), BF16),
        pltpu.VMEM((heads, LANES, rows), BF16),
        pltpu.SemaphoreType.DMA((transfers,)),
        pltpu.SemaphoreType.DMA((transfers,)),
    ]
    return pl.pallas_call(
        functools.partial(forward_kernel, student=student),
        grid=(heads,),
        in_specs=[pl.BlockSpec(memory_space=pltpu.SMEM)]
        + [whole(own_rows, width)] * 4
        + [whole(*a.shape) for a in (weight, bias, seg_lanes, blocked)]
        + [whole(*a.shape) if a.dtype == F32 else anywhere for a in moved],
        out_specs=[spec for spec, _ in outs],
        out_shape=[shape for _, shape in outs],
        scratch_shapes=scratch,
        compiler_params=pltpu.CompilerParams(
            collective_id=1 if student else 2, has_side_effects=True, vmem_limit_bytes=58 * 2**20
        ),
        cost_estimate=pl.CostEstimate(
            flops=16 * heads * rows * rows * HEAD_DIM,
            bytes_accessed=2 * rows * (width + 6 * heads * LANES),
            transcendentals=heads * rows * rows,
        ),
        name="student_attention" if student else "teacher_attention",
    )(base, *blocks, weight, bias, seg_lanes, blocked, *moved)


def in_pair(place, bit):
    digit = lax.rem(lax.div(place, bit), 2)
    return place + bit - 2 * bit * digit, digit


def halving_steps(partial, total, landing, rows, landing_row, order, place, copy_of, done=0, base=None):
    low, size = rows
    here = low if base is None else base
    steps, levels, used = [], [], landing_row
    for level, bit in enumerate(order):
        partner, digit = in_pair(place, bit)
        halved = size % 32 == 0
        count = size // 2 if halved else size
        low = pl.multiple_of(low + digit * count, 16) if halved else low
        if level >= done:
            give = pl.multiple_of(here + (1 - digit) * count, 16) if halved else here
            here = pl.multiple_of(here + digit * count, 16) if halved else here
            copy = copy_of(partial.at[pl.ds(give, count)], landing.at[pl.ds(used, count)], partner)
            last = level == len(order) - 1

            def add(used=used, here=here, count=count, out=total if last else partial, at=low if last else here):
                arrived = landing[used : used + count, :].astype(F32)
                mine = partial[pl.ds(here, count), :].astype(F32)
                out[pl.ds(at, count), :] = (mine + arrived).astype(out.dtype)

            steps.append((copy, add))
            used += count
        if halved:
            levels.append((count, low, partner))
        size = count
    for count, keep, partner in reversed(levels):
        where = total.at[pl.ds(keep, count)]
        steps.append((copy_of(where, where, partner), lambda: None))
    return steps, used


def run_step(plans, index):
    for steps in plans:
        if 0 < index <= len(steps):
            copy, after = steps[index - 1]
            copy().wait()
            after()
        if index < len(steps):
            steps[index][0]().start()


def split_rows(first, count):
    small = count // 2 if count % 512 == 0 else -(-count // 3 // 64) * 64
    return ((first, count - small), (first + count - small, small))


def dp_bits():
    bits = [1 << i for i in range((lax.axis_size("dp") - 1).bit_length())]
    return bits, (bits[1:2] + bits[:1] + bits[2:])


def backward_kernel(
    q_ref, k_ref, v_ref, ctx_ref, x_ref, w_ref, g0, g1, g2, g3, ffn_ref, outg_ref, small_ref,
    ffn_out, late_out, small_out, gx_out, gxfar_out,
    grads, wide, packed, keys_t, total, ffn_part, ffn, late_in, late, small, small_in, landing, small_land,
    out_near, out_near_land, out_far, out_far_land, gx_near, gx_near_land, gx_far, gx_far_land,
    send_sem, recv_sem, *, key_block,
):
    blocks = (g0, g1, g2, g3)
    own_rows = g0.shape[0]
    rows = own_rows * len(blocks)
    heads = grads.shape[0]
    head_cols = heads * HEAD_DIM
    head = pl.program_id(0)
    place = lax.axis_index("dp")
    near_id, far_id = neighbours()
    part = lambda j: slice(j * own_rows, (j + 1) * own_rows)
    bits, turned = dp_bits()

    copy_to = make_copies(send_sem, recv_sem)
    over_dp = lambda source, target, other: copy_to(source, target, "dp", other)
    over_tensor = lambda source, target, other: copy_to(source, target, "tensor", other)

    used = [0]

    def reduced(partial, target, first, size, done=0):
        plans, taken = [], 0
        for rows_of, order in zip(split_rows(first, size), (bits, turned)):
            steps, used[0] = halving_steps(
                partial, target, landing, rows_of, used[0], order, place, over_dp, done,
                taken if done else None,
            )
            plans.append(steps)
            taken += rows_of[1] // 2
        return plans

    width = x_ref.shape[1]
    ffn_plans = reduced(ffn_part, ffn, 0, ffn.shape[0], 1)
    early_plans = reduced(late_in, late, 0, 2 * head_cols)
    middle_plans = reduced(late_in, late, 2 * head_cols, head_cols)
    last_plans = reduced(late_in, late, 3 * head_cols, head_cols)
    small_steps = []
    for level, bit in enumerate(bits):
        partner, _ = in_pair(place, bit)
        small_steps.append(over_dp(small_in.at[level], small_land.at[level], partner))
    tensor_small = [
        over_tensor(small.at[0], small.at[1], near_id),
        over_tensor(small.at[2], small.at[3], far_id),
    ]
    out_steps = [
        over_tensor(out_near, out_near_land, near_id),
        over_tensor(out_far, out_far_land, far_id),
    ]
    gx_steps = [
        over_tensor(gx_near, gx_near_land, near_id),
        over_tensor(gx_far, gx_far_land, far_id),
    ]

    @pl.when(head == 0)
    def _():
        others = [{"tensor": near_id}, {"tensor": far_id}]
        greet(others + [{"dp": in_pair(place, bit)[0]} for bit in bits])
        ffn_part[...] = ffn_ref[...]
        run_step(ffn_plans, 0)
        out_near[0] = outg_ref[1]
        out_near[1] = outg_ref[3]
        out_steps[0]().start()
        small[0] = small_ref[...]
        tensor_small[0]().start()
        for h in range(heads):
            for j, block in enumerate(blocks):
                one = block[:, h * HEAD_DIM : (h + 1) * HEAD_DIM].astype(F32)
                grads[h, part(j), :] = jnp.concatenate(
                    [one, jnp.zeros_like(one)], axis=1
                ).astype(BF16)
        packed[...] = jnp.zeros_like(packed)
        wide[...] = jnp.zeros_like(wide)
        for h in range(heads):
            for c, scale in enumerate((0.125, 1.0, 1.0)):
                one = w_ref[c, :, h * HEAD_DIM : (h + 1) * HEAD_DIM] * scale
                wide[h, :, c * LANES : c * LANES + HEAD_DIM] = one

    queries = q_ref[0]
    slopes = grads[head]
    inner = -jnp.sum(slopes[:, :HEAD_DIM].astype(F32) * ctx_ref[0], axis=1, keepdims=True)
    slopes = slopes + in_lane((rows, LANES), 1, split_three(inner)).astype(BF16)
    keys_t[...] = k_ref[0].T

    def over_keys(first, last, query_grad):
        for start in range(first, last, key_block):
            span = slice(start, start + key_block)
            weights = jnp.exp(dot_cols(k_ref[0, span, :], queries))
            grad_weights = dot_cols(v_ref[0, span, :], slopes)
            grad_scores = (weights * grad_weights).astype(BF16)
            step = dot(keys_t[:, span], grad_scores)
            query_grad = step if query_grad is None else query_grad + step
            key_grad = dot(grad_scores, queries)[:, :HEAD_DIM]
            packed[span, LANES : LANES + HEAD_DIM] = key_grad.astype(BF16)
            value_grad = dot(weights.astype(BF16), slopes)[:, :HEAD_DIM]
            packed[span, 2 * LANES : 2 * LANES + HEAD_DIM] = value_grad.astype(BF16)
        return query_grad

    def at(which):
        return pl.when(head == which)

    quarter = rows // 4
    query_grad = over_keys(0, quarter, None)

    @at(1)
    def _():
        run_step(ffn_plans, 2)

    query_grad = over_keys(quarter, 2 * quarter, query_grad)

    @at(0)
    def _():
        run_step(ffn_plans, 1)
        out_steps[0]().wait_recv()
        out_far[...] = (outg_ref[2].astype(F32) + out_near_land[1].astype(F32)).astype(BF16)
        out_steps[1]().start()
        tensor_small[0]().wait_recv()
        small[2] = small[0] + small[1]
        tensor_small[1]().start()

    @at(1)
    def _():
        run_step(early_plans, 1)

    @at(2)
    def _():
        run_step(ffn_plans, 4)
        run_step(early_plans, 3)
        run_step(middle_plans, 1)

    query_grad = over_keys(2 * quarter, rows, query_grad)
    packed[:, :HEAD_DIM] = query_grad[:HEAD_DIM].T.astype(BF16)
    sums = jnp.sum(packed[...].astype(F32), axis=0, keepdims=True)
    small[4 + head, 0:1, : 3 * LANES] = sums
    weight_grad = dot_rows(packed[...], x_ref[...])
    slot = jnp.where(head == 0, 0, head_cols + head * head_cols)
    for c, factor in enumerate((0.125, 1.0, 1.0)):
        target = pl.multiple_of(slot + c * HEAD_DIM, HEAD_DIM)
        late_in[pl.ds(target, HEAD_DIM), :] = (
            weight_grad[c * LANES : c * LANES + HEAD_DIM] * factor
        ).astype(BF16)

    @pl.when(head == 0)
    def _():
        out_steps[1]().wait_recv()
        late_in[head_cols : 2 * head_cols, :] = (
            outg_ref[0].astype(F32)
            + out_near_land[0].astype(F32)
            + out_far_land[...].astype(F32)
        ).astype(BF16)
        tensor_small[1]().wait_recv()
        run_step(early_plans, 0)

    @pl.when(head == 1)
    def _():
        run_step(middle_plans, 0)
        run_step(ffn_plans, 3)
        run_step(early_plans, 2)

    @pl.when(head == 2)
    def _():
        run_step(last_plans, 0)
        small_in[0, :8, :] = small[2] + small[3]
        small_in[0, UP_ROW : UP_ROW + 1, :] = small_ref[UP_ROW : UP_ROW + 1, :]
        small_in[0, 8:, :] = jnp.zeros((8, width), F32)
        for h in range(heads):
            small_in[0, 8 + h : 9 + h, : 3 * LANES] = small[4 + h, 0:1, : 3 * LANES]
        small_steps[0]().start()

    for j in (1, 3, 2, 0):
        step = dot_cols(packed[part(j), :], wide[head])
        total[part(j), :] = jnp.where(head == 0, step, total[part(j), :] + step)

    @pl.when(head == heads - 1)
    def _():
        gx_near[0] = total[part(1), :].astype(BF16)
        gx_near[1] = total[part(3), :].astype(BF16)
        gx_steps[0]().start()
        run_step(last_plans, 1)
        gx_steps[0]().wait_recv()
        gx_far[...] = (total[part(2), :] + gx_near_land[1].astype(F32)).astype(BF16)
        gx_steps[1]().start()
        gx_out[...] = total[part(0), :] + gx_near_land[0].astype(F32)
        run_step(early_plans, 4)
        run_step(middle_plans, 2)
        for index in range(1, 2 * len(bits) + 1):
            if index > 1:
                run_step(last_plans, index)
            if index <= len(bits):
                small_steps[index - 1]().wait_recv()
                arrived = small_in[index - 1] + small_land[index - 1]
                if index < len(bits):
                    small_in[index] = arrived
                    small_steps[index]().start()
                else:
                    small_out[...] = arrived
            run_step(middle_plans, 2 + index)
            run_step(early_plans, 4 + index)
        for index in range(5, 2 * len(bits) + 1):
            run_step(ffn_plans, index)
        ffn_out[...] = ffn[...]
        late_out[...] = late[...]
        gx_steps[1]().wait_recv()
        gxfar_out[...] = gx_far_land[...]
        shared = small[2, LOSS_ROW : LOSS_ROW + 1, :] + small[3, LOSS_ROW : LOSS_ROW + 1, :]
        small_out[LOSS_ROW : LOSS_ROW + 1, :] = shared
        for copy in small_steps + tensor_small + out_steps + gx_steps:
            copy().wait_send()


def attend_backward(qkv, context, source, weight, blocks, ffn_grads, out_grads, small):
    rows, width = source.shape
    own_rows, head_cols = blocks[0].shape
    cols = 3 * LANES
    heads = head_cols // HEAD_DIM
    levels = (lax.axis_size("dp") - 1).bit_length()
    ffn_rows, late_rows = 2 * ffn_grads.shape[0], (heads + 1) * head_cols
    landing = ffn_rows + late_rows + 8 * 48 * levels
    transfers = 2 * 4 * 2 * levels + levels + 6
    array = jax.ShapeDtypeStruct
    whole = lambda *shape: pl.BlockSpec(shape, lambda h: (0,) * len(shape))
    head_block = lambda *shape: pl.BlockSpec((1,) + shape, lambda h: (h, 0, 0))
    return pl.pallas_call(
        functools.partial(backward_kernel, key_block=256),
        grid=(heads,),
        in_specs=[
            head_block(rows, LANES),
            head_block(rows, LANES),
            head_block(rows, LANES),
            head_block(rows, HEAD_DIM),
            whole(rows, width),
            whole(*weight.shape),
        ]
        + [whole(own_rows, head_cols)] * 4
        + [whole(*ffn_grads.shape), whole(*out_grads.shape), whole(*small.shape)],
        out_specs=[
            whole(ffn_rows, width),
            whole(late_rows, width),
            whole(16, width),
            whole(own_rows, width),
            whole(own_rows, width),
        ],
        out_shape=[
            array((ffn_rows, width), BF16),
            array((late_rows, width), BF16),
            array((16, width), F32),
            array((own_rows, width), F32),
            array((own_rows, width), BF16),
        ],
        scratch_shapes=[
            pltpu.VMEM((heads, rows, LANES), BF16),
            pltpu.VMEM((heads, width, cols), BF16),
            pltpu.VMEM((rows, cols), BF16),
            pltpu.VMEM((LANES, rows), BF16),
            pltpu.VMEM((rows, width), F32),
            pltpu.VMEM((ffn_rows // 2, width), BF16),
            pltpu.VMEM((ffn_rows, width), BF16),
            pltpu.VMEM((late_rows, width), BF16),
            pltpu.VMEM((late_rows, width), BF16),
            pltpu.VMEM((4 + heads, 8, width), F32),
            pltpu.VMEM((levels, 16, width), F32),
            pltpu.VMEM((landing, width), BF16),
            pltpu.VMEM((levels, 16, width), F32),
            pltpu.VMEM((2, head_cols, width), BF16),
            pltpu.VMEM((2, head_cols, width), BF16),
            pltpu.VMEM((head_cols, width), BF16),
            pltpu.VMEM((head_cols, width), BF16),
            pltpu.VMEM((2, own_rows, width), BF16),
            pltpu.VMEM((2, own_rows, width), BF16),
            pltpu.VMEM((own_rows, width), BF16),
            pltpu.VMEM((own_rows, width), BF16),
            pltpu.SemaphoreType.DMA((transfers,)),
            pltpu.SemaphoreType.DMA((transfers,)),
        ],
        compiler_params=pltpu.CompilerParams(
            collective_id=4, has_side_effects=True, vmem_limit_bytes=62 * 2**20
        ),
        cost_estimate=pl.CostEstimate(
            flops=60 * heads * rows * rows * HEAD_DIM,
            bytes_accessed=2 * rows * heads * (cols + 7 * LANES),
            transcendentals=heads * rows * rows,
        ),
        name="attention_backward",
    )(*qkv, context, source, weight, *blocks, ffn_grads, out_grads, small)


(OUT_BIAS, GAIN_1, SHIFT_1, DOWN_BIAS, GAIN_2, SHIFT_2, UP_BIAS) = range(7)
T_VECTORS = 7
LOSS_ROW, UP_ROW = 6, 7


def middle_kernel(
    x_ref, ca0, ca1, ca2, ca3, tc_ref, outs0, outs1, outs2, outs3, w_up, s_down, vec,
    pack_own, pack_near, piece_a, piece_b, piece_c, next_a, sums_ref,
    out_ref, gh_ref, kept_ref, outg_ref, g0_ref, g1_ref, g2_ref, g3_ref, small_ref, piece_d, next_b, next_c, next_d,
    tc1, tc2, tcf, tc3, y_all, g_all, slope, hid, gu_all, t_out, first, normed, two, inv,
    part0, part2, send1, send2, send3, near0, near2, far0, gs, gr, packs, ffn_ref, ffn_land, w_outs, w_down,
    send_sem, recv_sem, pack_sem,
):
    near_id, far_id = neighbours()
    own_rows, width = x_ref.shape
    hidden = s_down.shape[0]
    head_cols = ca0.shape[1]
    size = own_rows // CHUNKS
    chunks = [slice(c * size, (c + 1) * size) for c in range(CHUNKS)]
    tiles = [slice(n, n + 256) for n in range(0, hidden, 256)]
    group = lambda j: slice(j * head_cols, (j + 1) * head_cols)
    outs = (outs0, outs1, outs2, outs3)
    w_out = lambda j: w_outs[j]
    tw_out = lambda j: outs[j][head_cols:, :]
    row = lambda index: vec[index : index + 1, :]

    place = lax.axis_index("dp")
    first_bits = [order[0] for order in dp_bits()]
    others = [{"tensor": near_id}, {"tensor": far_id}]
    others += [{"dp": in_pair(place, bit)[0]} for bit in first_bits]
    greet(others)

    count = [0]
    started = []

    def put(source, target, device, axis="tensor"):
        index = count[0]
        count[0] += 1
        copy = pltpu.make_async_remote_copy(
            src_ref=source,
            dst_ref=target,
            send_sem=send_sem.at[index],
            recv_sem=recv_sem.at[index],
            device_id={axis: device},
            device_id_type=pl.DeviceIdType.MESH,
        )
        copy.start()
        started.append(copy)
        return copy

    t_far = put(tc_ref.at[2], tc2, far_id)
    t_pass = put(tc_ref.at[3], tcf, far_id)
    t_near = put(tc_ref.at[1], tc1, near_id)
    next_id, level = in_pair(place, 2)
    cut = piece_a.shape[0]
    here = pl.ds(pl.multiple_of(level * cut, 16), cut)
    there = pl.ds(pl.multiple_of((1 - level) * cut, 16), cut)
    next_copies = [
        put(next_a, next_c, near_id),
        put(piece_b, next_b, next_id, "dp"),
        put(piece_b, piece_d, near_id),
    ]

    pack_refs = [pack_own.at[0], pack_own.at[1], pack_near.at[0], pack_near.at[1]]
    pack_refs += [(piece_a, next_a), (piece_c, next_c), (piece_b, next_b), (piece_d, next_d)]

    def load_pack(index):
        slot = index % 2
        source, target = pack_refs[index], packs.at[slot]
        if not isinstance(source, tuple):
            return [pltpu.make_async_copy(source, target, pack_sem.at[slot])]
        return [
            pltpu.make_async_copy(source[0], target.at[here], pack_sem.at[slot]),
            pltpu.make_async_copy(source[1], target.at[there], pack_sem.at[2 + slot]),
        ]

    def start_pack(index):
        for copy in load_pack(index):
            copy.start()

    start_pack(0)
    a_out = (sums_ref[0:1, :] * (1.0 / width)).astype(BF16)
    a_down = (sums_ref[1:2, :] * (1.0 / (lax.axis_size("tensor") * hidden))).astype(BF16)
    for j in range(4):
        w_outs[j] = outs[j][:head_cols, :] * a_out
    w_down[...] = s_down[...] * a_down
    small_ref[...] = jnp.zeros_like(small_ref)

    def add_small(index, values):
        small_ref[index : index + 1, :] += jnp.sum(values, axis=0, keepdims=True)

    def share(own_block, where):
        return (
            put(own_block.at[0, where], own_block.at[1, where], near_id),
            put(own_block.at[0, where], own_block.at[2, where], far_id),
        )

    y_sent = []
    for rows in chunks:
        attn = dot(ca0[rows, :], w_out(0)) + dot(ca1[rows, :], w_out(1))
        attn += dot(ca2[rows, :], w_out(2)) + dot(ca3[rows, :], w_out(3))
        y_one, y_normed, y_inv = norm_forward(
            x_ref[rows, :].astype(F32) + attn + row(OUT_BIAS), row(GAIN_1), row(SHIFT_1)
        )
        first[rows, :] = y_one
        normed[rows, :] = y_normed
        inv[rows, :] = jnp.broadcast_to(y_inv, (size, LANES))
        y_all[0, rows, :] = clip_act(y_one).astype(BF16)
        y_sent.append(share(y_all, rows))

    def forward_block(j, rows):
        total = None
        for cols in tiles:
            upward = dot(y_all[j, rows, :], w_up[:, cols]) + row(UP_BIAS)[:, cols]
            cdf, bell = normal_parts(upward)
            level = jnp.tanh(upward * cdf * (1.0 / CLIP_RANGE))
            act = (CLIP_RANGE * level).astype(BF16)
            hid[j, rows, cols] = act
            slope[j, rows, cols] = (1.0 - level * level) * (
                cdf + upward * bell * 0.3989422804014327
            )
            step = dot(act, w_down[cols, :])
            total = step if total is None else total + step
        return total

    def backward_block(j, rows):
        total = None
        for cols in tiles:
            grad = dot_cols(g_all[j, rows, :], w_down[cols, :])
            grad = (grad * slope[j, rows, cols]).astype(BF16)
            gu_all[j, rows, cols] = grad
            small_ref[UP_ROW : UP_ROW + 1, cols] += jnp.sum(
                grad.astype(F32), axis=0, keepdims=True
            )
            step = dot_cols(grad, w_up[:, cols])
            total = step if total is None else total + step
        return total

    def near_blocks(work, sent):
        copies = []
        for rows in chunks:
            part0[rows, :] = work(0, rows)
        for rows, (near, _) in zip(chunks, sent):
            near.wait_recv()
            send1[rows, :] = work(1, rows).astype(BF16)
            copies.append(put(send1.at[rows], near0.at[rows], near_id))
        return copies

    def far_blocks(block, work, sent):
        copies = []
        for rows, (_, far) in zip(chunks, sent):
            far.wait_recv()
            passed = put(block.at[2, rows], block.at[3, rows], near_id)
            part2[rows, :] = work(2, rows)
            passed.wait_recv()
            send3[rows, :] = work(3, rows).astype(BF16)
            met = put(send3.at[rows], near2.at[rows], near_id)
            met.wait_recv()
            send2[rows, :] = (part2[rows, :] + near2[rows, :].astype(F32)).astype(BF16)
            copies.append(put(send2.at[rows], far0.at[rows], far_id))
        return copies

    def summed(rows, near, far):
        near.wait_recv()
        far.wait_recv()
        return part0[rows, :] + near0[rows, :].astype(F32) + far0[rows, :].astype(F32)

    y_near = near_blocks(forward_block, y_sent)

    t_pass.wait_recv()
    t_last = put(tcf, tc3, near_id)
    t_near.wait_recv()
    t_far.wait_recv()
    t_row = lambda index: row(T_VECTORS + index)
    t_attn = dot(tc_ref[0], tw_out(0)) + dot(tc1[...], tw_out(1)) + dot(tc2[...], tw_out(2))
    t_last.wait_recv()
    t_attn += dot(tc3[...], tw_out(3))
    t_one, _, _ = norm_forward(x_ref[...].astype(F32) + t_attn + t_row(0), t_row(1), t_row(2))
    two[...] = t_one
    t_out[...] = t_one + t_row(3)
    half = hidden // 2
    t_in = t_one.astype(BF16)
    for index in range(len(pack_refs)):
        slot = index % 2
        if index == 4:
            next_copies[0].wait_recv()
            next_copies[1].wait_recv()
            next_copies.append(put(next_b, next_d, near_id))
        if index == 6:
            next_copies[2].wait_recv()
            next_copies[3].wait_recv()
        if index + 1 < len(pack_refs):
            start_pack(index + 1)
        for copy in load_pack(index):
            copy.wait()
        upward = dot_cols(t_in, packs[slot, :half, :])
        upward = upward + packs[slot, hidden : hidden + 1, :half].astype(F32)
        act = (upward * normal_parts(upward)[0]).astype(BF16)
        t_out[...] += dot(act, packs[slot, half:hidden, :])
    t_out[...] = norm_forward(t_out[...], t_row(4), t_row(5))[0]

    y_far = far_blocks(y_all, forward_block, y_sent)

    g_sent = []
    for copy in started:
        copy.wait_send()
    started.clear()
    for rows, near, far in zip(chunks, y_near, y_far):
        ffn = summed(rows, near, far)
        out, n_two, inv_two = norm_forward(
            first[rows, :] + ffn + row(DOWN_BIAS), row(GAIN_2), row(SHIFT_2)
        )
        out_ref[rows, :] = out.astype(BF16)
        gap = out - t_out[rows, :]
        add_small(LOSS_ROW, gap * gap)
        add_small(GAIN_2, gap * n_two)
        add_small(SHIFT_2, gap)
        grad_two = norm_backward(gap, n_two, inv_two, row(GAIN_2))
        two[rows, :] = grad_two
        grad_ffn = grad_two.astype(BF16)
        add_small(DOWN_BIAS, grad_ffn.astype(F32))
        g_all[0, rows, :] = grad_ffn
        g_sent.append(share(g_all, rows))

    g_near = near_blocks(backward_block, g_sent)
    g_far = far_blocks(g_all, backward_block, g_sent)
    flat = lambda block: block[...].reshape(4 * own_rows, block.shape[2])
    ffn_ref[:width, :] = dot_rows(flat(y_all), flat(gu_all)).astype(BF16)
    ffn_ref[width:, :] = dot_rows(flat(hid), flat(g_all)).astype(BF16)
    halves, taken = [], 0
    for (low, size), bit in zip(split_rows(0, width + hidden), first_bits):
        partner, digit = in_pair(place, bit)
        size = size // 2
        give = ffn_ref.at[pl.ds(pl.multiple_of(low + (1 - digit) * size, 16), size)]
        keep = pl.multiple_of(low + digit * size, 16)
        land = slice(taken, taken + size)
        halves.append((put(give, ffn_land.at[land], partner, "dp"), keep, land))
        taken += size

    passes = []
    for c, (rows, near, far) in enumerate(zip(chunks, g_near, g_far)):
        y_one = first[rows, :]
        grad_one = two[rows, :] + summed(rows, near, far) * clip_slope(y_one)
        n_one = normed[rows, :]
        add_small(GAIN_1, grad_one * n_one)
        add_small(SHIFT_1, grad_one)
        grad_h = norm_backward(grad_one, n_one, inv[rows, :1], row(GAIN_1))
        gh_ref[rows, :] = grad_h
        grad_attn = grad_h.astype(BF16)
        add_small(OUT_BIAS, grad_attn.astype(F32))
        for j, ca in enumerate((ca0.at[rows], ca1.at[rows], ca2.at[rows], ca3.at[rows])):
            act = ca[...]
            level = act.astype(F32) * (1.0 / CLIP_RANGE)
            grad = dot_cols(grad_attn, w_out(j)) * (1.0 - level * level)
            gs[j, rows, :] = grad.astype(BF16)
            step = dot_rows(act, grad_attn)
            if c:
                step = step + part2[group(j), :]
            part2[group(j), :] = step
        passes.append(
            (
                put(gs.at[3, rows], gr.at[3, rows], far_id),
                put(gs.at[2, rows], gr.at[1, rows], far_id),
                put(gs.at[1, rows], gr.at[0, rows], near_id),
            )
        )
    g0_ref[...] = gs[0]
    for j in range(4):
        outg_ref[j] = part2[group(j), :].astype(BF16)
    lasts = []
    for rows, (passing, _, _) in zip(chunks, passes):
        passing.wait_recv()
        lasts.append(put(gr.at[3, rows], gr.at[2, rows], near_id))
    for rows, (_, far, near), last in zip(chunks, passes, lasts):
        near.wait_recv()
        g1_ref[rows, :] = gr[0, rows, :]
        far.wait_recv()
        g2_ref[rows, :] = gr[1, rows, :]
        last.wait_recv()
        g3_ref[rows, :] = gr[2, rows, :]
    for copy, keep, land in halves:
        copy.wait_recv()
        mine = ffn_ref[pl.ds(keep, land.stop - land.start), :].astype(F32)
        kept_ref[land, :] = (mine + ffn_land[land, :].astype(F32)).astype(BF16)
    for copy in started:
        copy.wait_send()


def middle(x_own, cas, tc, outs, w_up, s_down, vectors, packs, sums):
    own_rows, width = x_own.shape
    hidden = s_down.shape[0]
    head_cols = cas[0].shape[1]
    array = jax.ShapeDtypeStruct
    vmem = pl.BlockSpec(memory_space=pltpu.VMEM)
    transfers = 8 + 4 * 3 * CHUNKS + 4 * CHUNKS + 2
    four_outs = pltpu.VMEM((4, head_cols, width), BF16)
    square = lambda kind: pltpu.VMEM((own_rows, width), kind)
    four = lambda cols, kind: pltpu.VMEM((4, own_rows, cols), kind)
    return pl.pallas_call(
        middle_kernel,
        in_specs=[vmem] * 13 + [pl.BlockSpec(memory_space=pl.ANY)] * 6 + [vmem],
        out_specs=[vmem] * 9 + [pl.BlockSpec(memory_space=pl.ANY)] * 4,
        out_shape=[
            array((own_rows, width), BF16),
            array((own_rows, width), F32),
            array(((width + hidden) // 2, width), BF16),
            array((4, head_cols, width), BF16),
        ]
        + [array((own_rows, head_cols), BF16)] * 4
        + [array((8, width), F32)]
        + [array(packs[2].shape, BF16)] * 4,
        scratch_shapes=[pltpu.VMEM((own_rows, head_cols), BF16)] * 4
        + [four(width, BF16), four(width, BF16), four(hidden, F32), four(hidden, BF16)]
        + [four(hidden, BF16)]
        + [square(F32)] * 4
        + [pltpu.VMEM((own_rows, LANES), F32)]
        + [square(F32), pltpu.VMEM((4 * max(own_rows // 4, head_cols), width), F32)]
        + [square(BF16)] * 6
        + [four(head_cols, BF16), four(head_cols, BF16)]
        + [
            pltpu.VMEM(packs[0].shape, BF16),
            pltpu.VMEM((width + hidden, width), BF16),
            pltpu.VMEM(((width + hidden) // 2, width), BF16),
            four_outs,
            pltpu.VMEM(s_down.shape, BF16),
            pltpu.SemaphoreType.DMA((transfers,)),
            pltpu.SemaphoreType.DMA((transfers,)),
            pltpu.SemaphoreType.DMA((4,)),
        ],
        compiler_params=pltpu.CompilerParams(
            collective_id=3, has_side_effects=True, vmem_limit_bytes=62 * 2**20
        ),
        cost_estimate=pl.CostEstimate(
            flops=120 * own_rows * width * hidden, bytes_accessed=2**25, transcendentals=2**22
        ),
        name="middle",
    )(x_own, *cas, tc, *outs, w_up, s_down, vectors, *packs, sums)


def projection(weight, bias):
    rows = jnp.stack([bias[0], jnp.zeros_like(bias[0]), bias[1]]).astype(F32)
    return weight.transpose(1, 0, 2), jnp.pad(rows, ((0, 5), (0, 0)))


def body(
    tokens,
    seg_lengths,
    parents,
    qkv_latent,
    qv_bias,
    out_latent,
    out_bias,
    norm1_gain,
    norm1_shift,
    up_latent,
    up_bias,
    down_latent,
    down_bias,
    norm2_gain,
    norm2_shift,
    teacher_qkv,
    teacher_qv_bias,
    teacher_out,
    teacher_out_bias,
    teacher_norm1_gain,
    teacher_norm1_shift,
    teacher_up,
    teacher_up_bias,
    teacher_down,
    teacher_down_bias,
    teacher_norm2_gain,
    teacher_norm2_shift,
):
    own_rows, model_width = tokens.shape
    group = lax.axis_size("tensor")
    me = lax.axis_index("tensor")
    all_rows = own_rows * group
    local_cols = qkv_latent.shape[2]
    local_heads = local_cols // HEAD_DIM
    near_x = swap(tokens, 1)
    far_x = swap(tokens, 2)
    blocks = [tokens, near_x, far_x, swap(far_x, 1)]
    latents = [out_latent, teacher_out, up_latent, down_latent]
    latents += [teacher_up, teacher_down, teacher_up_bias]
    vectors = [out_bias, norm1_gain, norm1_shift, down_bias, norm2_gain, norm2_shift, up_bias]
    vectors += [teacher_out_bias, teacher_norm1_gain, teacher_norm1_shift]
    vectors += [teacher_down_bias, teacher_norm2_gain, teacher_norm2_shift]
    outs, w_up, s_down, pack, sums, vectors = prepare(latents, vectors)
    w_qkv = (jnp.mean(jnp.abs(qkv_latent), axis=0) * jnp.sign(qkv_latent)).astype(BF16)
    seg_lanes, blocked = segment_tables(seg_lengths[0], parents[0])
    base = jnp.stack([(me ^ j) * own_rows for j in range(group)]).astype(jnp.int32)

    w_three, b_three = projection(w_qkv, qv_bias)
    tables = (seg_lanes, blocked)
    *qkv, context, x_in_all, ca_own, ca_near, ca_far, sums, pack_near, piece_a, outs1, outs2 = attend_forward(
        base, blocks, w_three, b_three, *tables, [pack, outs, sums], True
    )
    t_context, ca1, ca2, _, ca3, outs3, next_a, piece_b, piece_c = attend_forward(
        base, blocks, *projection(teacher_qkv, teacher_qv_bias), *tables,
        [ca_near, ca_far, outs2, piece_a], False,
    )
    cas, outs = [ca_own, ca1, ca2, ca3], [outs, outs1, outs2, outs3]
    packs = [pack, pack_near, piece_a, piece_b, piece_c, next_a]
    out_own, grad_h, ffn_grads, out_grads, g0, g1, g2, g3, small, *_ = middle(
        tokens, cas, t_context, outs, w_up, s_down, vectors, packs, sums
    )
    ffn_grads, late, small, gx_own, gx_far = attend_backward(
        qkv, context, x_in_all, w_three, [g0, g1, g2, g3], ffn_grads, out_grads, small
    )
    grad_x_in = gx_own + gx_far.astype(F32)
    input_grad = grad_h + grad_x_in * clip_slope(tokens.astype(F32))
    ffn_grads = ffn_grads.astype(F32)
    tree_loss = jnp.sum(small[LOSS_ROW])[None] / (all_rows * model_width)
    proj_bias_grad = small[8 : 8 + local_heads, : 3 * LANES].reshape(local_heads, 3, LANES)
    proj_bias_grad = proj_bias_grad[:, :, :HEAD_DIM].transpose(1, 0, 2).reshape(3, local_cols)
    proj_bias_grad = jnp.stack([proj_bias_grad[0] * 0.125, proj_bias_grad[2]])
    late = late.astype(F32)
    qkv_grad = jnp.concatenate([late[:local_cols], late[2 * local_cols :]])
    qkv_grad = qkv_grad.reshape(local_heads, 3, HEAD_DIM, model_width)
    qkv_grad = qkv_grad.transpose(3, 1, 0, 2).reshape(model_width, 3, local_cols)
    return (
        out_own,
        tree_loss,
        input_grad,
        qkv_grad,
        proj_bias_grad,
        late[local_cols : 2 * local_cols],
        small[0],
        small[1],
        small[2],
        ffn_grads[:model_width],
        small[7],
        ffn_grads[model_width:],
        small[3],
        small[4],
        small[5],
    )


def solution(mesh):
    rows, cols = ("dp", "tensor"), "tensor"
    vec = P()
    params = (
        P(None, None, cols),
        P(None, cols),
        P(cols, None),
        vec,
        vec,
        vec,
        P(None, cols),
        P(cols),
        P(cols, None),
        vec,
        vec,
        vec,
    )
    in_specs = (P(rows, None), P("dp", None), P("dp", None)) + params + params
    out_specs = (P(rows, None), P("dp"), P(rows, None)) + params
    return jax.shard_map(body, mesh=mesh, in_specs=in_specs, out_specs=out_specs, check_vma=False)
```

```python
import functools

import jax
import jax.numpy as jnp
from jax import lax
from jax.experimental import pallas as pl
from jax.experimental.pallas import tpu as pltpu
from jax.sharding import PartitionSpec as P

HEAD_DIM = 64
LANES = 128
CLIP_RANGE = 3.0
NORM_EPSILON = 1e-05
MASKED_SCORE = -1e30
SEG_LANE = HEAD_DIM
ROW_TERM = HEAD_DIM + 16
Q_BLOCK = 256
PACK_PAD = 32
CHUNKS = 2
BF16, F32 = jnp.bfloat16, jnp.float32
ROWS_ROWS = (((0,), (0,)), ((), ()))
COLS_COLS = (((1,), (1,)), ((), ()))


def clip_act(values):
    return CLIP_RANGE * jnp.tanh(values / CLIP_RANGE)


def clip_slope(values):
    level = jnp.tanh(values / CLIP_RANGE)
    return 1.0 - level * level


def normal_parts(values):
    bell = jnp.exp(-0.5 * values * values)
    step = 1.0 / (1.0 + 0.23164188843 * jnp.abs(values))
    series = 0.5307027145 * step - 0.7265760135
    series = series * step + 0.7107068705
    series = series * step - 0.142248368
    series = series * step + 0.127414796
    tail = series * step * bell
    return jnp.where(values >= 0.0, 1.0 - tail, tail), bell


def norm_forward(hidden, gain, shift):
    row_mean = jnp.mean(hidden, axis=-1, keepdims=True)
    centred = hidden - row_mean
    inv_std = lax.rsqrt(jnp.mean(centred * centred, axis=-1, keepdims=True) + NORM_EPSILON)
    normed = centred * inv_std
    return (normed * gain + shift, normed, inv_std)


def norm_backward(grad_out, normed, inv_std, gain):
    grad_normed = grad_out * gain
    centre = jnp.mean(grad_normed, axis=-1, keepdims=True)
    inner_sum = jnp.mean(grad_normed * normed, axis=-1, keepdims=True)
    return inv_std * (grad_normed - centre - normed * inner_sum)


def dot(left, right):
    return jnp.dot(left, right, preferred_element_type=F32)


def dot_rows(left, right):
    return lax.dot_general(left, right, ROWS_ROWS, preferred_element_type=F32)


def dot_cols(left, right):
    return lax.dot_general(left, right, COLS_COLS, preferred_element_type=F32)


def swap(array, bit):
    size = lax.axis_size("tensor")
    return lax.ppermute(array, "tensor", [(i, i ^ bit) for i in range(size)])


def lookup(indices, lookup_table):
    labels = jnp.arange(lookup_table.shape[0], dtype=jnp.int32)
    picked = jnp.where(indices[:, None] == labels[None, :], lookup_table[None, :], 0)
    return jnp.sum(picked, axis=1)


def segment_tables(lengths, parent):
    count = lengths.shape[0]
    labels = jnp.arange(count, dtype=jnp.int32)
    row, col = labels[:, None], labels[None, :]
    starts = jnp.sum(jnp.where(col < row, lengths[None, :], 0), axis=1)
    two = lookup(parent, parent)
    allowed = (col == row) | (col == parent[:, None]) | (col == two[:, None])
    allowed = allowed | (parent[None, :] == row) | (two[None, :] == row)
    after = LANES - SEG_LANE - count
    lanes = jnp.pad(jnp.stack([starts, starts + lengths]), ((0, 6), (SEG_LANE, after)))
    blocked = jnp.pad((~allowed).astype(BF16), ((SEG_LANE, after), (SEG_LANE, after)))
    return lanes, blocked


def split_three(values):
    first = values.astype(BF16).astype(F32)
    second = (values - first).astype(BF16).astype(F32)
    return first, second, values - first - second


def sign_of(values):
    return jnp.where(values > 0.0, 1.0, jnp.where(values < 0.0, -1.0, 0.0))


def prepare_kernel(
    out_ref, t_out_ref, up_ref, down_ref, t_up_ref, t_down_ref, t_bias_ref, *rest
):
    *vectors, outs_ref, w_up_ref, s_down_ref, pack_ref, sums_ref, vec_ref = rest
    vec_ref[...] = jnp.zeros_like(vec_ref)
    for index, vector in enumerate(vectors):
        vec_ref[index : index + 1, :] = vector[...].astype(F32).reshape(1, -1)
    hidden, width = down_ref.shape
    half = hidden // 2
    rows = out_ref.shape[0]
    total = lambda ref: jnp.sum(jnp.abs(ref[...]), axis=0, keepdims=True)
    sums_ref[...] = jnp.zeros_like(sums_ref)
    sums_ref[0:1, :] = total(out_ref)
    sums_ref[1:2, :] = total(down_ref)
    outs_ref[:rows, :] = sign_of(out_ref[...]).astype(BF16)
    outs_ref[rows:, :] = t_out_ref[...]
    w_up_ref[...] = (total(up_ref) * (1.0 / width) * sign_of(up_ref[...])).astype(BF16)
    s_down_ref[...] = sign_of(down_ref[...]).astype(BF16)
    up_t = t_up_ref[...].T
    pack_ref[:, hidden:, :] = jnp.zeros((2, PACK_PAD, width), BF16)
    for side in range(2):
        cols = slice(side * half, (side + 1) * half)
        pack_ref[side, :half, :] = up_t[cols]
        pack_ref[side, half:hidden, :] = t_down_ref[cols, :]
        bias = t_bias_ref[cols].astype(F32).reshape(1, -1)
        pack_ref[side, hidden : hidden + 1, :half] = bias.astype(BF16)


def prepare(latents, vectors):
    array = jax.ShapeDtypeStruct
    out_latent, _, up_latent, down_latent, *_ = latents
    hidden, width = down_latent.shape
    return pl.pallas_call(
        prepare_kernel,
        out_shape=[
            array((2 * out_latent.shape[0], width), BF16),
            array(up_latent.shape, BF16),
            array(down_latent.shape, BF16),
            array((2, hidden + PACK_PAD, width), BF16),
            array((8, width), F32),
            array((16, width), F32),
        ],
        compiler_params=pltpu.CompilerParams(vmem_limit_bytes=58 * 2**20),
        name="prepare",
    )(*latents, *vectors)


def in_lane(shape, axis, terms):
    lane = lax.broadcasted_iota(jnp.int32, shape, axis)
    spread = jnp.zeros(shape, F32)
    for offset, term in enumerate(terms):
        spread = jnp.where(lane == ROW_TERM + offset, term, spread)
    return spread


def make_copies(send_sem, recv_sem):
    count = [0]

    def copy_to(source, target, axis, device):
        index = count[0]
        count[0] += 1

        def make():
            return pltpu.make_async_remote_copy(
                src_ref=source,
                dst_ref=target,
                send_sem=send_sem.at[index],
                recv_sem=recv_sem.at[index],
                device_id={axis: device},
                device_id_type=pl.DeviceIdType.MESH,
            )

        return make

    return copy_to


def greet(others):
    barrier = pltpu.get_barrier_semaphore()
    for other in others:
        pl.semaphore_signal(barrier, inc=1, device_id=other, device_id_type=pl.DeviceIdType.MESH)
    pl.semaphore_wait(barrier, len(others))


def neighbours():
    me = lax.axis_index("tensor")
    return me + 1 - 2 * lax.rem(me, 2), lax.rem(me + 2, lax.axis_size("tensor"))


def forward_kernel(base_ref, x0, x1, x2, x3, w_ref, b_ref, seg_ref, blocked_ref, *rest, student):
    if student:
        pack_ref, outs, sums_ref, *rest = rest
        q_ref, k_ref, v_ref, ctx_ref, source, own, near, far, *rest = rest
        sums_out, pack_near, piece_a, outs1, outs2, sums, *rest = rest
    else:
        ca_near, ca_far, outs2, piece_a, *rest = rest
        sent, ta0, ca1, ca2, ca_pass, ca3, ta1, ta2, ta_pass, ta3, *rest = rest
        outs3, next_a, piece_b, piece_c, source, send_a, *rest = rest
    joined, queries, keys, vals_t, send_sem, recv_sem = rest
    blocks = (x0, x1, x2, x3)
    own_rows = x0.shape[0]
    rows = own_rows * len(blocks)
    heads = joined.shape[0]
    head = pl.program_id(0)
    near_id, far_id = neighbours()
    place = lax.axis_index("dp")
    copy_to = make_copies(send_sem, recv_sem)
    side_id, side = in_pair(place, 1)
    next_id, level = in_pair(place, 2)
    others = [{"tensor": near_id}, {"tensor": far_id}, {"dp": side_id}]
    if not student:
        others.append({"dp": next_id})
    if student:
        size = piece_a.shape[0]
        quarter = pack_ref.at[side, pl.ds(pl.multiple_of(level * size, 16), size)]
        half = outs.shape[0] // 2
        rows_of = pl.ds(pl.multiple_of(side * half, 16), half)
        outs_far = copy_to(outs.at[rows_of], outs2.at[rows_of], "tensor", far_id)
        pack_far = copy_to(quarter, piece_a, "tensor", far_id)
        sum_near = copy_to(sums.at[0], sums.at[1], "tensor", near_id)
        sum_far = copy_to(sums.at[2], sums.at[3], "tensor", far_id)
        stages = [
            (
                [],
                [
                    sum_near,
                    outs_far,
                    copy_to(outs, outs1, "tensor", near_id),
                    copy_to(pack_ref, pack_near, "tensor", near_id),
                ],
            ),
            ([outs_far], [pack_far, copy_to(outs2.at[rows_of], outs2.at[rows_of], "dp", side_id)]),
            ([], []),
        ]
    else:
        passing = copy_to(ca_far.at[1], ca_pass, "tensor", far_id)
        stages = [
            (
                [],
                [
                    passing,
                    copy_to(ca_far.at[0], ca2, "tensor", far_id),
                    copy_to(ca_near, ca1, "tensor", near_id),
                    copy_to(outs2, outs3, "tensor", near_id),
                    copy_to(piece_a, next_a, "dp", next_id),
                    copy_to(piece_a, piece_c, "tensor", near_id),
                    copy_to(piece_a, piece_b, "dp", side_id),
                ],
            ),
            ([], []),
            ([passing], [copy_to(ca_pass, ca3, "tensor", near_id)]),
        ]
        a_passing = copy_to(send_a.at[3], ta_pass, "tensor", far_id)
        a_copies = [
            a_passing,
            copy_to(send_a.at[2], ta2, "tensor", far_id),
            copy_to(send_a.at[1], ta1, "tensor", near_id),
        ]
        a_last = copy_to(ta_pass, ta3, "tensor", near_id)

    def run_stage(index):
        before, copies = stages[index]
        for copy in before:
            copy().wait_recv()
        for copy in copies:
            copy().start()

    @pl.when(head == 0)
    def _():
        if student:
            sums[0] = sums_ref[...]
        greet(others)
        run_stage(0)
        lane = lax.broadcasted_iota(jnp.int32, (own_rows, LANES), 1)
        ones = (lane >= ROW_TERM) & (lane < ROW_TERM + 3)
        for j, block in enumerate(blocks):
            part = slice(j * own_rows, (j + 1) * own_rows)
            if student:
                source[part, :] = clip_act(block[...].astype(F32)).astype(BF16)
            else:
                source[part, :] = block[...]
            spot = lax.broadcasted_iota(jnp.int32, (own_rows, LANES), 0) + base_ref[j]
            inside = (spot >= seg_ref[0:1, :]) & (spot < seg_ref[1:2, :])
            links = dot(jnp.where(inside, 1.0, 0.0).astype(BF16), blocked_ref[...])
            extras = (
                jnp.where(inside, MASKED_SCORE, 0.0).astype(BF16),
                jnp.where(ones, 1.0, links).astype(BF16),
                jnp.where(ones, 1.0, 0.0).astype(BF16),
            )
            for c, (scale, extra) in enumerate(zip((0.125, 1.0, 1.0), extras)):
                proj = dot(source[part, :], w_ref[c]) + b_ref[c : c + 1, :]
                proj = proj.astype(BF16)
                for h in range(heads):
                    one = proj[:, h * HEAD_DIM : (h + 1) * HEAD_DIM] * scale
                    wide = jnp.concatenate([one, jnp.zeros_like(one)], axis=1) + extra
                    if c == 0:
                        queries[h, part, :] = wide
                    elif c == 1:
                        keys[h, part, :] = wide
                    else:
                        vals_t[h, :, part] = wide.T
                        if student:
                            v_ref[h, part, :] = wide

    if student:
        k_ref[0] = keys[head]
    else:

        @pl.when(head == heads - 1)
        def _():
            for j in range(len(blocks)):
                part = slice(j * own_rows, (j + 1) * own_rows)
                pair = jnp.concatenate([joined[0, part, :], joined[1, part, :]], axis=1)
                send_a[j] = pair.astype(BF16)
            for copy in a_copies:
                copy().start()

    scores = {}
    for index in range(rows // Q_BLOCK):
        if index % (rows // Q_BLOCK // 2) == 0:
            if index:

                @pl.when(head == 0)
                def _():
                    run_stage(1)

                @pl.when(head == 1)
                def _():
                    run_stage(2)
                    if student:
                        sum_near().wait_recv()
                        sums[2] = sums[0] + sums[1]
                        sum_far().start()

            for later in range(index, index + rows // Q_BLOCK // 2):
                start = later * Q_BLOCK
                scores[later] = dot_cols(keys[head], queries[head, start : start + Q_BLOCK, :])
        block = scores[index]
        part = slice(index * Q_BLOCK, (index + 1) * Q_BLOCK)
        peak = jnp.max(block, axis=0, keepdims=True)
        raised = jnp.exp(block - peak)
        total = jnp.sum(raised, axis=0, keepdims=True)
        weights = (raised * (1.0 / total)).astype(BF16)
        context = dot(vals_t[head], weights)[:HEAD_DIM].T
        joined[head, part, :] = context
        if student:
            ctx_ref[0, part, :] = context
            terms = split_three(-(peak + jnp.log(total)))
            spread = in_lane((LANES, Q_BLOCK), 0, terms)
            q_ref[0, part, :] = queries[head, part, :] + spread.T.astype(BF16)

    @pl.when(head == heads - 1)
    def _():
        for j in range(len(blocks)):
            part = slice(j * own_rows, (j + 1) * own_rows)
            if not student:
                sent[j] = stacked(joined[heads - 1, part, :]).astype(BF16)
                continue
            block = jnp.concatenate([joined[h, part, :] for h in range(heads)], axis=1)
            if j < 2:
                (own, near)[j][...] = clip_act(block).astype(BF16)
            else:
                far[j - 2] = clip_act(block).astype(BF16)
        waited = [copy for before, _ in stages for copy in before]
        if not student:
            ta0[...] = send_a[0]
            a_passing().wait_recv()
            a_last().start()
            for copy in a_copies:
                copy().wait_send()
            for copy in a_copies[1:] + [a_last]:
                copy().wait_recv()
            a_last().wait_send()
        if student:
            sum_far().wait_recv()
            sums_out[...] = sums[2] + sums[3]
            sum_far().wait_send()
            waited.append(sum_near)
        for _, copies in stages:
            for copy in copies:
                copy().wait_send()
                if copy not in waited:
                    copy().wait_recv()


def attend_forward(base, blocks, weight, bias, seg_lanes, blocked, moved, student):
    own_rows, width = blocks[0].shape
    rows = own_rows * len(blocks)
    head_cols = weight.shape[2]
    heads = head_cols // HEAD_DIM
    whole = lambda *shape: pl.BlockSpec(shape, lambda h: (0,) * len(shape))
    anywhere = pl.BlockSpec(memory_space=pl.ANY)
    array = jax.ShapeDtypeStruct
    per_head = lambda cols: pl.BlockSpec((1, rows, cols), lambda h: (h, 0, 0))
    if student:
        pack, out_weights, sums = moved
        piece = (pack.shape[1] // 2, width)
        outs = [
            (per_head(LANES), array((heads, rows, LANES), BF16)),
            (per_head(LANES), array((heads, rows, LANES), BF16)),
            (whole(heads, rows, LANES), array((heads, rows, LANES), BF16)),
            (per_head(HEAD_DIM), array((heads, rows, HEAD_DIM), F32)),
            (whole(rows, width), array((rows, width), BF16)),
            (whole(own_rows, head_cols), array((own_rows, head_cols), BF16)),
            (whole(own_rows, head_cols), array((own_rows, head_cols), BF16)),
            (whole(2, own_rows, head_cols), array((2, own_rows, head_cols), BF16)),
            (whole(*sums.shape), array(sums.shape, F32)),
            (anywhere, array(pack.shape, BF16)),
        ]
        outs += [(anywhere, array(piece, BF16))]
        outs += [(anywhere, array(out_weights.shape, BF16))] * 2
        scratch, transfers = [pltpu.VMEM((4,) + sums.shape, F32)], 7
    else:
        ca_near, ca_far, out_weights, piece = moved
        last = (len(blocks), own_rows // 2, LANES)
        pair = array((own_rows, LANES), BF16)
        outs = [(whole(*last), array(last, BF16)), (whole(*pair.shape), pair)]
        outs += [(anywhere, array(ca_near.shape, BF16))] * 4 + [(anywhere, pair)] * 4
        outs += [(anywhere, array(out_weights.shape, BF16))]
        outs += [(anywhere, array(piece.shape, BF16))] * 3
        scratch, transfers = [pltpu.VMEM((rows, width), BF16)], 12
        scratch.append(pltpu.VMEM((len(blocks),) + pair.shape, BF16))
    scratch += [
        pltpu.VMEM((heads, rows, HEAD_DIM), F32),
        pltpu.VMEM((heads, rows, LANES), BF16),
        pltpu.VMEM((heads, rows, LANES), BF16),
        pltpu.VMEM((heads, LANES, rows), BF16),
        pltpu.SemaphoreType.DMA((transfers,)),
        pltpu.SemaphoreType.DMA((transfers,)),
    ]
    return pl.pallas_call(
        functools.partial(forward_kernel, student=student),
        grid=(heads,),
        in_specs=[pl.BlockSpec(memory_space=pltpu.SMEM)]
        + [whole(own_rows, width)] * 4
        + [whole(*a.shape) for a in (weight, bias, seg_lanes, blocked)]
        + [whole(*a.shape) if a.dtype == F32 else anywhere for a in moved],
        out_specs=[spec for spec, _ in outs],
        out_shape=[shape for _, shape in outs],
        scratch_shapes=scratch,
        compiler_params=pltpu.CompilerParams(
            collective_id=1 if student else 2, has_side_effects=True, vmem_limit_bytes=58 * 2**20
        ),
        cost_estimate=pl.CostEstimate(
            flops=16 * heads * rows * rows * HEAD_DIM,
            bytes_accessed=2 * rows * (width + 6 * heads * LANES),
            transcendentals=heads * rows * rows,
        ),
        name="student_attention" if student else "teacher_attention",
    )(base, *blocks, weight, bias, seg_lanes, blocked, *moved)


def in_pair(place, bit):
    digit = lax.rem(lax.div(place, bit), 2)
    return place + bit - 2 * bit * digit, digit


def halving_steps(partial, total, landing, rows, landing_row, order, place, copy_of, done=0, base=None):
    low, size = rows
    here = low if base is None else base
    steps, levels, used = [], [], landing_row
    for level, bit in enumerate(order):
        partner, digit = in_pair(place, bit)
        halved = size % 32 == 0
        count = size // 2 if halved else size
        low = pl.multiple_of(low + digit * count, 16) if halved else low
        if level >= done:
            give = pl.multiple_of(here + (1 - digit) * count, 16) if halved else here
            here = pl.multiple_of(here + digit * count, 16) if halved else here
            copy = copy_of(partial.at[pl.ds(give, count)], landing.at[pl.ds(used, count)], partner)
            last = level == len(order) - 1

            def add(used=used, here=here, count=count, out=total if last else partial, at=low if last else here):
                arrived = landing[used : used + count, :].astype(F32)
                mine = partial[pl.ds(here, count), :].astype(F32)
                out[pl.ds(at, count), :] = (mine + arrived).astype(out.dtype)

            steps.append((copy, add))
            used += count
        if halved:
            levels.append((count, low, partner))
        size = count
    for count, keep, partner in reversed(levels):
        where = total.at[pl.ds(keep, count)]
        steps.append((copy_of(where, where, partner), lambda: None))
    return steps, used


def run_step(plans, index):
    for steps in plans:
        if 0 < index <= len(steps):
            copy, after = steps[index - 1]
            copy().wait()
            after()
        if index < len(steps):
            steps[index][0]().start()


def split_rows(first, count):
    small = count // 2 if count % 512 == 0 else -(-count // 3 // 64) * 64
    return ((first, count - small), (first + count - small, small))


def dp_bits():
    bits = [1 << i for i in range((lax.axis_size("dp") - 1).bit_length())]
    return bits, (bits[1:2] + bits[:1] + bits[2:])


def backward_kernel(
    q_ref, k_ref, v_ref, ctx_ref, x_ref, w_ref, g0, g1, g2, g3, ffn_ref, outg_ref, small_ref,
    ffn_out, late_out, small_out, gx_out, gxfar_out,
    grads, wide, packed, keys_t, total, ffn_part, ffn, late_in, late, small, small_in, landing, small_land,
    out_near, out_near_land, out_far, out_far_land, gx_near, gx_near_land, gx_far, gx_far_land,
    send_sem, recv_sem, write_sem, *, key_block,
):
    blocks = (g0, g1, g2, g3)
    rows = x_ref.shape[0]
    own_rows = rows // len(blocks)
    heads = grads.shape[0]
    head_cols = heads * HEAD_DIM
    head = pl.program_id(0)
    place = lax.axis_index("dp")
    near_id, far_id = neighbours()
    part = lambda j: slice(j * own_rows, (j + 1) * own_rows)
    bits, turned = dp_bits()

    copy_to = make_copies(send_sem, recv_sem)
    over_dp = lambda source, target, other: copy_to(source, target, "dp", other)
    over_tensor = lambda source, target, other: copy_to(source, target, "tensor", other)

    used = [0]

    def reduced(partial, target, first, size, done=0):
        plans, taken = [], 0
        for rows_of, order in zip(split_rows(first, size), (bits, turned)):
            steps, used[0] = halving_steps(
                partial, target, landing, rows_of, used[0], order, place, over_dp, done,
                taken if done else None,
            )
            plans.append(steps)
            taken += rows_of[1] >> done
        return plans

    width = x_ref.shape[1]
    ffn_plans = reduced(ffn_part, ffn, 0, ffn.shape[0], 1)
    early_plans = reduced(late_in, late, 0, 2 * head_cols)
    middle_plans = reduced(late_in, late, 2 * head_cols, head_cols)
    last_plans = reduced(late_in, late, 3 * head_cols, head_cols)
    small_steps = []
    for level, bit in enumerate(bits):
        partner, _ = in_pair(place, bit)
        small_steps.append(over_dp(small_in.at[level], small_land.at[level], partner))
    tensor_small = [
        over_tensor(small.at[0], small.at[1], near_id),
        over_tensor(small.at[2], small.at[3], far_id),
    ]
    out_steps = [
        over_tensor(out_near, out_near_land, near_id),
        over_tensor(out_far, out_far_land, far_id),
    ]
    gx_steps = [
        over_tensor(gx_near, gx_near_land, near_id),
        over_tensor(gx_far, gx_far_land, far_id),
    ]

    @pl.when(head == 0)
    def _():
        others = [{"tensor": near_id}, {"tensor": far_id}]
        greet(others + [{"dp": in_pair(place, bit)[0]} for bit in bits])
        ffn_part[...] = ffn_ref[...]
        run_step(ffn_plans, 0)
        out_near[0] = outg_ref[1]
        out_near[1] = outg_ref[3]
        out_steps[0]().start()
        small[0] = small_ref[...]
        tensor_small[0]().start()
        size = own_rows // CHUNKS
        for j, block in enumerate(blocks):
            for c in range(CHUNKS):
                where = slice(j * own_rows + c * size, j * own_rows + (c + 1) * size)
                pair = block[c, :size, :]
                ones = [pair[:, :HEAD_DIM], pair[:, HEAD_DIM:], side_by_side(block[c, size:, :])]
                for h, one in enumerate(ones):
                    grads[h, where, :] = jnp.concatenate([one, jnp.zeros_like(one)], axis=1)
        packed[...] = jnp.zeros_like(packed)
        wide[...] = jnp.zeros_like(wide)
        for h in range(heads):
            for c, scale in enumerate((0.125, 1.0, 1.0)):
                one = w_ref[c, :, h * HEAD_DIM : (h + 1) * HEAD_DIM] * scale
                wide[h, :, c * LANES : c * LANES + HEAD_DIM] = one

    queries = q_ref[0]
    slopes = grads[head]
    inner = -jnp.sum(slopes[:, :HEAD_DIM].astype(F32) * ctx_ref[0], axis=1, keepdims=True)
    slopes = slopes + in_lane((rows, LANES), 1, split_three(inner)).astype(BF16)
    keys_t[...] = k_ref[0].T

    def over_keys(first, last, query_grad):
        for start in range(first, last, key_block):
            span = slice(start, start + key_block)
            weights = jnp.exp(dot_cols(k_ref[0, span, :], queries))
            grad_weights = dot_cols(v_ref[0, span, :], slopes)
            grad_scores = (weights * grad_weights).astype(BF16)
            step = dot(keys_t[:, span], grad_scores)
            query_grad = step if query_grad is None else query_grad + step
            key_grad = dot(grad_scores, queries)[:, :HEAD_DIM]
            packed[span, LANES : LANES + HEAD_DIM] = key_grad.astype(BF16)
            value_grad = dot(weights.astype(BF16), slopes)[:, :HEAD_DIM]
            packed[span, 2 * LANES : 2 * LANES + HEAD_DIM] = value_grad.astype(BF16)
        return query_grad

    def at(which):
        return pl.when(head == which)

    quarter = rows // 4
    query_grad = over_keys(0, quarter, None)

    @at(1)
    def _():
        run_step(ffn_plans, 2)

    query_grad = over_keys(quarter, 2 * quarter, query_grad)

    @at(0)
    def _():
        run_step(ffn_plans, 1)
        out_steps[0]().wait_recv()
        out_far[...] = (outg_ref[2].astype(F32) + out_near_land[1].astype(F32)).astype(BF16)
        out_steps[1]().start()
        tensor_small[0]().wait_recv()
        small[2] = small[0] + small[1]
        tensor_small[1]().start()

    @at(1)
    def _():
        run_step(early_plans, 1)

    @at(2)
    def _():
        run_step(ffn_plans, 4)
        run_step(early_plans, 3)
        run_step(middle_plans, 1)

    query_grad = over_keys(2 * quarter, rows, query_grad)
    packed[:, :HEAD_DIM] = query_grad[:HEAD_DIM].T.astype(BF16)
    sums = jnp.sum(packed[...].astype(F32), axis=0, keepdims=True)
    small[4 + head, 0:1, : 3 * LANES] = sums
    weight_grad = dot_rows(packed[...], x_ref[...])
    slot = jnp.where(head == 0, 0, head_cols + head * head_cols)
    for c, factor in enumerate((0.125, 1.0, 1.0)):
        target = pl.multiple_of(slot + c * HEAD_DIM, HEAD_DIM)
        late_in[pl.ds(target, HEAD_DIM), :] = (
            weight_grad[c * LANES : c * LANES + HEAD_DIM] * factor
        ).astype(BF16)

    @pl.when(head == 0)
    def _():
        out_steps[1]().wait_recv()
        late_in[head_cols : 2 * head_cols, :] = (
            outg_ref[0].astype(F32)
            + out_near_land[0].astype(F32)
            + out_far_land[...].astype(F32)
        ).astype(BF16)
        tensor_small[1]().wait_recv()
        run_step(early_plans, 0)

    @pl.when(head == 1)
    def _():
        run_step(middle_plans, 0)
        run_step(ffn_plans, 3)
        run_step(early_plans, 2)

    @pl.when(head == 2)
    def _():
        run_step(last_plans, 0)
        small_in[0, :8, :] = small[2] + small[3]
        small_in[0, UP_ROW : UP_ROW + 1, :] = small_ref[UP_ROW : UP_ROW + 1, :]
        small_in[0, 8:, :] = jnp.zeros((8, width), F32)
        for h in range(heads):
            small_in[0, 8 + h : 9 + h, : 3 * LANES] = small[4 + h, 0:1, : 3 * LANES]
        small_steps[0]().start()

    for j in (1, 3, 2, 0):
        step = dot_cols(packed[part(j), :], wide[head])
        total[part(j), :] = jnp.where(head == 0, step, total[part(j), :] + step)

    @pl.when(head == heads - 1)
    def _():
        gx_near[0] = total[part(1), :].astype(BF16)
        gx_near[1] = total[part(3), :].astype(BF16)
        gx_steps[0]().start()
        run_step(last_plans, 1)
        gx_steps[0]().wait_recv()
        gx_far[...] = (total[part(2), :] + gx_near_land[1].astype(F32)).astype(BF16)
        gx_steps[1]().start()
        total[part(0), :] = total[part(0), :] + gx_near_land[0].astype(F32)
        gx_write = pltpu.make_async_copy(total.at[part(0)], gx_out, write_sem.at[0])
        gx_write.start()
        run_step(early_plans, 4)
        run_step(middle_plans, 2)
        for index in range(1, 2 * len(bits) + 1):
            if index > 1:
                run_step(last_plans, index)
            if index <= len(bits):
                small_steps[index - 1]().wait_recv()
                arrived = small_in[index - 1] + small_land[index - 1]
                if index < len(bits):
                    small_in[index] = arrived
                    small_steps[index]().start()
                else:
                    small_out[...] = arrived
            run_step(middle_plans, 2 + index)
            run_step(early_plans, 4 + index)
        for index in range(5, 2 * len(bits) + 1):
            run_step(ffn_plans, index)
        ffn_write = pltpu.make_async_copy(ffn, ffn_out, write_sem.at[1])
        ffn_write.start()
        late_write = pltpu.make_async_copy(late, late_out, write_sem.at[2])
        late_write.start()
        gx_steps[1]().wait_recv()
        far_write = pltpu.make_async_copy(gx_far_land, gxfar_out, write_sem.at[3])
        far_write.start()
        shared = small[2, LOSS_ROW : LOSS_ROW + 1, :] + small[3, LOSS_ROW : LOSS_ROW + 1, :]
        small_out[LOSS_ROW : LOSS_ROW + 1, :] = shared
        for copy in small_steps + tensor_small + out_steps + gx_steps:
            copy().wait_send()
        for copy in (gx_write, ffn_write, late_write, far_write):
            copy.wait()


def attend_backward(qkv, context, source, weight, blocks, ffn_grads, out_grads, small):
    rows, width = source.shape
    own_rows, head_cols = rows // len(blocks), weight.shape[2]
    cols = 3 * LANES
    heads = head_cols // HEAD_DIM
    levels = (lax.axis_size("dp") - 1).bit_length()
    ffn_rows, late_rows = 2 * ffn_grads.shape[0], (heads + 1) * head_cols
    landing = ffn_rows + late_rows + 8 * 48 * levels
    transfers = 2 * 4 * 2 * levels + levels + 6
    array = jax.ShapeDtypeStruct
    whole = lambda *shape: pl.BlockSpec(shape, lambda h: (0,) * len(shape))
    head_block = lambda *shape: pl.BlockSpec((1,) + shape, lambda h: (h, 0, 0))
    anywhere = pl.BlockSpec(memory_space=pl.ANY)
    return pl.pallas_call(
        functools.partial(backward_kernel, key_block=256),
        grid=(heads,),
        in_specs=[
            head_block(rows, LANES),
            head_block(rows, LANES),
            head_block(rows, LANES),
            head_block(rows, HEAD_DIM),
            whole(rows, width),
            whole(*weight.shape),
        ]
        + [whole(*block.shape) for block in blocks]
        + [whole(*ffn_grads.shape), whole(*out_grads.shape), whole(*small.shape)],
        out_specs=[
            anywhere,
            anywhere,
            whole(16, width),
            anywhere,
            anywhere,
        ],
        out_shape=[
            array((ffn_rows, width), BF16),
            array((late_rows, width), BF16),
            array((16, width), F32),
            array((own_rows, width), F32),
            array((own_rows, width), BF16),
        ],
        scratch_shapes=[
            pltpu.VMEM((heads, rows, LANES), BF16),
            pltpu.VMEM((heads, width, cols), BF16),
            pltpu.VMEM((rows, cols), BF16),
            pltpu.VMEM((LANES, rows), BF16),
            pltpu.VMEM((rows, width), F32),
            pltpu.VMEM((ffn_rows // 2, width), BF16),
            pltpu.VMEM((ffn_rows, width), BF16),
            pltpu.VMEM((late_rows, width), BF16),
            pltpu.VMEM((late_rows, width), BF16),
            pltpu.VMEM((4 + heads, 8, width), F32),
            pltpu.VMEM((levels, 16, width), F32),
            pltpu.VMEM((landing, width), BF16),
            pltpu.VMEM((levels, 16, width), F32),
            pltpu.VMEM((2, head_cols, width), BF16),
            pltpu.VMEM((2, head_cols, width), BF16),
            pltpu.VMEM((head_cols, width), BF16),
            pltpu.VMEM((head_cols, width), BF16),
            pltpu.VMEM((2, own_rows, width), BF16),
            pltpu.VMEM((2, own_rows, width), BF16),
            pltpu.VMEM((own_rows, width), BF16),
            pltpu.VMEM((own_rows, width), BF16),
            pltpu.SemaphoreType.DMA((transfers,)),
            pltpu.SemaphoreType.DMA((transfers,)),
            pltpu.SemaphoreType.DMA((4,)),
        ],
        compiler_params=pltpu.CompilerParams(
            collective_id=4, has_side_effects=True, vmem_limit_bytes=62 * 2**20
        ),
        cost_estimate=pl.CostEstimate(
            flops=60 * heads * rows * rows * HEAD_DIM,
            bytes_accessed=2 * rows * heads * (cols + 7 * LANES),
            transcendentals=heads * rows * rows,
        ),
        name="attention_backward",
    )(*qkv, context, source, weight, *blocks, ffn_grads, out_grads, small)


def stacked(block):
    half = block.shape[0] // 2
    return jnp.concatenate([block[:half], block[half:]], axis=1)


def side_by_side(block):
    return jnp.concatenate([block[:, :HEAD_DIM], block[:, HEAD_DIM:]], axis=0)


(OUT_BIAS, GAIN_1, SHIFT_1, DOWN_BIAS, GAIN_2, SHIFT_2, UP_BIAS) = range(7)
T_VECTORS = 7
LOSS_ROW, UP_ROW = 6, 7


def middle_kernel(
    x_ref, ca0, ca1, ca2, ca3, tc_ref, ta0, ta1, ta2, ta3, outs0, outs1, outs2, outs3, w_up, s_down, vec,
    pack_own, pack_near, piece_a, piece_b, piece_c, next_a, sums_ref,
    out_ref, gh_ref, kept_ref, outg_ref, g0_ref, g1_ref, g2_ref, g3_ref, small_ref, piece_d, next_b, next_c, next_d,
    tc1, tc2, tcf, tc3, y_all, g_all, slope, hid, gu_all, t_out, first, normed, two, inv,
    part0, part2, send1, send2, send3, near0, near2, far0, gs, gr, packs, ffn_ref, ffn_land, w_outs, w_down,
    send_sem, recv_sem, pack_sem,
):
    near_id, far_id = neighbours()
    own_rows, width = x_ref.shape
    hidden = s_down.shape[0]
    head_cols = ca0.shape[1]
    size = own_rows // CHUNKS
    chunks = [slice(c * size, (c + 1) * size) for c in range(CHUNKS)]
    tiles = [slice(n, n + 256) for n in range(0, hidden, 256)]
    group = lambda j: slice(j * head_cols, (j + 1) * head_cols)
    outs = (outs0, outs1, outs2, outs3)
    w_out = lambda j: w_outs[j]
    tw_out = lambda j: outs[j][head_cols:, :]
    row = lambda index: vec[index : index + 1, :]

    place = lax.axis_index("dp")
    others = [{"tensor": near_id}, {"tensor": far_id}]
    others += [{"dp": in_pair(place, bit)[0]} for bit in dp_bits()[0][:2]]
    greet(others)

    count = [0]
    started = []

    def put(source, target, device, axis="tensor"):
        index = count[0]
        count[0] += 1
        copy = pltpu.make_async_remote_copy(
            src_ref=source,
            dst_ref=target,
            send_sem=send_sem.at[index],
            recv_sem=recv_sem.at[index],
            device_id={axis: device},
            device_id_type=pl.DeviceIdType.MESH,
        )
        copy.start()
        started.append(copy)
        return copy

    t_far = put(tc_ref.at[2], tc2, far_id)
    t_pass = put(tc_ref.at[3], tcf, far_id)
    t_near = put(tc_ref.at[1], tc1, near_id)
    next_id, level = in_pair(place, 2)
    cut = piece_a.shape[0]
    here = pl.ds(pl.multiple_of(level * cut, 16), cut)
    there = pl.ds(pl.multiple_of((1 - level) * cut, 16), cut)
    next_copies = [
        put(next_a, next_c, near_id),
        put(piece_b, next_b, next_id, "dp"),
        put(piece_b, piece_d, near_id),
    ]

    pack_refs = [pack_own.at[0], pack_own.at[1], pack_near.at[0], pack_near.at[1]]
    pack_refs += [(piece_a, next_a), (piece_c, next_c), (piece_b, next_b), (piece_d, next_d)]

    def load_pack(index):
        slot = index % 2
        source, target = pack_refs[index], packs.at[slot]
        if not isinstance(source, tuple):
            return [pltpu.make_async_copy(source, target, pack_sem.at[slot])]
        return [
            pltpu.make_async_copy(source[0], target.at[here], pack_sem.at[slot]),
            pltpu.make_async_copy(source[1], target.at[there], pack_sem.at[2 + slot]),
        ]

    def start_pack(index):
        for copy in load_pack(index):
            copy.start()

    start_pack(0)
    a_out = (sums_ref[0:1, :] * (1.0 / width)).astype(BF16)
    a_down = (sums_ref[1:2, :] * (1.0 / (lax.axis_size("tensor") * hidden))).astype(BF16)
    for j in range(4):
        w_outs[j] = outs[j][:head_cols, :] * a_out
    w_down[...] = s_down[...] * a_down
    small_ref[...] = jnp.zeros_like(small_ref)

    def add_small(index, values):
        small_ref[index : index + 1, :] += jnp.sum(values, axis=0, keepdims=True)

    def share(own_block, where):
        return (
            put(own_block.at[0, where], own_block.at[1, where], near_id),
            put(own_block.at[0, where], own_block.at[2, where], far_id),
        )

    y_sent = []
    for rows in chunks:
        attn = dot(ca0[rows, :], w_out(0)) + dot(ca1[rows, :], w_out(1))
        attn += dot(ca2[rows, :], w_out(2)) + dot(ca3[rows, :], w_out(3))
        y_one, y_normed, y_inv = norm_forward(
            x_ref[rows, :].astype(F32) + attn + row(OUT_BIAS), row(GAIN_1), row(SHIFT_1)
        )
        first[rows, :] = y_one
        normed[rows, :] = y_normed
        inv[rows, :] = jnp.broadcast_to(y_inv, (size, LANES))
        y_all[0, rows, :] = clip_act(y_one).astype(BF16)
        y_sent.append(share(y_all, rows))

    def forward_block(j, rows):
        total = None
        for cols in tiles:
            upward = dot(y_all[j, rows, :], w_up[:, cols]) + row(UP_BIAS)[:, cols]
            cdf, bell = normal_parts(upward)
            level = jnp.tanh(upward * cdf * (1.0 / CLIP_RANGE))
            act = (CLIP_RANGE * level).astype(BF16)
            hid[j, rows, cols] = act
            slope[j, rows, cols] = (1.0 - level * level) * (
                cdf + upward * bell * 0.3989422804014327
            )
            step = dot(act, w_down[cols, :])
            total = step if total is None else total + step
        return total

    def backward_block(j, rows):
        total = None
        for cols in tiles:
            grad = dot_cols(g_all[j, rows, :], w_down[cols, :])
            grad = (grad * slope[j, rows, cols]).astype(BF16)
            gu_all[j, rows, cols] = grad
            small_ref[UP_ROW : UP_ROW + 1, cols] += jnp.sum(
                grad.astype(F32), axis=0, keepdims=True
            )
            step = dot_cols(grad, w_up[:, cols])
            total = step if total is None else total + step
        return total

    def near_blocks(work, sent):
        copies = []
        for rows in chunks:
            part0[rows, :] = work(0, rows)
        for rows, (near, _) in zip(chunks, sent):
            near.wait_recv()
            send1[rows, :] = work(1, rows).astype(BF16)
            copies.append(put(send1.at[rows], near0.at[rows], near_id))
        return copies

    def far_blocks(block, work, sent, between=()):
        copies = []
        for c, (rows, (_, far)) in enumerate(zip(chunks, sent)):
            far.wait_recv()
            passed = put(block.at[2, rows], block.at[3, rows], near_id)
            part2[rows, :] = work(2, rows)
            passed.wait_recv()
            send3[rows, :] = work(3, rows).astype(BF16)
            met = put(send3.at[rows], near2.at[rows], near_id)
            met.wait_recv()
            send2[rows, :] = (part2[rows, :] + near2[rows, :].astype(F32)).astype(BF16)
            copies.append(put(send2.at[rows], far0.at[rows], far_id))
            if between:
                between[c]()
        return copies

    def summed(rows, near, far):
        near.wait_recv()
        far.wait_recv()
        return part0[rows, :] + near0[rows, :].astype(F32) + far0[rows, :].astype(F32)

    y_near = near_blocks(forward_block, y_sent)

    t_pass.wait_recv()
    t_last = put(tcf, tc3, near_id)
    t_near.wait_recv()
    t_far.wait_recv()
    t_row = lambda index: row(T_VECTORS + index)
    t_last.wait_recv()
    t_attn = None
    for j, (wide, last) in enumerate(zip((ta0, ta1, ta2, ta3), (tc_ref.at[0], tc1, tc2, tc3))):
        both = jnp.concatenate([wide[...], side_by_side(last[...])], axis=1)
        step = dot(both, tw_out(j))
        t_attn = step if t_attn is None else t_attn + step
    t_one, _, _ = norm_forward(x_ref[...].astype(F32) + t_attn + t_row(0), t_row(1), t_row(2))
    two[...] = t_one
    t_out[...] = t_one + t_row(3)
    half = hidden // 2
    t_in = t_one.astype(BF16)

    def teacher_packs(first, last):
        for index in range(first, last):
            slot = index % 2
            if index == 4:
                next_copies[0].wait_recv()
                next_copies[1].wait_recv()
                next_copies.append(put(next_b, next_d, near_id))
            if index == 6:
                next_copies[2].wait_recv()
                next_copies[3].wait_recv()
            if index + 1 < len(pack_refs):
                start_pack(index + 1)
            for copy in load_pack(index):
                copy.wait()
            upward = dot_cols(t_in, packs[slot, :half, :])
            upward = upward + packs[slot, hidden : hidden + 1, :half].astype(F32)
            act = (upward * normal_parts(upward)[0]).astype(BF16)
            t_out[...] += dot(act, packs[slot, half:hidden, :])

    middle_pack = len(pack_refs) // 2
    between = [
        functools.partial(teacher_packs, 0, middle_pack),
        functools.partial(teacher_packs, middle_pack, len(pack_refs)),
    ]
    y_far = far_blocks(y_all, forward_block, y_sent, between)
    t_out[...] = norm_forward(t_out[...], t_row(4), t_row(5))[0]

    g_sent = []
    earlier = list(started)
    started.clear()
    for rows, near, far in zip(chunks, y_near, y_far):
        ffn = summed(rows, near, far)
        out, n_two, inv_two = norm_forward(
            first[rows, :] + ffn + row(DOWN_BIAS), row(GAIN_2), row(SHIFT_2)
        )
        out_ref[rows, :] = out.astype(BF16)
        gap = out - t_out[rows, :]
        add_small(LOSS_ROW, gap * gap)
        add_small(GAIN_2, gap * n_two)
        add_small(SHIFT_2, gap)
        grad_two = norm_backward(gap, n_two, inv_two, row(GAIN_2))
        two[rows, :] = grad_two
        grad_ffn = grad_two.astype(BF16)
        add_small(DOWN_BIAS, grad_ffn.astype(F32))
        g_all[0, rows, :] = grad_ffn
        g_sent.append(share(g_all, rows))

    for copy in earlier:
        copy.wait_send()
    g_near = near_blocks(backward_block, g_sent)
    g_far = far_blocks(g_all, backward_block, g_sent)
    flat = lambda block: block[...].reshape(4 * own_rows, block.shape[2])

    def weight_gradients():
        ffn_ref[:width, :] = dot_rows(flat(y_all), flat(gu_all)).astype(BF16)
        ffn_ref[width:, :] = dot_rows(flat(hid), flat(g_all)).astype(BF16)
        sent, taken = [], 0
        for (low, count), order in zip(split_rows(0, width + hidden), dp_bits()):
            partner, digit = in_pair(place, order[0])
            count = count // 2
            give = ffn_ref.at[pl.ds(pl.multiple_of(low + (1 - digit) * count, 16), count)]
            keep = pl.multiple_of(low + digit * count, 16)
            land = ffn_land.at[taken : taken + count]
            sent.append((put(give, land, partner, "dp"), (keep, count)))
            taken += count
        return sent

    passes = []
    for c, (rows, near, far) in enumerate(zip(chunks, g_near, g_far)):
        y_one = first[rows, :]
        grad_one = two[rows, :] + summed(rows, near, far) * clip_slope(y_one)
        n_one = normed[rows, :]
        add_small(GAIN_1, grad_one * n_one)
        add_small(SHIFT_1, grad_one)
        grad_h = norm_backward(grad_one, n_one, inv[rows, :1], row(GAIN_1))
        gh_ref[rows, :] = grad_h
        grad_attn = grad_h.astype(BF16)
        add_small(OUT_BIAS, grad_attn.astype(F32))
        for j, ca in enumerate((ca0.at[rows], ca1.at[rows], ca2.at[rows], ca3.at[rows])):
            act = ca[...]
            level = act.astype(F32) * (1.0 / CLIP_RANGE)
            grad = dot_cols(grad_attn, w_out(j)) * (1.0 - level * level)
            grad = grad.astype(BF16)
            gs[j, c, :size, :] = grad[:, :LANES]
            gs[j, c, size:, :] = stacked(grad[:, LANES:])
            step = dot_rows(act, grad_attn)
            if c:
                step = step + part2[group(j), :]
            part2[group(j), :] = step
        passes.append(
            (
                put(gs.at[3, c], gr.at[3, c], far_id),
                put(gs.at[2, c], gr.at[1, c], far_id),
                put(gs.at[1, c], gr.at[0, c], near_id),
            )
        )
        if c == 0:
            halves = weight_gradients()
    g0_ref[...] = gs[0]
    for j in range(4):
        outg_ref[j] = part2[group(j), :].astype(BF16)
    lasts = []
    for c, (passing, _, _) in enumerate(passes):
        passing.wait_recv()
        lasts.append(put(gr.at[3, c], gr.at[2, c], near_id))
    for c, ((_, far, near), last) in enumerate(zip(passes, lasts)):
        near.wait_recv()
        g1_ref[c] = gr[0, c]
        far.wait_recv()
        g2_ref[c] = gr[1, c]
        last.wait_recv()
        g3_ref[c] = gr[2, c]
    taken = 0
    for copy, (keep, part_size) in halves:
        copy.wait_recv()
        land = slice(taken, taken + part_size)
        mine = ffn_ref[pl.ds(keep, part_size), :].astype(F32)
        kept_ref[land, :] = (mine + ffn_land[land, :].astype(F32)).astype(BF16)
        taken += part_size
    for copy in started:
        copy.wait_send()


def middle(x_own, cas, tcs, outs, w_up, s_down, vectors, packs, sums):
    own_rows, width = x_own.shape
    hidden = s_down.shape[0]
    head_cols = cas[0].shape[1]
    array = jax.ShapeDtypeStruct
    vmem = pl.BlockSpec(memory_space=pltpu.VMEM)
    transfers = 8 + 4 * 3 * CHUNKS + 4 * CHUNKS + 2
    packed = (CHUNKS, own_rows // CHUNKS * 3 // 2, LANES)
    four_outs = pltpu.VMEM((4, head_cols, width), BF16)
    square = lambda kind: pltpu.VMEM((own_rows, width), kind)
    four = lambda cols, kind: pltpu.VMEM((4, own_rows, cols), kind)
    return pl.pallas_call(
        middle_kernel,
        in_specs=[vmem] * 17 + [pl.BlockSpec(memory_space=pl.ANY)] * 6 + [vmem],
        out_specs=[vmem] * 9 + [pl.BlockSpec(memory_space=pl.ANY)] * 4,
        out_shape=[
            array((own_rows, width), BF16),
            array((own_rows, width), F32),
            array(((width + hidden) // 2, width), BF16),
            array((4, head_cols, width), BF16),
        ]
        + [array(packed, BF16)] * 4
        + [array((8, width), F32)]
        + [array(packs[2].shape, BF16)] * 4,
        scratch_shapes=[pltpu.VMEM(tcs[0].shape[1:], BF16)] * 4
        + [four(width, BF16), four(width, BF16), four(hidden, F32), four(hidden, BF16)]
        + [four(hidden, BF16)]
        + [square(F32)] * 4
        + [pltpu.VMEM((own_rows, LANES), F32)]
        + [square(F32), pltpu.VMEM((4 * max(own_rows // 4, head_cols), width), F32)]
        + [square(BF16)] * 6
        + [pltpu.VMEM((4,) + packed, BF16)] * 2
        + [
            pltpu.VMEM(packs[0].shape, BF16),
            pltpu.VMEM((width + hidden, width), BF16),
            pltpu.VMEM(((width + hidden) // 2, width), BF16),
            four_outs,
            pltpu.VMEM(s_down.shape, BF16),
            pltpu.SemaphoreType.DMA((transfers,)),
            pltpu.SemaphoreType.DMA((transfers,)),
            pltpu.SemaphoreType.DMA((4,)),
        ],
        compiler_params=pltpu.CompilerParams(
            collective_id=3, has_side_effects=True, vmem_limit_bytes=62 * 2**20
        ),
        cost_estimate=pl.CostEstimate(
            flops=120 * own_rows * width * hidden, bytes_accessed=2**25, transcendentals=2**22
        ),
        name="middle",
    )(x_own, *cas, *tcs, *outs, w_up, s_down, vectors, *packs, sums)


def projection(weight, bias):
    rows = jnp.stack([bias[0], jnp.zeros_like(bias[0]), bias[1]]).astype(F32)
    return weight.transpose(1, 0, 2), jnp.pad(rows, ((0, 5), (0, 0)))


def body(
    tokens,
    seg_lengths,
    parents,
    qkv_latent,
    qv_bias,
    out_latent,
    out_bias,
    norm1_gain,
    norm1_shift,
    up_latent,
    up_bias,
    down_latent,
    down_bias,
    norm2_gain,
    norm2_shift,
    teacher_qkv,
    teacher_qv_bias,
    teacher_out,
    teacher_out_bias,
    teacher_norm1_gain,
    teacher_norm1_shift,
    teacher_up,
    teacher_up_bias,
    teacher_down,
    teacher_down_bias,
    teacher_norm2_gain,
    teacher_norm2_shift,
):
    own_rows, model_width = tokens.shape
    group = lax.axis_size("tensor")
    me = lax.axis_index("tensor")
    all_rows = own_rows * group
    local_cols = qkv_latent.shape[2]
    local_heads = local_cols // HEAD_DIM
    near_x = swap(tokens, 1)
    far_x = swap(tokens, 2)
    blocks = [tokens, near_x, far_x, swap(far_x, 1)]
    latents = [out_latent, teacher_out, up_latent, down_latent]
    latents += [teacher_up, teacher_down, teacher_up_bias]
    vectors = [out_bias, norm1_gain, norm1_shift, down_bias, norm2_gain, norm2_shift, up_bias]
    vectors += [teacher_out_bias, teacher_norm1_gain, teacher_norm1_shift]
    vectors += [teacher_down_bias, teacher_norm2_gain, teacher_norm2_shift]
    outs, w_up, s_down, pack, sums, vectors = prepare(latents, vectors)
    w_qkv = (jnp.mean(jnp.abs(qkv_latent), axis=0) * jnp.sign(qkv_latent)).astype(BF16)
    seg_lanes, blocked = segment_tables(seg_lengths[0], parents[0])
    base = jnp.stack([(me ^ j) * own_rows for j in range(group)]).astype(jnp.int32)

    w_three, b_three = projection(w_qkv, qv_bias)
    tables = (seg_lanes, blocked)
    *qkv, context, x_in_all, ca_own, ca_near, ca_far, sums, pack_near, piece_a, outs1, outs2 = attend_forward(
        base, blocks, w_three, b_three, *tables, [pack, outs, sums], True
    )
    t_last, ta0, ca1, ca2, _, ca3, ta1, ta2, _, ta3, outs3, next_a, piece_b, piece_c = attend_forward(
        base, blocks, *projection(teacher_qkv, teacher_qv_bias), *tables,
        [ca_near, ca_far, outs2, piece_a], False,
    )
    cas, outs = [ca_own, ca1, ca2, ca3], [outs, outs1, outs2, outs3]
    packs = [pack, pack_near, piece_a, piece_b, piece_c, next_a]
    out_own, grad_h, ffn_grads, out_grads, g0, g1, g2, g3, small, *_ = middle(
        tokens, cas, [t_last, ta0, ta1, ta2, ta3], outs, w_up, s_down, vectors, packs, sums
    )
    ffn_grads, late, small, gx_own, gx_far = attend_backward(
        qkv, context, x_in_all, w_three, [g0, g1, g2, g3], ffn_grads, out_grads, small
    )
    grad_x_in = gx_own + gx_far.astype(F32)
    input_grad = grad_h + grad_x_in * clip_slope(tokens.astype(F32))
    ffn_grads = ffn_grads.astype(F32)
    tree_loss = jnp.sum(small[LOSS_ROW])[None] / (all_rows * model_width)
    proj_bias_grad = small[8 : 8 + local_heads, : 3 * LANES].reshape(local_heads, 3, LANES)
    proj_bias_grad = proj_bias_grad[:, :, :HEAD_DIM].transpose(1, 0, 2).reshape(3, local_cols)
    proj_bias_grad = jnp.stack([proj_bias_grad[0] * 0.125, proj_bias_grad[2]])
    late = late.astype(F32)
    qkv_grad = jnp.concatenate([late[:local_cols], late[2 * local_cols :]])
    qkv_grad = qkv_grad.reshape(local_heads, 3, HEAD_DIM, model_width)
    qkv_grad = qkv_grad.transpose(3, 1, 0, 2).reshape(model_width, 3, local_cols)
    return (
        out_own,
        tree_loss,
        input_grad,
        qkv_grad,
        proj_bias_grad,
        late[local_cols : 2 * local_cols],
        small[0],
        small[1],
        small[2],
        ffn_grads[:model_width],
        small[7],
        ffn_grads[model_width:],
        small[3],
        small[4],
        small[5],
    )


def solution(mesh):
    rows, cols = ("dp", "tensor"), "tensor"
    vec = P()
    params = (
        P(None, None, cols),
        P(None, cols),
        P(cols, None),
        vec,
        vec,
        vec,
        P(None, cols),
        P(cols),
        P(cols, None),
        vec,
        vec,
        vec,
    )
    in_specs = (P(rows, None), P("dp", None), P("dp", None)) + params + params
    out_specs = (P(rows, None), P("dp"), P(rows, None)) + params
    return jax.shard_map(body, mesh=mesh, in_specs=in_specs, out_specs=out_specs, check_vma=False)
```

```python
import functools

import jax
import jax.numpy as jnp
from jax import lax
from jax.experimental import pallas as pl
from jax.experimental.pallas import tpu as pltpu
from jax.sharding import PartitionSpec as P

HEAD_DIM = 64
LANES = 128
CLIP_RANGE = 3.0
NORM_EPSILON = 1e-05
MASKED_SCORE = -1e30
SEG_LANE = HEAD_DIM
ROW_TERM = HEAD_DIM + 16
Q_BLOCK = 256
PACK_PAD = 32
CHUNKS = 2
BF16, F32 = jnp.bfloat16, jnp.float32
ROWS_ROWS = (((0,), (0,)), ((), ()))
COLS_COLS = (((1,), (1,)), ((), ()))


def clip_act(values):
    return CLIP_RANGE * jnp.tanh(values / CLIP_RANGE)


def clip_slope(values):
    level = jnp.tanh(values / CLIP_RANGE)
    return 1.0 - level * level


def normal_parts(values):
    bell = jnp.exp(-0.5 * values * values)
    step = 1.0 / (1.0 + 0.23164188843 * jnp.abs(values))
    series = 0.5307027145 * step - 0.7265760135
    series = series * step + 0.7107068705
    series = series * step - 0.142248368
    series = series * step + 0.127414796
    tail = series * step * bell
    return jnp.where(values >= 0.0, 1.0 - tail, tail), bell


def norm_forward(hidden, gain, shift):
    row_mean = jnp.mean(hidden, axis=-1, keepdims=True)
    centred = hidden - row_mean
    inv_std = lax.rsqrt(jnp.mean(centred * centred, axis=-1, keepdims=True) + NORM_EPSILON)
    normed = centred * inv_std
    return (normed * gain + shift, normed, inv_std)


def norm_backward(grad_out, normed, inv_std, gain):
    grad_normed = grad_out * gain
    centre = jnp.mean(grad_normed, axis=-1, keepdims=True)
    inner_sum = jnp.mean(grad_normed * normed, axis=-1, keepdims=True)
    return inv_std * (grad_normed - centre - normed * inner_sum)


def dot(left, right):
    return jnp.dot(left, right, preferred_element_type=F32)


def dot_rows(left, right):
    return lax.dot_general(left, right, ROWS_ROWS, preferred_element_type=F32)


def dot_cols(left, right):
    return lax.dot_general(left, right, COLS_COLS, preferred_element_type=F32)


def swap(array, bit):
    size = lax.axis_size("tensor")
    return lax.ppermute(array, "tensor", [(i, i ^ bit) for i in range(size)])


def lookup(indices, lookup_table):
    labels = jnp.arange(lookup_table.shape[0], dtype=jnp.int32)
    picked = jnp.where(indices[:, None] == labels[None, :], lookup_table[None, :], 0)
    return jnp.sum(picked, axis=1)


def segment_tables(lengths, parent):
    count = lengths.shape[0]
    labels = jnp.arange(count, dtype=jnp.int32)
    row, col = labels[:, None], labels[None, :]
    starts = jnp.sum(jnp.where(col < row, lengths[None, :], 0), axis=1)
    two = lookup(parent, parent)
    allowed = (col == row) | (col == parent[:, None]) | (col == two[:, None])
    allowed = allowed | (parent[None, :] == row) | (two[None, :] == row)
    after = LANES - SEG_LANE - count
    lanes = jnp.pad(jnp.stack([starts, starts + lengths]), ((0, 6), (SEG_LANE, after)))
    blocked = jnp.pad((~allowed).astype(BF16), ((SEG_LANE, after), (SEG_LANE, after)))
    return lanes, blocked


def split_three(values):
    first = values.astype(BF16).astype(F32)
    second = (values - first).astype(BF16).astype(F32)
    return first, second, values - first - second


def sign_of(values):
    return jnp.where(values > 0.0, 1.0, jnp.where(values < 0.0, -1.0, 0.0))


def prepare_kernel(
    qkv_ref, out_ref, t_out_ref, up_ref, down_ref, t_up_ref, t_down_ref, t_bias_ref, *rest
):
    *vectors, w_qkv_ref, outs_ref, w_up_ref, s_down_ref, pack_ref, sums_ref, vec_ref = rest
    vec_ref[...] = jnp.zeros_like(vec_ref)
    for index, vector in enumerate(vectors):
        vec_ref[index : index + 1, :] = vector[...].astype(F32).reshape(1, -1)
    hidden, width = down_ref.shape
    half = hidden // 2
    rows = out_ref.shape[0]
    for c in range(3):
        latent = qkv_ref[c]
        scale = jnp.sum(jnp.abs(latent), axis=1, keepdims=True) * (1.0 / width)
        w_qkv_ref[c] = (scale * sign_of(latent)).astype(BF16)
    total = lambda ref: jnp.sum(jnp.abs(ref[...]), axis=0, keepdims=True)
    sums_ref[...] = jnp.zeros_like(sums_ref)
    sums_ref[0:1, :] = total(out_ref)
    sums_ref[1:2, :] = total(down_ref)
    outs_ref[:rows, :] = sign_of(out_ref[...]).astype(BF16)
    outs_ref[rows:, :] = t_out_ref[...]
    w_up_ref[...] = (total(up_ref) * (1.0 / width) * sign_of(up_ref[...])).astype(BF16)
    s_down_ref[...] = sign_of(down_ref[...]).astype(BF16)
    up_t = t_up_ref[...].T
    pack_ref[:, hidden:, :] = jnp.zeros((2, PACK_PAD, width), BF16)
    for side in range(2):
        cols = slice(side * half, (side + 1) * half)
        pack_ref[side, :half, :] = up_t[cols]
        pack_ref[side, half:hidden, :] = t_down_ref[cols, :]
        bias = t_bias_ref[cols].astype(F32).reshape(1, -1)
        pack_ref[side, hidden : hidden + 1, :half] = bias.astype(BF16)


def prepare(latents, vectors):
    array = jax.ShapeDtypeStruct
    qkv_latent, out_latent, _, up_latent, down_latent, *_ = latents
    hidden, width = down_latent.shape
    return pl.pallas_call(
        prepare_kernel,
        out_shape=[
            array(qkv_latent.shape, BF16),
            array((2 * out_latent.shape[0], width), BF16),
            array(up_latent.shape, BF16),
            array(down_latent.shape, BF16),
            array((2, hidden + PACK_PAD, width), BF16),
            array((8, width), F32),
            array((16, width), F32),
        ],
        compiler_params=pltpu.CompilerParams(vmem_limit_bytes=58 * 2**20),
        cost_estimate=pl.CostEstimate(
            flops=16 * 10**9, bytes_accessed=24 * width * hidden, transcendentals=0
        ),
        name="prepare",
    )(*latents, *vectors)


def in_lane(shape, axis, terms):
    lane = lax.broadcasted_iota(jnp.int32, shape, axis)
    spread = jnp.zeros(shape, F32)
    for offset, term in enumerate(terms):
        spread = jnp.where(lane == ROW_TERM + offset, term, spread)
    return spread


def make_copies(send_sem, recv_sem):
    count = [0]

    def copy_to(source, target, axis, device):
        index = count[0]
        count[0] += 1

        def make():
            return pltpu.make_async_remote_copy(
                src_ref=source,
                dst_ref=target,
                send_sem=send_sem.at[index],
                recv_sem=recv_sem.at[index],
                device_id={axis: device},
                device_id_type=pl.DeviceIdType.MESH,
            )

        return make

    return copy_to


def greet(others):
    barrier = pltpu.get_barrier_semaphore()
    for other in others:
        pl.semaphore_signal(barrier, inc=1, device_id=other, device_id_type=pl.DeviceIdType.MESH)
    pl.semaphore_wait(barrier, len(others))


def neighbours():
    me = lax.axis_index("tensor")
    return me + 1 - 2 * lax.rem(me, 2), lax.rem(me + 2, lax.axis_size("tensor"))


def forward_kernel(base_ref, x0, x1, x2, w_ref, b_ref, seg_ref, blocked_ref, *rest, student):
    if student:
        pack_ref, outs, sums_ref, *rest = rest
        q_ref, k_ref, v_ref, ctx_ref, source, own, near, far, *rest = rest
        sums_out, pack_near, piece_a, outs1, outs2, sums, *rest = rest
    else:
        ca_near, ca_far, outs2, piece_a, *rest = rest
        sent, ta0, ca1, ca2, ca_pass, ca3, ta1, ta2, ta_pass, ta3, *rest = rest
        outs3, next_a, piece_b, piece_c, source, send_a, *rest = rest
    x3, joined, queries, keys, vals_t, send_sem, recv_sem = rest
    blocks = (x0, x1, x2, x3)
    own_rows = x0.shape[0]
    rows = own_rows * len(blocks)
    heads = joined.shape[0]
    head = pl.program_id(0)
    near_id, far_id = neighbours()
    place = lax.axis_index("dp")
    copy_to = make_copies(send_sem, recv_sem)
    side_id, side = in_pair(place, 1)
    next_id, level = in_pair(place, 2)
    others = [{"tensor": near_id}, {"tensor": far_id}, {"dp": side_id}]
    if not student:
        others.append({"dp": next_id})
    if student:
        size = piece_a.shape[0]
        quarter = pack_ref.at[side, pl.ds(pl.multiple_of(level * size, 16), size)]
        half = outs.shape[0] // 2
        rows_of = pl.ds(pl.multiple_of(side * half, 16), half)
        outs_far = copy_to(outs.at[rows_of], outs2.at[rows_of], "tensor", far_id)
        pack_far = copy_to(quarter, piece_a, "tensor", far_id)
        sum_near = copy_to(sums.at[0], sums.at[1], "tensor", near_id)
        sum_far = copy_to(sums.at[2], sums.at[3], "tensor", far_id)
        stages = [
            (
                [],
                [
                    sum_near,
                    outs_far,
                    copy_to(outs, outs1, "tensor", near_id),
                    copy_to(pack_ref, pack_near, "tensor", near_id),
                ],
            ),
            ([outs_far], [pack_far, copy_to(outs2.at[rows_of], outs2.at[rows_of], "dp", side_id)]),
            ([], []),
        ]
    else:
        passing = copy_to(ca_far.at[1], ca_pass, "tensor", far_id)
        stages = [
            (
                [],
                [
                    passing,
                    copy_to(ca_far.at[0], ca2, "tensor", far_id),
                    copy_to(ca_near, ca1, "tensor", near_id),
                    copy_to(outs2, outs3, "tensor", near_id),
                    copy_to(piece_a, next_a, "dp", next_id),
                    copy_to(piece_a, piece_c, "tensor", near_id),
                    copy_to(piece_a, piece_b, "dp", side_id),
                ],
            ),
            ([], []),
            ([passing], [copy_to(ca_pass, ca3, "tensor", near_id)]),
        ]
        a_passing = copy_to(send_a.at[3], ta_pass, "tensor", far_id)
        a_copies = [
            a_passing,
            copy_to(send_a.at[2], ta2, "tensor", far_id),
            copy_to(send_a.at[1], ta1, "tensor", near_id),
        ]
        a_last = copy_to(ta_pass, ta3, "tensor", near_id)

    last_block = copy_to(x2, x3, "tensor", near_id)

    def run_stage(index):
        before, copies = stages[index]
        for copy in before:
            copy().wait_recv()
        for copy in copies:
            copy().start()

    @pl.when(head == 0)
    def _():
        if student:
            sums[0] = sums_ref[...]
        greet(others)
        last_block().start()
        run_stage(0)
        lane = lax.broadcasted_iota(jnp.int32, (own_rows, LANES), 1)
        ones = (lane >= ROW_TERM) & (lane < ROW_TERM + 3)
        for j, block in enumerate(blocks):
            if j == 3:
                last_block().wait()
            part = slice(j * own_rows, (j + 1) * own_rows)
            if student:
                source[part, :] = clip_act(block[...].astype(F32)).astype(BF16)
            else:
                source[part, :] = block[...]
            spot = lax.broadcasted_iota(jnp.int32, (own_rows, LANES), 0) + base_ref[j]
            inside = (spot >= seg_ref[0:1, :]) & (spot < seg_ref[1:2, :])
            links = dot(jnp.where(inside, 1.0, 0.0).astype(BF16), blocked_ref[...])
            extras = (
                jnp.where(inside, MASKED_SCORE, 0.0).astype(BF16),
                jnp.where(ones, 1.0, links).astype(BF16),
                jnp.where(ones, 1.0, 0.0).astype(BF16),
            )
            for c, (scale, extra) in enumerate(zip((0.125, 1.0, 1.0), extras)):
                proj = dot_cols(source[part, :], w_ref[c])
                if c != 1:
                    proj = proj + b_ref[c // 2 : c // 2 + 1, :].astype(F32)
                proj = proj.astype(BF16)
                for h in range(heads):
                    one = proj[:, h * HEAD_DIM : (h + 1) * HEAD_DIM] * scale
                    wide = jnp.concatenate([one, jnp.zeros_like(one)], axis=1) + extra
                    if c == 0:
                        queries[h, part, :] = wide
                    elif c == 1:
                        keys[h, part, :] = wide
                    else:
                        vals_t[h, :, part] = wide.T
                        if student:
                            v_ref[h, part, :] = wide

    if student:
        k_ref[0] = keys[head]
    else:

        @pl.when(head == heads - 1)
        def _():
            for j in range(len(blocks)):
                part = slice(j * own_rows, (j + 1) * own_rows)
                pair = jnp.concatenate([joined[0, part, :], joined[1, part, :]], axis=1)
                send_a[j] = pair.astype(BF16)
            for copy in a_copies:
                copy().start()

    scores = {}
    for index in range(rows // Q_BLOCK):
        if index % (rows // Q_BLOCK // 2) == 0:
            if index:

                @pl.when(head == 0)
                def _():
                    run_stage(1)

                @pl.when(head == 1)
                def _():
                    run_stage(2)
                    if student:
                        sum_near().wait_recv()
                        sums[2] = sums[0] + sums[1]
                        sum_far().start()

            for later in range(index, index + rows // Q_BLOCK // 2):
                start = later * Q_BLOCK
                scores[later] = dot_cols(keys[head], queries[head, start : start + Q_BLOCK, :])
        block = scores[index]
        part = slice(index * Q_BLOCK, (index + 1) * Q_BLOCK)
        peak = jnp.max(block, axis=0, keepdims=True)
        raised = jnp.exp(block - peak)
        total = jnp.sum(raised, axis=0, keepdims=True)
        weights = (raised * (1.0 / total)).astype(BF16)
        context = dot(vals_t[head], weights)[:HEAD_DIM].T
        joined[head, part, :] = context
        if student:
            ctx_ref[0, part, :] = context
            terms = split_three(-(peak + jnp.log(total)))
            spread = in_lane((LANES, Q_BLOCK), 0, terms)
            q_ref[0, part, :] = queries[head, part, :] + spread.T.astype(BF16)

    @pl.when(head == heads - 1)
    def _():
        for j in range(len(blocks)):
            part = slice(j * own_rows, (j + 1) * own_rows)
            if not student:
                sent[j] = stacked(joined[heads - 1, part, :]).astype(BF16)
                continue
            block = jnp.concatenate([joined[h, part, :] for h in range(heads)], axis=1)
            if j < 2:
                (own, near)[j][...] = clip_act(block).astype(BF16)
            else:
                far[j - 2] = clip_act(block).astype(BF16)
        waited = [copy for before, _ in stages for copy in before]
        if not student:
            ta0[...] = send_a[0]
            a_passing().wait_recv()
            a_last().start()
            for copy in a_copies:
                copy().wait_send()
            for copy in a_copies[1:] + [a_last]:
                copy().wait_recv()
            a_last().wait_send()
        if student:
            sum_far().wait_recv()
            sums_out[...] = sums[2] + sums[3]
            sum_far().wait_send()
            waited.append(sum_near)
        for _, copies in stages:
            for copy in copies:
                copy().wait_send()
                if copy not in waited:
                    copy().wait_recv()


def attend_forward(base, blocks, weight, bias, seg_lanes, blocked, moved, student):
    own_rows, width = blocks[0].shape
    group = len(blocks) + 1
    rows = own_rows * group
    head_cols = weight.shape[1]
    heads = head_cols // HEAD_DIM
    whole = lambda *shape: pl.BlockSpec(shape, lambda h: (0,) * len(shape))
    anywhere = pl.BlockSpec(memory_space=pl.ANY)
    array = jax.ShapeDtypeStruct
    per_head = lambda cols: pl.BlockSpec((1, rows, cols), lambda h: (h, 0, 0))
    if student:
        pack, out_weights, sums = moved
        piece = (pack.shape[1] // 2, width)
        outs = [
            (per_head(LANES), array((heads, rows, LANES), BF16)),
            (per_head(LANES), array((heads, rows, LANES), BF16)),
            (whole(heads, rows, LANES), array((heads, rows, LANES), BF16)),
            (per_head(HEAD_DIM), array((heads, rows, HEAD_DIM), F32)),
            (whole(rows, width), array((rows, width), BF16)),
            (whole(own_rows, head_cols), array((own_rows, head_cols), BF16)),
            (whole(own_rows, head_cols), array((own_rows, head_cols), BF16)),
            (whole(2, own_rows, head_cols), array((2, own_rows, head_cols), BF16)),
            (whole(*sums.shape), array(sums.shape, F32)),
            (anywhere, array(pack.shape, BF16)),
        ]
        outs += [(anywhere, array(piece, BF16))]
        outs += [(anywhere, array(out_weights.shape, BF16))] * 2
        scratch, transfers = [pltpu.VMEM((4,) + sums.shape, F32)], 8
    else:
        ca_near, ca_far, out_weights, piece = moved
        last = (group, own_rows // 2, LANES)
        pair = array((own_rows, LANES), BF16)
        outs = [(whole(*last), array(last, BF16)), (whole(*pair.shape), pair)]
        outs += [(anywhere, array(ca_near.shape, BF16))] * 4 + [(anywhere, pair)] * 4
        outs += [(anywhere, array(out_weights.shape, BF16))]
        outs += [(anywhere, array(piece.shape, BF16))] * 3
        scratch, transfers = [pltpu.VMEM((rows, width), BF16)], 13
        scratch.append(pltpu.VMEM((group,) + pair.shape, BF16))
    scratch += [
        pltpu.VMEM((own_rows, width), BF16),
        pltpu.VMEM((heads, rows, HEAD_DIM), F32),
        pltpu.VMEM((heads, rows, LANES), BF16),
        pltpu.VMEM((heads, rows, LANES), BF16),
        pltpu.VMEM((heads, LANES, rows), BF16),
        pltpu.SemaphoreType.DMA((transfers,)),
        pltpu.SemaphoreType.DMA((transfers,)),
    ]
    return pl.pallas_call(
        functools.partial(forward_kernel, student=student),
        grid=(heads,),
        in_specs=[pl.BlockSpec(memory_space=pltpu.SMEM)]
        + [whole(own_rows, width)] * 3
        + [whole(*a.shape) for a in (weight, bias, seg_lanes, blocked)]
        + [whole(*a.shape) if a.dtype == F32 else anywhere for a in moved],
        out_specs=[spec for spec, _ in outs],
        out_shape=[shape for _, shape in outs],
        scratch_shapes=scratch,
        compiler_params=pltpu.CompilerParams(
            collective_id=1 if student else 2, has_side_effects=True, vmem_limit_bytes=58 * 2**20
        ),
        cost_estimate=pl.CostEstimate(
            flops=16 * heads * rows * rows * HEAD_DIM,
            bytes_accessed=2 * rows * (width + 6 * heads * LANES),
            transcendentals=heads * rows * rows,
        ),
        name="student_attention" if student else "teacher_attention",
    )(base, *blocks, weight, bias, seg_lanes, blocked, *moved)


def in_pair(place, bit):
    digit = lax.rem(lax.div(place, bit), 2)
    return place + bit - 2 * bit * digit, digit


def halving_steps(partial, total, landing, rows, landing_row, order, place, copy_of, done=0, base=None):
    low, size = rows
    here = low if base is None else base
    steps, levels, used = [], [], landing_row
    for level, bit in enumerate(order):
        partner, digit = in_pair(place, bit)
        halved = size % 32 == 0
        count = size // 2 if halved else size
        low = pl.multiple_of(low + digit * count, 16) if halved else low
        if level >= done:
            give = pl.multiple_of(here + (1 - digit) * count, 16) if halved else here
            here = pl.multiple_of(here + digit * count, 16) if halved else here
            copy = copy_of(partial.at[pl.ds(give, count)], landing.at[pl.ds(used, count)], partner)
            last = level == len(order) - 1

            def add(used=used, here=here, count=count, out=total if last else partial, at=low if last else here):
                arrived = landing[used : used + count, :].astype(F32)
                mine = partial[pl.ds(here, count), :].astype(F32)
                out[pl.ds(at, count), :] = (mine + arrived).astype(out.dtype)

            steps.append((copy, add))
            used += count
        if halved:
            levels.append((count, low, partner))
        size = count
    for count, keep, partner in reversed(levels):
        where = total.at[pl.ds(keep, count)]
        steps.append((copy_of(where, where, partner), lambda: None))
    return steps, used


def run_step(plans, index):
    for steps in plans:
        if 0 < index <= len(steps):
            copy, after = steps[index - 1]
            copy().wait()
            after()
        if index < len(steps):
            steps[index][0]().start()


def split_rows(first, count):
    small = count // 2 if count % 512 == 0 else -(-count // 3 // 64) * 64
    return ((first, count - small), (first + count - small, small))


def dp_bits():
    bits = [1 << i for i in range((lax.axis_size("dp") - 1).bit_length())]
    return bits, (bits[1:2] + bits[:1] + bits[2:])


def backward_kernel(
    q_ref, k_ref, v_ref, ctx_ref, x_ref, w_ref, g0, g1, g2, g3, ffn_ref, outg_ref, small_ref,
    ffn_out, late_out, small_out, gx_out, gxfar_out,
    grads, wide, packed, keys_t, total, ffn_part, ffn, late_in, late, small, small_in, landing, small_land,
    out_near, out_near_land, out_far, out_far_land, gx_near, gx_near_land, gx_far, gx_far_land,
    send_sem, recv_sem, write_sem, *, key_block,
):
    blocks = (g0, g1, g2, g3)
    rows = x_ref.shape[0]
    own_rows = rows // len(blocks)
    heads = grads.shape[0]
    head_cols = heads * HEAD_DIM
    head = pl.program_id(0)
    place = lax.axis_index("dp")
    near_id, far_id = neighbours()
    part = lambda j: slice(j * own_rows, (j + 1) * own_rows)
    bits, turned = dp_bits()

    copy_to = make_copies(send_sem, recv_sem)
    over_dp = lambda source, target, other: copy_to(source, target, "dp", other)
    over_tensor = lambda source, target, other: copy_to(source, target, "tensor", other)

    used = [0]

    def reduced(partial, target, first, size, done=0):
        plans, taken = [], 0
        for rows_of, order in zip(split_rows(first, size), (bits, turned)):
            steps, used[0] = halving_steps(
                partial, target, landing, rows_of, used[0], order, place, over_dp, done,
                taken if done else None,
            )
            plans.append(steps)
            taken += rows_of[1] >> done
        return plans

    width = x_ref.shape[1]
    ffn_plans = reduced(ffn_part, ffn, 0, ffn.shape[0], 1)
    early_plans = reduced(late_in, late, 0, 2 * head_cols)
    middle_plans = reduced(late_in, late, 2 * head_cols, head_cols)
    last_plans = reduced(late_in, late, 3 * head_cols, head_cols)
    small_steps = []
    for level, bit in enumerate(bits):
        partner, _ = in_pair(place, bit)
        small_steps.append(over_dp(small_in.at[level], small_land.at[level], partner))
    tensor_small = [
        over_tensor(small.at[0], small.at[1], near_id),
        over_tensor(small.at[2], small.at[3], far_id),
    ]
    out_steps = [
        over_tensor(out_near, out_near_land, near_id),
        over_tensor(out_far, out_far_land, far_id),
    ]
    gx_steps = [
        over_tensor(gx_near.at[1], gx_near_land.at[1], near_id),
        over_tensor(gx_near.at[0], gx_near_land.at[0], near_id),
        over_tensor(gx_far, gx_far_land, far_id),
    ]

    @pl.when(head == 0)
    def _():
        others = [{"tensor": near_id}, {"tensor": far_id}]
        greet(others + [{"dp": in_pair(place, bit)[0]} for bit in bits])
        ffn_part[...] = ffn_ref[...]
        run_step(ffn_plans, 0)
        out_near[0] = outg_ref[1]
        out_near[1] = outg_ref[3]
        out_steps[0]().start()
        small[0] = small_ref[...]
        tensor_small[0]().start()
        size = own_rows // CHUNKS
        for j, block in enumerate(blocks):
            for c in range(CHUNKS):
                where = slice(j * own_rows + c * size, j * own_rows + (c + 1) * size)
                pair = block[c, :size, :]
                ones = [pair[:, :HEAD_DIM], pair[:, HEAD_DIM:], side_by_side(block[c, size:, :])]
                for h, one in enumerate(ones):
                    grads[h, where, :] = jnp.concatenate([one, jnp.zeros_like(one)], axis=1)
        packed[...] = jnp.zeros_like(packed)
        wide[...] = jnp.zeros_like(wide)
        for h in range(heads):
            for c, scale in enumerate((0.125, 1.0, 1.0)):
                one = w_ref[c, h * HEAD_DIM : (h + 1) * HEAD_DIM, :] * scale
                wide[h, c * LANES : c * LANES + HEAD_DIM, :] = one

    queries = q_ref[0]
    slopes = grads[head]
    inner = -jnp.sum(slopes[:, :HEAD_DIM].astype(F32) * ctx_ref[0], axis=1, keepdims=True)
    slopes = slopes + in_lane((rows, LANES), 1, split_three(inner)).astype(BF16)
    keys_t[...] = k_ref[0].T

    def over_keys(first, last, query_grad):
        for start in range(first, last, key_block):
            span = slice(start, start + key_block)
            weights = jnp.exp(dot_cols(k_ref[0, span, :], queries))
            grad_weights = dot_cols(v_ref[0, span, :], slopes)
            grad_scores = (weights * grad_weights).astype(BF16)
            step = dot(keys_t[:, span], grad_scores)
            query_grad = step if query_grad is None else query_grad + step
            key_grad = dot(grad_scores, queries)[:, :HEAD_DIM]
            packed[span, LANES : LANES + HEAD_DIM] = key_grad.astype(BF16)
            value_grad = dot(weights.astype(BF16), slopes)[:, :HEAD_DIM]
            packed[span, 2 * LANES : 2 * LANES + HEAD_DIM] = value_grad.astype(BF16)
        return query_grad

    def at(which):
        return pl.when(head == which)

    quarter = rows // 4
    query_grad = over_keys(0, quarter, None)

    @at(1)
    def _():
        run_step(ffn_plans, 2)

    query_grad = over_keys(quarter, 2 * quarter, query_grad)

    @at(0)
    def _():
        run_step(ffn_plans, 1)
        out_steps[0]().wait_recv()
        out_far[...] = (outg_ref[2].astype(F32) + out_near_land[1].astype(F32)).astype(BF16)
        out_steps[1]().start()
        tensor_small[0]().wait_recv()
        small[2] = small[0] + small[1]
        tensor_small[1]().start()

    @at(1)
    def _():
        run_step(early_plans, 1)

    @at(2)
    def _():
        run_step(ffn_plans, 4)
        run_step(early_plans, 3)
        run_step(middle_plans, 1)

    query_grad = over_keys(2 * quarter, rows, query_grad)
    packed[:, :HEAD_DIM] = query_grad[:HEAD_DIM].T.astype(BF16)
    sums = jnp.sum(packed[...].astype(F32), axis=0, keepdims=True)
    small[4 + head, 0:1, : 3 * LANES] = sums
    weight_grad = dot_rows(packed[...], x_ref[...])
    slot = jnp.where(head == 0, 0, head_cols + head * head_cols)
    for c, factor in enumerate((0.125, 1.0, 1.0)):
        target = pl.multiple_of(slot + c * HEAD_DIM, HEAD_DIM)
        late_in[pl.ds(target, HEAD_DIM), :] = (
            weight_grad[c * LANES : c * LANES + HEAD_DIM] * factor
        ).astype(BF16)

    @pl.when(head == 0)
    def _():
        out_steps[1]().wait_recv()
        late_in[head_cols : 2 * head_cols, :] = (
            outg_ref[0].astype(F32)
            + out_near_land[0].astype(F32)
            + out_far_land[...].astype(F32)
        ).astype(BF16)
        tensor_small[1]().wait_recv()
        run_step(early_plans, 0)

    @pl.when(head == 1)
    def _():
        run_step(middle_plans, 0)
        run_step(ffn_plans, 3)
        run_step(early_plans, 2)

    @pl.when(head == 2)
    def _():
        run_step(last_plans, 0)
        small_in[0, :8, :] = small[2] + small[3]
        small_in[0, UP_ROW : UP_ROW + 1, :] = small_ref[UP_ROW : UP_ROW + 1, :]
        small_in[0, 8:, :] = jnp.zeros((8, width), F32)
        for h in range(heads):
            small_in[0, 8 + h : 9 + h, : 3 * LANES] = small[4 + h, 0:1, : 3 * LANES]
        small_steps[0]().start()

    for j in (3, 2, 1, 0):
        step = dot(packed[part(j), :], wide[head])
        total[part(j), :] = jnp.where(head == 0, step, total[part(j), :] + step)
        if j % 2:

            @pl.when(head == heads - 1)
            def _(j=j):
                gx_near[j // 2] = total[part(j), :].astype(BF16)
                gx_steps[1 - j // 2]().start()

    @pl.when(head == heads - 1)
    def _():
        run_step(last_plans, 1)
        gx_steps[0]().wait_recv()
        gx_far[...] = (total[part(2), :] + gx_near_land[1].astype(F32)).astype(BF16)
        gx_steps[2]().start()
        gx_steps[1]().wait_recv()
        total[part(0), :] = total[part(0), :] + gx_near_land[0].astype(F32)
        gx_write = pltpu.make_async_copy(total.at[part(0)], gx_out, write_sem.at[0])
        gx_write.start()
        run_step(early_plans, 4)
        run_step(middle_plans, 2)
        for index in range(1, 2 * len(bits) + 1):
            if index > 1:
                run_step(last_plans, index)
            if index <= len(bits):
                small_steps[index - 1]().wait_recv()
                arrived = small_in[index - 1] + small_land[index - 1]
                if index < len(bits):
                    small_in[index] = arrived
                    small_steps[index]().start()
                else:
                    small_out[...] = arrived
            run_step(middle_plans, 2 + index)
            run_step(early_plans, 4 + index)
        for index in range(5, 2 * len(bits) + 1):
            run_step(ffn_plans, index)
        ffn_write = pltpu.make_async_copy(ffn, ffn_out, write_sem.at[1])
        ffn_write.start()
        late_write = pltpu.make_async_copy(late, late_out, write_sem.at[2])
        late_write.start()
        gx_steps[2]().wait_recv()
        far_write = pltpu.make_async_copy(gx_far_land, gxfar_out, write_sem.at[3])
        far_write.start()
        shared = small[2, LOSS_ROW : LOSS_ROW + 1, :] + small[3, LOSS_ROW : LOSS_ROW + 1, :]
        small_out[LOSS_ROW : LOSS_ROW + 1, :] = shared
        for copy in small_steps + tensor_small + out_steps + gx_steps:
            copy().wait_send()
        for copy in (gx_write, ffn_write, late_write, far_write):
            copy.wait()


def attend_backward(qkv, context, source, weight, blocks, ffn_grads, out_grads, small):
    rows, width = source.shape
    own_rows, head_cols = rows // len(blocks), weight.shape[1]
    cols = 3 * LANES
    heads = head_cols // HEAD_DIM
    levels = (lax.axis_size("dp") - 1).bit_length()
    ffn_rows, late_rows = 2 * ffn_grads.shape[0], (heads + 1) * head_cols
    landing = ffn_rows + late_rows + 8 * 48 * levels
    transfers = 2 * 4 * 2 * levels + levels + 7
    array = jax.ShapeDtypeStruct
    whole = lambda *shape: pl.BlockSpec(shape, lambda h: (0,) * len(shape))
    head_block = lambda *shape: pl.BlockSpec((1,) + shape, lambda h: (h, 0, 0))
    anywhere = pl.BlockSpec(memory_space=pl.ANY)
    return pl.pallas_call(
        functools.partial(backward_kernel, key_block=256),
        grid=(heads,),
        in_specs=[
            head_block(rows, LANES),
            head_block(rows, LANES),
            head_block(rows, LANES),
            head_block(rows, HEAD_DIM),
            whole(rows, width),
            whole(*weight.shape),
        ]
        + [whole(*block.shape) for block in blocks]
        + [whole(*ffn_grads.shape), whole(*out_grads.shape), whole(*small.shape)],
        out_specs=[
            anywhere,
            anywhere,
            whole(16, width),
            anywhere,
            anywhere,
        ],
        out_shape=[
            array((ffn_rows, width), BF16),
            array((late_rows, width), BF16),
            array((16, width), F32),
            array((own_rows, width), F32),
            array((own_rows, width), BF16),
        ],
        scratch_shapes=[
            pltpu.VMEM((heads, rows, LANES), BF16),
            pltpu.VMEM((heads, cols, width), BF16),
            pltpu.VMEM((rows, cols), BF16),
            pltpu.VMEM((LANES, rows), BF16),
            pltpu.VMEM((rows, width), F32),
            pltpu.VMEM((ffn_rows // 2, width), BF16),
            pltpu.VMEM((ffn_rows, width), BF16),
            pltpu.VMEM((late_rows, width), BF16),
            pltpu.VMEM((late_rows, width), BF16),
            pltpu.VMEM((4 + heads, 8, width), F32),
            pltpu.VMEM((levels, 16, width), F32),
            pltpu.VMEM((landing, width), BF16),
            pltpu.VMEM((levels, 16, width), F32),
            pltpu.VMEM((2, head_cols, width), BF16),
            pltpu.VMEM((2, head_cols, width), BF16),
            pltpu.VMEM((head_cols, width), BF16),
            pltpu.VMEM((head_cols, width), BF16),
            pltpu.VMEM((2, own_rows, width), BF16),
            pltpu.VMEM((2, own_rows, width), BF16),
            pltpu.VMEM((own_rows, width), BF16),
            pltpu.VMEM((own_rows, width), BF16),
            pltpu.SemaphoreType.DMA((transfers,)),
            pltpu.SemaphoreType.DMA((transfers,)),
            pltpu.SemaphoreType.DMA((4,)),
        ],
        compiler_params=pltpu.CompilerParams(
            collective_id=4, has_side_effects=True, vmem_limit_bytes=62 * 2**20
        ),
        cost_estimate=pl.CostEstimate(
            flops=60 * heads * rows * rows * HEAD_DIM,
            bytes_accessed=2 * rows * heads * (cols + 7 * LANES),
            transcendentals=heads * rows * rows,
        ),
        name="attention_backward",
    )(*qkv, context, source, weight, *blocks, ffn_grads, out_grads, small)


def stacked(block):
    half = block.shape[0] // 2
    return jnp.concatenate([block[:half], block[half:]], axis=1)


def side_by_side(block):
    return jnp.concatenate([block[:, :HEAD_DIM], block[:, HEAD_DIM:]], axis=0)


(OUT_BIAS, GAIN_1, SHIFT_1, DOWN_BIAS, GAIN_2, SHIFT_2, UP_BIAS) = range(7)
T_VECTORS = 7
LOSS_ROW, UP_ROW = 6, 7


def middle_kernel(
    x_ref, ca0, ca1, ca2, ca3, tc_ref, ta0, ta1, ta2, ta3, outs0, outs1, outs2, outs3, w_up, s_down, vec,
    pack_own, pack_near, piece_a, piece_b, piece_c, next_a, sums_ref,
    out_ref, gh_ref, kept_ref, outg_ref, g0_ref, g1_ref, g2_ref, g3_ref, small_ref, piece_d, next_b, next_c, next_d,
    tc1, tc2, tcf, tc3, y_all, g_all, slope, hid, gu_all, t_out, first, normed, two, inv,
    part0, part2, send1, send2, send3, near0, near2, far0, gs, gr, packs, ffn_ref, ffn_land, w_outs, w_down,
    send_sem, recv_sem, pack_sem,
):
    near_id, far_id = neighbours()
    own_rows, width = x_ref.shape
    hidden = s_down.shape[0]
    head_cols = ca0.shape[1]
    size = own_rows // CHUNKS
    chunks = [slice(c * size, (c + 1) * size) for c in range(CHUNKS)]
    tiles = [slice(n, n + 256) for n in range(0, hidden, 256)]
    group = lambda j: slice(j * head_cols, (j + 1) * head_cols)
    outs = (outs0, outs1, outs2, outs3)
    w_out = lambda j: w_outs[j]
    tw_out = lambda j: outs[j][head_cols:, :]
    row = lambda index: vec[index : index + 1, :]

    place = lax.axis_index("dp")
    others = [{"tensor": near_id}, {"tensor": far_id}]
    others += [{"dp": in_pair(place, bit)[0]} for bit in dp_bits()[0][:2]]
    greet(others)

    count = [0]
    started = []

    def put(source, target, device, axis="tensor"):
        index = count[0]
        count[0] += 1
        copy = pltpu.make_async_remote_copy(
            src_ref=source,
            dst_ref=target,
            send_sem=send_sem.at[index],
            recv_sem=recv_sem.at[index],
            device_id={axis: device},
            device_id_type=pl.DeviceIdType.MESH,
        )
        copy.start()
        started.append(copy)
        return copy

    t_far = put(tc_ref.at[2], tc2, far_id)
    t_pass = put(tc_ref.at[3], tcf, far_id)
    t_near = put(tc_ref.at[1], tc1, near_id)
    next_id, level = in_pair(place, 2)
    cut = piece_a.shape[0]
    here = pl.ds(pl.multiple_of(level * cut, 16), cut)
    there = pl.ds(pl.multiple_of((1 - level) * cut, 16), cut)
    next_copies = [
        put(next_a, next_c, near_id),
        put(piece_b, next_b, next_id, "dp"),
        put(piece_b, piece_d, near_id),
    ]

    pack_refs = [pack_own.at[0], pack_own.at[1], pack_near.at[0], pack_near.at[1]]
    pack_refs += [(piece_a, next_a), (piece_c, next_c), (piece_b, next_b), (piece_d, next_d)]

    def load_pack(index):
        slot = index % 2
        source, target = pack_refs[index], packs.at[slot]
        if not isinstance(source, tuple):
            return [pltpu.make_async_copy(source, target, pack_sem.at[slot])]
        return [
            pltpu.make_async_copy(source[0], target.at[here], pack_sem.at[slot]),
            pltpu.make_async_copy(source[1], target.at[there], pack_sem.at[2 + slot]),
        ]

    def start_pack(index):
        for copy in load_pack(index):
            copy.start()

    start_pack(0)
    a_out = (sums_ref[0:1, :] * (1.0 / width)).astype(BF16)
    a_down = (sums_ref[1:2, :] * (1.0 / (lax.axis_size("tensor") * hidden))).astype(BF16)
    for j in range(4):
        w_outs[j] = outs[j][:head_cols, :] * a_out
    w_down[...] = s_down[...] * a_down
    small_ref[...] = jnp.zeros_like(small_ref)

    def add_small(index, values):
        small_ref[index : index + 1, :] += jnp.sum(values, axis=0, keepdims=True)

    def share(own_block, where):
        return (
            put(own_block.at[0, where], own_block.at[1, where], near_id),
            put(own_block.at[0, where], own_block.at[2, where], far_id),
        )

    y_sent = []
    for rows in chunks:
        attn = dot(ca0[rows, :], w_out(0)) + dot(ca1[rows, :], w_out(1))
        attn += dot(ca2[rows, :], w_out(2)) + dot(ca3[rows, :], w_out(3))
        y_one, y_normed, y_inv = norm_forward(
            x_ref[rows, :].astype(F32) + attn + row(OUT_BIAS), row(GAIN_1), row(SHIFT_1)
        )
        first[rows, :] = y_one
        normed[rows, :] = y_normed
        inv[rows, :] = jnp.broadcast_to(y_inv, (size, LANES))
        y_all[0, rows, :] = clip_act(y_one).astype(BF16)
        y_sent.append(share(y_all, rows))

    def forward_block(j, rows):
        total = None
        for cols in tiles:
            upward = dot(y_all[j, rows, :], w_up[:, cols]) + row(UP_BIAS)[:, cols]
            cdf, bell = normal_parts(upward)
            level = jnp.tanh(upward * cdf * (1.0 / CLIP_RANGE))
            act = (CLIP_RANGE * level).astype(BF16)
            hid[j, rows, cols] = act
            slope[j, rows, cols] = (1.0 - level * level) * (
                cdf + upward * bell * 0.3989422804014327
            )
            step = dot(act, w_down[cols, :])
            total = step if total is None else total + step
        return total

    def backward_block(j, rows):
        total = None
        for cols in tiles:
            grad = dot_cols(g_all[j, rows, :], w_down[cols, :])
            grad = (grad * slope[j, rows, cols]).astype(BF16)
            gu_all[j, rows, cols] = grad
            small_ref[UP_ROW : UP_ROW + 1, cols] += jnp.sum(
                grad.astype(F32), axis=0, keepdims=True
            )
            step = dot_cols(grad, w_up[:, cols])
            total = step if total is None else total + step
        return total

    def near_blocks(work, sent):
        copies = []
        for rows in chunks:
            part0[rows, :] = work(0, rows)
        for rows, (near, _) in zip(chunks, sent):
            near.wait_recv()
            send1[rows, :] = work(1, rows).astype(BF16)
            copies.append(put(send1.at[rows], near0.at[rows], near_id))
        return copies

    def far_blocks(block, work, sent, between=()):
        copies = []
        for c, (rows, (_, far)) in enumerate(zip(chunks, sent)):
            far.wait_recv()
            passed = put(block.at[2, rows], block.at[3, rows], near_id)
            part2[rows, :] = work(2, rows)
            passed.wait_recv()
            send3[rows, :] = work(3, rows).astype(BF16)
            met = put(send3.at[rows], near2.at[rows], near_id)
            met.wait_recv()
            send2[rows, :] = (part2[rows, :] + near2[rows, :].astype(F32)).astype(BF16)
            copies.append(put(send2.at[rows], far0.at[rows], far_id))
            if between:
                between[c]()
        return copies

    def summed(rows, near, far):
        near.wait_recv()
        far.wait_recv()
        return part0[rows, :] + near0[rows, :].astype(F32) + far0[rows, :].astype(F32)

    y_near = near_blocks(forward_block, y_sent)

    t_pass.wait_recv()
    t_last = put(tcf, tc3, near_id)
    t_near.wait_recv()
    t_far.wait_recv()
    t_row = lambda index: row(T_VECTORS + index)
    t_last.wait_recv()
    t_attn = None
    for j, (wide, last) in enumerate(zip((ta0, ta1, ta2, ta3), (tc_ref.at[0], tc1, tc2, tc3))):
        both = jnp.concatenate([wide[...], side_by_side(last[...])], axis=1)
        step = dot(both, tw_out(j))
        t_attn = step if t_attn is None else t_attn + step
    t_one, _, _ = norm_forward(x_ref[...].astype(F32) + t_attn + t_row(0), t_row(1), t_row(2))
    two[...] = t_one
    t_out[...] = t_one + t_row(3)
    half = hidden // 2
    t_in = t_one.astype(BF16)

    def teacher_packs(first, last):
        for index in range(first, last):
            slot = index % 2
            if index == 4:
                next_copies[0].wait_recv()
                next_copies[1].wait_recv()
                next_copies.append(put(next_b, next_d, near_id))
            if index == 6:
                next_copies[2].wait_recv()
                next_copies[3].wait_recv()
            if index + 1 < len(pack_refs):
                start_pack(index + 1)
            for copy in load_pack(index):
                copy.wait()
            upward = dot_cols(t_in, packs[slot, :half, :])
            upward = upward + packs[slot, hidden : hidden + 1, :half].astype(F32)
            act = (upward * normal_parts(upward)[0]).astype(BF16)
            t_out[...] += dot(act, packs[slot, half:hidden, :])

    middle_pack = len(pack_refs) // 2
    between = [
        functools.partial(teacher_packs, 0, middle_pack),
        functools.partial(teacher_packs, middle_pack, len(pack_refs)),
    ]
    y_far = far_blocks(y_all, forward_block, y_sent, between)
    t_out[...] = norm_forward(t_out[...], t_row(4), t_row(5))[0]

    g_sent = []
    earlier = list(started)
    started.clear()
    for rows, near, far in zip(chunks, y_near, y_far):
        ffn = summed(rows, near, far)
        out, n_two, inv_two = norm_forward(
            first[rows, :] + ffn + row(DOWN_BIAS), row(GAIN_2), row(SHIFT_2)
        )
        out_ref[rows, :] = out.astype(BF16)
        gap = out - t_out[rows, :]
        add_small(LOSS_ROW, gap * gap)
        add_small(GAIN_2, gap * n_two)
        add_small(SHIFT_2, gap)
        grad_two = norm_backward(gap, n_two, inv_two, row(GAIN_2))
        two[rows, :] = grad_two
        grad_ffn = grad_two.astype(BF16)
        add_small(DOWN_BIAS, grad_ffn.astype(F32))
        g_all[0, rows, :] = grad_ffn
        g_sent.append(share(g_all, rows))

    for copy in earlier:
        copy.wait_send()
    g_near = near_blocks(backward_block, g_sent)
    g_far = far_blocks(g_all, backward_block, g_sent)
    flat = lambda block: block[...].reshape(4 * own_rows, block.shape[2])

    def weight_gradients():
        ffn_ref[:width, :] = dot_rows(flat(y_all), flat(gu_all)).astype(BF16)
        ffn_ref[width:, :] = dot_rows(flat(hid), flat(g_all)).astype(BF16)
        sent, taken = [], 0
        for (low, count), order in zip(split_rows(0, width + hidden), dp_bits()):
            partner, digit = in_pair(place, order[0])
            count = count // 2
            give = ffn_ref.at[pl.ds(pl.multiple_of(low + (1 - digit) * count, 16), count)]
            keep = pl.multiple_of(low + digit * count, 16)
            land = ffn_land.at[taken : taken + count]
            sent.append((put(give, land, partner, "dp"), (keep, count)))
            taken += count
        return sent

    passes = []
    for c, (rows, near, far) in enumerate(zip(chunks, g_near, g_far)):
        y_one = first[rows, :]
        grad_one = two[rows, :] + summed(rows, near, far) * clip_slope(y_one)
        n_one = normed[rows, :]
        add_small(GAIN_1, grad_one * n_one)
        add_small(SHIFT_1, grad_one)
        grad_h = norm_backward(grad_one, n_one, inv[rows, :1], row(GAIN_1))
        gh_ref[rows, :] = grad_h
        grad_attn = grad_h.astype(BF16)
        add_small(OUT_BIAS, grad_attn.astype(F32))
        for j, ca in enumerate((ca0.at[rows], ca1.at[rows], ca2.at[rows], ca3.at[rows])):
            act = ca[...]
            level = act.astype(F32) * (1.0 / CLIP_RANGE)
            grad = dot_cols(grad_attn, w_out(j)) * (1.0 - level * level)
            grad = grad.astype(BF16)
            gs[j, c, :size, :] = grad[:, :LANES]
            gs[j, c, size:, :] = stacked(grad[:, LANES:])
            step = dot_rows(act, grad_attn)
            if c:
                step = step + part2[group(j), :]
            part2[group(j), :] = step
        passes.append(
            (
                put(gs.at[3, c], gr.at[3, c], far_id),
                put(gs.at[2, c], gr.at[1, c], far_id),
                put(gs.at[1, c], gr.at[0, c], near_id),
            )
        )
        if c == 0:
            halves = weight_gradients()
    g0_ref[...] = gs[0]
    for j in range(4):
        outg_ref[j] = part2[group(j), :].astype(BF16)
    lasts = []
    for c, (passing, _, _) in enumerate(passes):
        passing.wait_recv()
        lasts.append(put(gr.at[3, c], gr.at[2, c], near_id))
    for c, ((_, far, near), last) in enumerate(zip(passes, lasts)):
        near.wait_recv()
        g1_ref[c] = gr[0, c]
        far.wait_recv()
        g2_ref[c] = gr[1, c]
        last.wait_recv()
        g3_ref[c] = gr[2, c]
    taken = 0
    for copy, (keep, part_size) in halves:
        copy.wait_recv()
        land = slice(taken, taken + part_size)
        mine = ffn_ref[pl.ds(keep, part_size), :].astype(F32)
        kept_ref[land, :] = (mine + ffn_land[land, :].astype(F32)).astype(BF16)
        taken += part_size
    for copy in started:
        copy.wait_send()


def middle(x_own, cas, tcs, outs, w_up, s_down, vectors, packs, sums):
    own_rows, width = x_own.shape
    hidden = s_down.shape[0]
    head_cols = cas[0].shape[1]
    array = jax.ShapeDtypeStruct
    vmem = pl.BlockSpec(memory_space=pltpu.VMEM)
    transfers = 8 + 4 * 3 * CHUNKS + 4 * CHUNKS + 2
    packed = (CHUNKS, own_rows // CHUNKS * 3 // 2, LANES)
    four_outs = pltpu.VMEM((4, head_cols, width), BF16)
    square = lambda kind: pltpu.VMEM((own_rows, width), kind)
    four = lambda cols, kind: pltpu.VMEM((4, own_rows, cols), kind)
    return pl.pallas_call(
        middle_kernel,
        in_specs=[vmem] * 17 + [pl.BlockSpec(memory_space=pl.ANY)] * 6 + [vmem],
        out_specs=[vmem] * 9 + [pl.BlockSpec(memory_space=pl.ANY)] * 4,
        out_shape=[
            array((own_rows, width), BF16),
            array((own_rows, width), F32),
            array(((width + hidden) // 2, width), BF16),
            array((4, head_cols, width), BF16),
        ]
        + [array(packed, BF16)] * 4
        + [array((8, width), F32)]
        + [array(packs[2].shape, BF16)] * 4,
        scratch_shapes=[pltpu.VMEM(tcs[0].shape[1:], BF16)] * 4
        + [four(width, BF16), four(width, BF16), four(hidden, F32), four(hidden, BF16)]
        + [four(hidden, BF16)]
        + [square(F32)] * 4
        + [pltpu.VMEM((own_rows, LANES), F32)]
        + [square(F32), pltpu.VMEM((4 * max(own_rows // 4, head_cols), width), F32)]
        + [square(BF16)] * 6
        + [pltpu.VMEM((4,) + packed, BF16)] * 2
        + [
            pltpu.VMEM(packs[0].shape, BF16),
            pltpu.VMEM((width + hidden, width), BF16),
            pltpu.VMEM(((width + hidden) // 2, width), BF16),
            four_outs,
            pltpu.VMEM(s_down.shape, BF16),
            pltpu.SemaphoreType.DMA((transfers,)),
            pltpu.SemaphoreType.DMA((transfers,)),
            pltpu.SemaphoreType.DMA((4,)),
        ],
        compiler_params=pltpu.CompilerParams(
            collective_id=3, has_side_effects=True, vmem_limit_bytes=62 * 2**20
        ),
        cost_estimate=pl.CostEstimate(
            flops=120 * own_rows * width * hidden, bytes_accessed=2**25, transcendentals=2**22
        ),
        name="middle",
    )(x_own, *cas, *tcs, *outs, w_up, s_down, vectors, *packs, sums)


def finish_kernel(
    ffn_ref, late_ref, small_ref, gx_ref, gx_far_ref, gh_ref, x_ref, y_ref,
    up_ref, down_ref, qkv_ref, out_ref, input_ref, y_out, bias_ref, loss_ref, *vectors, tokens
):
    up_ref[...] = ffn_ref[0].astype(F32)
    down_ref[...] = ffn_ref[1].astype(F32)
    grad = gx_ref[...] + gx_far_ref[...].astype(F32)
    input_ref[...] = gh_ref[...] + grad * clip_slope(x_ref[...].astype(F32))
    y_out[...] = y_ref[...]

    @pl.when(pl.program_id(0) == 0)
    def _():
        cols = out_ref.shape[0]
        heads = cols // HEAD_DIM
        out_ref[...] = late_ref[cols : 2 * cols, :].astype(F32)
        for h in range(heads):
            first = 0 if h == 0 else cols + h * cols
            for c in range(3):
                rows = slice(first + c * HEAD_DIM, first + (c + 1) * HEAD_DIM)
                qkv_ref[c, h * HEAD_DIM : (h + 1) * HEAD_DIM, :] = late_ref[rows, :].astype(F32)
        for index, (lane, factor) in enumerate(((0, 0.125), (2 * LANES, 1.0))):
            parts = [small_ref[8 + h : 9 + h, lane : lane + HEAD_DIM] for h in range(heads)]
            bias_ref[index : index + 1, :] = jnp.concatenate(parts, axis=1) * factor
        for row, vector in zip((0, 1, 2, UP_ROW, 3, 4, 5), vectors):
            vector[...] = small_ref[row : row + 1, :].reshape(vector.shape)
        loss_ref[0] = jnp.sum(small_ref[LOSS_ROW : LOSS_ROW + 1, :]) * (1.0 / tokens)


def finish(ffn, late, small, gx, gx_far, grad_h, x_own, out_own, head_cols, tokens):
    own_rows, width = x_own.shape
    steps = 4
    array = jax.ShapeDtypeStruct
    whole = lambda *shape: pl.BlockSpec(shape, lambda i: (0,) * len(shape))
    by_rows = lambda rows: pl.BlockSpec((rows // steps, width), lambda i: (i, 0))
    hidden = ffn.shape[0] // 2
    return pl.pallas_call(
        functools.partial(finish_kernel, tokens=tokens),
        grid=(steps,),
        in_specs=[
            pl.BlockSpec((2, hidden // steps, width), lambda i: (0, i, 0)),
            whole(*late.shape),
            whole(*small.shape),
        ]
        + [by_rows(own_rows)] * 5,
        out_specs=[
            by_rows(hidden),
            by_rows(hidden),
            whole(3, head_cols, width),
            whole(head_cols, width),
            by_rows(own_rows),
            by_rows(own_rows),
            whole(2, head_cols),
            pl.BlockSpec(memory_space=pltpu.SMEM),
        ]
        + [whole(width)] * 7,
        out_shape=[
            array((hidden, width), F32),
            array((hidden, width), F32),
            array((3, head_cols, width), F32),
            array((head_cols, width), F32),
            array((own_rows, width), F32),
            array((own_rows, width), BF16),
            array((2, head_cols), F32),
            array((1,), F32),
        ]
        + [array((width,), F32)] * 7,
        compiler_params=pltpu.CompilerParams(vmem_limit_bytes=58 * 2**20),
        name="finish",
    )(ffn.reshape(2, hidden, width), late, small, gx, gx_far, grad_h, x_own, out_own)


def body(
    tokens,
    seg_lengths,
    parents,
    qkv_latent,
    qv_bias,
    out_latent,
    out_bias,
    norm1_gain,
    norm1_shift,
    up_latent,
    up_bias,
    down_latent,
    down_bias,
    norm2_gain,
    norm2_shift,
    teacher_qkv,
    teacher_qv_bias,
    teacher_out,
    teacher_out_bias,
    teacher_norm1_gain,
    teacher_norm1_shift,
    teacher_up,
    teacher_up_bias,
    teacher_down,
    teacher_down_bias,
    teacher_norm2_gain,
    teacher_norm2_shift,
):
    own_rows, model_width = tokens.shape
    group = lax.axis_size("tensor")
    me = lax.axis_index("tensor")
    all_rows = own_rows * group
    local_cols = qkv_latent.shape[2]
    blocks = [tokens, swap(tokens, 1), swap(tokens, 2)]
    qkv_latent, teacher_qkv = qkv_latent.transpose(1, 2, 0), teacher_qkv.transpose(1, 2, 0)
    latents = [qkv_latent, out_latent, teacher_out, up_latent, down_latent]
    latents += [teacher_up, teacher_down, teacher_up_bias]
    vectors = [out_bias, norm1_gain, norm1_shift, down_bias, norm2_gain, norm2_shift, up_bias]
    vectors += [teacher_out_bias, teacher_norm1_gain, teacher_norm1_shift]
    vectors += [teacher_down_bias, teacher_norm2_gain, teacher_norm2_shift]
    w_qkv, outs, w_up, s_down, pack, sums, vectors = prepare(latents, vectors)
    seg_lanes, blocked = segment_tables(seg_lengths[0], parents[0])
    base = jnp.stack([(me ^ j) * own_rows for j in range(group)]).astype(jnp.int32)

    tables = (seg_lanes, blocked)
    *qkv, context, x_in_all, ca_own, ca_near, ca_far, sums, pack_near, piece_a, outs1, outs2 = attend_forward(
        base, blocks, w_qkv, qv_bias, *tables, [pack, outs, sums], True
    )
    t_last, ta0, ca1, ca2, _, ca3, ta1, ta2, _, ta3, outs3, next_a, piece_b, piece_c = attend_forward(
        base, blocks, teacher_qkv, teacher_qv_bias, *tables,
        [ca_near, ca_far, outs2, piece_a], False,
    )
    cas, outs = [ca_own, ca1, ca2, ca3], [outs, outs1, outs2, outs3]
    packs = [pack, pack_near, piece_a, piece_b, piece_c, next_a]
    out_own, grad_h, ffn_grads, out_grads, g0, g1, g2, g3, small, *_ = middle(
        tokens, cas, [t_last, ta0, ta1, ta2, ta3], outs, w_up, s_down, vectors, packs, sums
    )
    ffn_grads, late, small, gx_own, gx_far = attend_backward(
        qkv, context, x_in_all, w_qkv, [g0, g1, g2, g3], ffn_grads, out_grads, small
    )
    up_grad, down_grad, qkv_grad, out_grad, input_grad, out_own, bias_grad, loss, *vectors = finish(
        ffn_grads, late, small, gx_own, gx_far, grad_h, tokens, out_own, local_cols,
        all_rows * model_width,
    )
    return (
        out_own,
        loss,
        input_grad,
        qkv_grad.transpose(2, 0, 1),
        bias_grad,
        out_grad,
        *vectors[:3],
        up_grad,
        vectors[3],
        down_grad,
        *vectors[4:],
    )


def solution(mesh):
    rows, cols = ("dp", "tensor"), "tensor"
    vec = P()
    params = (
        P(None, None, cols),
        P(None, cols),
        P(cols, None),
        vec,
        vec,
        vec,
        P(None, cols),
        P(cols),
        P(cols, None),
        vec,
        vec,
        vec,
    )
    in_specs = (P(rows, None), P("dp", None), P("dp", None)) + params + params
    out_specs = (P(rows, None), P("dp"), P(rows, None)) + params
    return jax.shard_map(body, mesh=mesh, in_specs=in_specs, out_specs=out_specs, check_vma=False)
```

```python
import functools

import jax
import jax.numpy as jnp
from jax import lax
from jax.experimental import pallas as pl
from jax.experimental.pallas import tpu as pltpu
from jax.sharding import PartitionSpec as P

HEAD_DIM = 64
LANES = 128
CLIP_RANGE = 3.0
NORM_EPSILON = 1e-05
MASKED_SCORE = -1e30
SEG_LANE = HEAD_DIM
ROW_TERM = HEAD_DIM + 16
Q_BLOCK = 256
PACK_PAD = 32
CHUNKS = 2
BF16, F32 = jnp.bfloat16, jnp.float32
ROWS_ROWS = (((0,), (0,)), ((), ()))
COLS_COLS = (((1,), (1,)), ((), ()))


def clip_act(values):
    return CLIP_RANGE * jnp.tanh(values / CLIP_RANGE)


def clip_slope(values):
    level = jnp.tanh(values / CLIP_RANGE)
    return 1.0 - level * level


def normal_parts(values):
    bell = jnp.exp(-0.5 * values * values)
    step = 1.0 / (1.0 + 0.23164188843 * jnp.abs(values))
    series = 0.5307027145 * step - 0.7265760135
    series = series * step + 0.7107068705
    series = series * step - 0.142248368
    series = series * step + 0.127414796
    tail = series * step * bell
    return jnp.where(values >= 0.0, 1.0 - tail, tail), bell


def norm_forward(hidden, gain, shift):
    row_mean = jnp.mean(hidden, axis=-1, keepdims=True)
    centred = hidden - row_mean
    inv_std = lax.rsqrt(jnp.mean(centred * centred, axis=-1, keepdims=True) + NORM_EPSILON)
    normed = centred * inv_std
    return (normed * gain + shift, normed, inv_std)


def norm_backward(grad_out, normed, inv_std, gain):
    grad_normed = grad_out * gain
    centre = jnp.mean(grad_normed, axis=-1, keepdims=True)
    inner_sum = jnp.mean(grad_normed * normed, axis=-1, keepdims=True)
    return inv_std * (grad_normed - centre - normed * inner_sum)


def dot(left, right):
    return jnp.dot(left, right, preferred_element_type=F32)


def dot_rows(left, right):
    return lax.dot_general(left, right, ROWS_ROWS, preferred_element_type=F32)


def dot_cols(left, right):
    return lax.dot_general(left, right, COLS_COLS, preferred_element_type=F32)


def swap(array, bit):
    size = lax.axis_size("tensor")
    return lax.ppermute(array, "tensor", [(i, i ^ bit) for i in range(size)])


def lookup(indices, lookup_table):
    labels = jnp.arange(lookup_table.shape[0], dtype=jnp.int32)
    picked = jnp.where(indices[:, None] == labels[None, :], lookup_table[None, :], 0)
    return jnp.sum(picked, axis=1)


def segment_tables(lengths, parent):
    count = lengths.shape[0]
    labels = jnp.arange(count, dtype=jnp.int32)
    row, col = labels[:, None], labels[None, :]
    starts = jnp.sum(jnp.where(col < row, lengths[None, :], 0), axis=1)
    two = lookup(parent, parent)
    allowed = (col == row) | (col == parent[:, None]) | (col == two[:, None])
    allowed = allowed | (parent[None, :] == row) | (two[None, :] == row)
    after = LANES - SEG_LANE - count
    lanes = jnp.pad(jnp.stack([starts, starts + lengths]), ((0, 6), (SEG_LANE, after)))
    blocked = jnp.pad((~allowed).astype(BF16), ((SEG_LANE, after), (SEG_LANE, after)))
    return lanes, blocked


def split_three(values):
    first = values.astype(BF16).astype(F32)
    second = (values - first).astype(BF16).astype(F32)
    return first, second, values - first - second


def sign_of(values):
    return jnp.where(values > 0.0, 1.0, jnp.where(values < 0.0, -1.0, 0.0))


def prepare_kernel(
    qkv_ref, out_ref, t_out_ref, up_ref, down_ref, t_up_ref, t_down_ref, t_bias_ref, *rest
):
    *vectors, w_qkv_ref, outs_ref, w_up_ref, s_down_ref, pack_ref, sums_ref, vec_ref = rest
    vec_ref[...] = jnp.zeros_like(vec_ref)
    for index, vector in enumerate(vectors):
        vec_ref[index : index + 1, :] = vector[...].astype(F32).reshape(1, -1)
    hidden, width = down_ref.shape
    half = hidden // 2
    rows = out_ref.shape[0]
    for c in range(3):
        latent = qkv_ref[c]
        scale = jnp.sum(jnp.abs(latent), axis=1, keepdims=True) * (1.0 / width)
        w_qkv_ref[c] = (scale * sign_of(latent)).astype(BF16)
    total = lambda ref: jnp.sum(jnp.abs(ref[...]), axis=0, keepdims=True)
    sums_ref[...] = jnp.zeros_like(sums_ref)
    sums_ref[0:1, :] = total(out_ref)
    sums_ref[1:2, :] = total(down_ref)
    outs_ref[:rows, :] = sign_of(out_ref[...]).astype(BF16)
    outs_ref[rows:, :] = t_out_ref[...]
    w_up_ref[...] = (total(up_ref) * (1.0 / width) * sign_of(up_ref[...])).astype(BF16)
    s_down_ref[...] = sign_of(down_ref[...]).astype(BF16)
    up_t = t_up_ref[...].T
    pack_ref[:, hidden:, :] = jnp.zeros((2, PACK_PAD, width), BF16)
    for side in range(2):
        cols = slice(side * half, (side + 1) * half)
        pack_ref[side, :half, :] = up_t[cols]
        pack_ref[side, half:hidden, :] = t_down_ref[cols, :]
        bias = t_bias_ref[cols].astype(F32).reshape(1, -1)
        pack_ref[side, hidden : hidden + 1, :half] = bias.astype(BF16)


def prepare(latents, vectors):
    array = jax.ShapeDtypeStruct
    qkv_latent, out_latent, _, up_latent, down_latent, *_ = latents
    hidden, width = down_latent.shape
    return pl.pallas_call(
        prepare_kernel,
        out_shape=[
            array(qkv_latent.shape, BF16),
            array((2 * out_latent.shape[0], width), BF16),
            array(up_latent.shape, BF16),
            array(down_latent.shape, BF16),
            array((2, hidden + PACK_PAD, width), BF16),
            array((8, width), F32),
            array((16, width), F32),
        ],
        compiler_params=pltpu.CompilerParams(vmem_limit_bytes=58 * 2**20),
        cost_estimate=pl.CostEstimate(
            flops=16 * 10**9, bytes_accessed=24 * width * hidden, transcendentals=0
        ),
        name="prepare",
    )(*latents, *vectors)


def in_lane(shape, axis, terms):
    lane = lax.broadcasted_iota(jnp.int32, shape, axis)
    spread = jnp.zeros(shape, F32)
    for offset, term in enumerate(terms):
        spread = jnp.where(lane == ROW_TERM + offset, term, spread)
    return spread


def make_copies(send_sem, recv_sem):
    count = [0]

    def copy_to(source, target, axis, device):
        index = count[0]
        count[0] += 1

        def make():
            return pltpu.make_async_remote_copy(
                src_ref=source,
                dst_ref=target,
                send_sem=send_sem.at[index],
                recv_sem=recv_sem.at[index],
                device_id={axis: device},
                device_id_type=pl.DeviceIdType.MESH,
            )

        return make

    return copy_to


def greet(others):
    barrier = pltpu.get_barrier_semaphore()
    for other in others:
        pl.semaphore_signal(barrier, inc=1, device_id=other, device_id_type=pl.DeviceIdType.MESH)
    pl.semaphore_wait(barrier, len(others))


def neighbours():
    me = lax.axis_index("tensor")
    return me + 1 - 2 * lax.rem(me, 2), lax.rem(me + 2, lax.axis_size("tensor"))


def forward_kernel(base_ref, x0, x1, x2, w_ref, b_ref, seg_ref, blocked_ref, *rest, student):
    if student:
        pack_ref, outs, sums_ref, *rest = rest
        q_ref, k_ref, v_ref, ctx_ref, source, own, near, far, *rest = rest
        sums_out, pack_near, piece_a, outs1, outs2, sums, *rest = rest
    else:
        ca_near, ca_far, outs2, piece_a, *rest = rest
        sent, ta0, ca1, ca2, ca_pass, ca3, ta1, ta2, ta_pass, ta3, *rest = rest
        outs3, next_a, piece_b, piece_c, source, send_a, *rest = rest
    x3, joined, queries, keys, vals_t, send_sem, recv_sem = rest
    blocks = (x0, x1, x2, x3)
    own_rows = x0.shape[0]
    rows = own_rows * len(blocks)
    heads = joined.shape[0]
    head = pl.program_id(0)
    near_id, far_id = neighbours()
    place = lax.axis_index("dp")
    copy_to = make_copies(send_sem, recv_sem)
    side_id, side = in_pair(place, 1)
    next_id, level = in_pair(place, 2)
    others = [{"tensor": near_id}, {"tensor": far_id}, {"dp": side_id}]
    if not student:
        others.append({"dp": next_id})
    if student:
        size = piece_a.shape[0]
        quarter = pack_ref.at[side, pl.ds(pl.multiple_of(level * size, 16), size)]
        half = outs.shape[0] // 2
        rows_of = pl.ds(pl.multiple_of(side * half, 16), half)
        outs_far = copy_to(outs.at[rows_of], outs2.at[rows_of], "tensor", far_id)
        pack_far = copy_to(quarter, piece_a, "tensor", far_id)
        sum_near = copy_to(sums.at[0], sums.at[1], "tensor", near_id)
        sum_far = copy_to(sums.at[2], sums.at[3], "tensor", far_id)
        stages = [
            (
                [],
                [
                    sum_near,
                    outs_far,
                    copy_to(outs, outs1, "tensor", near_id),
                    copy_to(pack_ref, pack_near, "tensor", near_id),
                ],
            ),
            ([outs_far], [pack_far, copy_to(outs2.at[rows_of], outs2.at[rows_of], "dp", side_id)]),
            ([], []),
        ]
    else:
        passing = copy_to(ca_far.at[1], ca_pass, "tensor", far_id)
        stages = [
            (
                [],
                [
                    passing,
                    copy_to(ca_far.at[0], ca2, "tensor", far_id),
                    copy_to(ca_near, ca1, "tensor", near_id),
                    copy_to(outs2, outs3, "tensor", near_id),
                    copy_to(piece_a, next_a, "dp", next_id),
                    copy_to(piece_a, piece_c, "tensor", near_id),
                    copy_to(piece_a, piece_b, "dp", side_id),
                ],
            ),
            ([], []),
            ([passing], [copy_to(ca_pass, ca3, "tensor", near_id)]),
        ]
        a_passing = copy_to(send_a.at[3], ta_pass, "tensor", far_id)
        a_copies = [
            a_passing,
            copy_to(send_a.at[2], ta2, "tensor", far_id),
            copy_to(send_a.at[1], ta1, "tensor", near_id),
        ]
        a_last = copy_to(ta_pass, ta3, "tensor", near_id)

    last_block = copy_to(x2, x3, "tensor", near_id)

    def run_stage(index):
        before, copies = stages[index]
        for copy in before:
            copy().wait_recv()
        for copy in copies:
            copy().start()

    @pl.when(head == 0)
    def _():
        if student:
            sums[0] = sums_ref[...]
        greet(others)
        last_block().start()
        run_stage(0)
        lane = lax.broadcasted_iota(jnp.int32, (own_rows, LANES), 1)
        ones = (lane >= ROW_TERM) & (lane < ROW_TERM + 3)
        for j, block in enumerate(blocks):
            if j == 3:
                last_block().wait()
            part = slice(j * own_rows, (j + 1) * own_rows)
            if student:
                source[part, :] = clip_act(block[...].astype(F32)).astype(BF16)
            else:
                source[part, :] = block[...]
            spot = lax.broadcasted_iota(jnp.int32, (own_rows, LANES), 0) + base_ref[j]
            inside = (spot >= seg_ref[0:1, :]) & (spot < seg_ref[1:2, :])
            links = dot(jnp.where(inside, 1.0, 0.0).astype(BF16), blocked_ref[...])
            extras = (
                jnp.where(inside, MASKED_SCORE, 0.0).astype(BF16),
                jnp.where(ones, 1.0, links).astype(BF16),
                jnp.where(ones, 1.0, 0.0).astype(BF16),
            )
            for c, (scale, extra) in enumerate(zip((0.125, 1.0, 1.0), extras)):
                proj = dot_cols(source[part, :], w_ref[c])
                if c != 1:
                    proj = proj + b_ref[c // 2 : c // 2 + 1, :].astype(F32)
                proj = proj.astype(BF16)
                for h in range(heads):
                    one = proj[:, h * HEAD_DIM : (h + 1) * HEAD_DIM] * scale
                    wide = jnp.concatenate([one, jnp.zeros_like(one)], axis=1) + extra
                    if c == 0:
                        queries[h, part, :] = wide
                    elif c == 1:
                        keys[h, part, :] = wide
                    else:
                        vals_t[h, :, part] = wide.T
                        if student:
                            v_ref[h, part, :] = wide

    if student:
        k_ref[0] = keys[head]
    else:

        @pl.when(head == heads - 1)
        def _():
            for j in range(len(blocks)):
                part = slice(j * own_rows, (j + 1) * own_rows)
                pair = jnp.concatenate([joined[0, part, :], joined[1, part, :]], axis=1)
                send_a[j] = pair.astype(BF16)
            for copy in a_copies:
                copy().start()

    scores = {}
    for index in range(rows // Q_BLOCK):
        if index % (rows // Q_BLOCK // 2) == 0:
            if index:

                @pl.when(head == 0)
                def _():
                    run_stage(1)

                @pl.when(head == 1)
                def _():
                    run_stage(2)
                    if student:
                        sum_near().wait_recv()
                        sums[2] = sums[0] + sums[1]
                        sum_far().start()

            for later in range(index, index + rows // Q_BLOCK // 2):
                start = later * Q_BLOCK
                scores[later] = dot_cols(keys[head], queries[head, start : start + Q_BLOCK, :])
        block = scores[index]
        part = slice(index * Q_BLOCK, (index + 1) * Q_BLOCK)
        peak = jnp.max(block, axis=0, keepdims=True)
        raised = jnp.exp(block - peak)
        total = jnp.sum(raised, axis=0, keepdims=True)
        weights = (raised * (1.0 / total)).astype(BF16)
        context = dot(vals_t[head], weights)[:HEAD_DIM].T
        joined[head, part, :] = context
        if student:
            ctx_ref[0, part, :] = context
            terms = split_three(-(peak + jnp.log(total)))
            spread = in_lane((LANES, Q_BLOCK), 0, terms)
            q_ref[0, part, :] = queries[head, part, :] + spread.T.astype(BF16)

    @pl.when(head == heads - 1)
    def _():
        for j in range(len(blocks)):
            part = slice(j * own_rows, (j + 1) * own_rows)
            if not student:
                sent[j] = stacked(joined[heads - 1, part, :]).astype(BF16)
                continue
            block = jnp.concatenate([joined[h, part, :] for h in range(heads)], axis=1)
            if j < 2:
                (own, near)[j][...] = clip_act(block).astype(BF16)
            else:
                far[j - 2] = clip_act(block).astype(BF16)
        waited = [copy for before, _ in stages for copy in before]
        if not student:
            ta0[...] = send_a[0]
            a_passing().wait_recv()
            a_last().start()
            for copy in a_copies:
                copy().wait_send()
            for copy in a_copies[1:] + [a_last]:
                copy().wait_recv()
            a_last().wait_send()
        if student:
            sum_far().wait_recv()
            sums_out[...] = sums[2] + sums[3]
            sum_far().wait_send()
            waited.append(sum_near)
        for _, copies in stages:
            for copy in copies:
                copy().wait_send()
                if copy not in waited:
                    copy().wait_recv()


def attend_forward(base, blocks, weight, bias, seg_lanes, blocked, moved, student):
    own_rows, width = blocks[0].shape
    group = len(blocks) + 1
    rows = own_rows * group
    head_cols = weight.shape[1]
    heads = head_cols // HEAD_DIM
    whole = lambda *shape: pl.BlockSpec(shape, lambda h: (0,) * len(shape))
    anywhere = pl.BlockSpec(memory_space=pl.ANY)
    array = jax.ShapeDtypeStruct
    per_head = lambda cols: pl.BlockSpec((1, rows, cols), lambda h: (h, 0, 0))
    if student:
        pack, out_weights, sums = moved
        piece = (pack.shape[1] // 2, width)
        outs = [
            (per_head(LANES), array((heads, rows, LANES), BF16)),
            (per_head(LANES), array((heads, rows, LANES), BF16)),
            (whole(heads, rows, LANES), array((heads, rows, LANES), BF16)),
            (per_head(HEAD_DIM), array((heads, rows, HEAD_DIM), F32)),
            (whole(rows, width), array((rows, width), BF16)),
            (whole(own_rows, head_cols), array((own_rows, head_cols), BF16)),
            (whole(own_rows, head_cols), array((own_rows, head_cols), BF16)),
            (whole(2, own_rows, head_cols), array((2, own_rows, head_cols), BF16)),
            (whole(*sums.shape), array(sums.shape, F32)),
            (anywhere, array(pack.shape, BF16)),
        ]
        outs += [(anywhere, array(piece, BF16))]
        outs += [(anywhere, array(out_weights.shape, BF16))] * 2
        scratch, transfers = [pltpu.VMEM((4,) + sums.shape, F32)], 8
    else:
        ca_near, ca_far, out_weights, piece = moved
        last = (group, own_rows // 2, LANES)
        pair = array((own_rows, LANES), BF16)
        outs = [(whole(*last), array(last, BF16)), (whole(*pair.shape), pair)]
        outs += [(anywhere, array(ca_near.shape, BF16))] * 4 + [(anywhere, pair)] * 4
        outs += [(anywhere, array(out_weights.shape, BF16))]
        outs += [(anywhere, array(piece.shape, BF16))] * 3
        scratch, transfers = [pltpu.VMEM((rows, width), BF16)], 13
        scratch.append(pltpu.VMEM((group,) + pair.shape, BF16))
    scratch += [
        pltpu.VMEM((own_rows, width), BF16),
        pltpu.VMEM((heads, rows, HEAD_DIM), F32),
        pltpu.VMEM((heads, rows, LANES), BF16),
        pltpu.VMEM((heads, rows, LANES), BF16),
        pltpu.VMEM((heads, LANES, rows), BF16),
        pltpu.SemaphoreType.DMA((transfers,)),
        pltpu.SemaphoreType.DMA((transfers,)),
    ]
    return pl.pallas_call(
        functools.partial(forward_kernel, student=student),
        grid=(heads,),
        in_specs=[pl.BlockSpec(memory_space=pltpu.SMEM)]
        + [whole(own_rows, width)] * 3
        + [whole(*a.shape) for a in (weight, bias, seg_lanes, blocked)]
        + [whole(*a.shape) if a.dtype == F32 else anywhere for a in moved],
        out_specs=[spec for spec, _ in outs],
        out_shape=[shape for _, shape in outs],
        scratch_shapes=scratch,
        compiler_params=pltpu.CompilerParams(
            collective_id=1 if student else 2, has_side_effects=True, vmem_limit_bytes=58 * 2**20
        ),
        cost_estimate=pl.CostEstimate(
            flops=16 * heads * rows * rows * HEAD_DIM,
            bytes_accessed=2 * rows * (width + 6 * heads * LANES),
            transcendentals=heads * rows * rows,
        ),
        name="student_attention" if student else "teacher_attention",
    )(base, *blocks, weight, bias, seg_lanes, blocked, *moved)


def in_pair(place, bit):
    digit = lax.rem(lax.div(place, bit), 2)
    return place + bit - 2 * bit * digit, digit


def halving_steps(partial, total, landing, rows, landing_row, order, place, copy_of, done=0, base=None):
    low, size = rows
    here = low if base is None else base
    steps, levels, used = [], [], landing_row
    for level, bit in enumerate(order):
        partner, digit = in_pair(place, bit)
        halved = size % 32 == 0
        count = size // 2 if halved else size
        low = pl.multiple_of(low + digit * count, 16) if halved else low
        if level >= done:
            give = pl.multiple_of(here + (1 - digit) * count, 16) if halved else here
            here = pl.multiple_of(here + digit * count, 16) if halved else here
            copy = copy_of(partial.at[pl.ds(give, count)], landing.at[pl.ds(used, count)], partner)
            last = level == len(order) - 1

            def add(used=used, here=here, count=count, out=total if last else partial, at=low if last else here):
                arrived = landing[used : used + count, :].astype(F32)
                mine = partial[pl.ds(here, count), :].astype(F32)
                out[pl.ds(at, count), :] = (mine + arrived).astype(out.dtype)

            steps.append((copy, add))
            used += count
        if halved:
            levels.append((count, low, partner))
        size = count
    for count, keep, partner in reversed(levels):
        where = total.at[pl.ds(keep, count)]
        steps.append((copy_of(where, where, partner), lambda: None))
    return steps, used


def run_step(plans, index):
    for steps in plans:
        if 0 < index <= len(steps):
            copy, after = steps[index - 1]
            copy().wait()
            after()
        if index < len(steps):
            steps[index][0]().start()


def split_rows(first, count):
    small = count // 2 if count % 512 == 0 else -(-count // 3 // 64) * 64
    return ((first, count - small), (first + count - small, small))


def dp_bits():
    bits = [1 << i for i in range((lax.axis_size("dp") - 1).bit_length())]
    return bits, (bits[1:2] + bits[:1] + bits[2:])


def backward_kernel(
    q_ref, k_ref, v_ref, ctx_ref, x_hbm, w_ref, g0, g1, g2, g3, ffn_hbm, outg_ref, small_ref,
    ffn_out, late_out, small_out, gx_out, gxfar_out,
    grads, wide, packed, keys_t, total, ffn_part, ffn, late_in, late, small, small_in, landing, small_land,
    out_near, out_near_land, out_far, out_far_land, gx_near, gx_near_land, gx_far, gx_far_land,
    x_ref, send_sem, recv_sem, write_sem, *, key_block,
):
    blocks = (g0, g1, g2, g3)
    rows = x_ref.shape[0]
    own_rows = rows // len(blocks)
    heads = grads.shape[0]
    head_cols = heads * HEAD_DIM
    head = pl.program_id(0)
    place = lax.axis_index("dp")
    near_id, far_id = neighbours()
    part = lambda j: slice(j * own_rows, (j + 1) * own_rows)
    bits, turned = dp_bits()

    copy_to = make_copies(send_sem, recv_sem)
    over_dp = lambda source, target, other: copy_to(source, target, "dp", other)
    over_tensor = lambda source, target, other: copy_to(source, target, "tensor", other)

    used = [0]

    def reduced(partial, target, first, size, done=0):
        plans, taken = [], 0
        for rows_of, order in zip(split_rows(first, size), (bits, turned)):
            steps, used[0] = halving_steps(
                partial, target, landing, rows_of, used[0], order, place, over_dp, done,
                taken if done else None,
            )
            plans.append(steps)
            taken += rows_of[1] >> done
        return plans

    width = x_ref.shape[1]
    ffn_plans = reduced(ffn_part, ffn, 0, ffn.shape[0], 1)
    early_plans = reduced(late_in, late, 0, 2 * head_cols)
    middle_plans = reduced(late_in, late, 2 * head_cols, head_cols)
    last_plans = reduced(late_in, late, 3 * head_cols, head_cols)
    small_steps = []
    for level, bit in enumerate(bits):
        partner, _ = in_pair(place, bit)
        small_steps.append(over_dp(small_in.at[level], small_land.at[level], partner))
    tensor_small = [
        over_tensor(small.at[0], small.at[1], near_id),
        over_tensor(small.at[2], small.at[3], far_id),
    ]
    out_steps = [
        over_tensor(out_near, out_near_land, near_id),
        over_tensor(out_far, out_far_land, far_id),
    ]
    gx_steps = [
        over_tensor(gx_near.at[1], gx_near_land.at[1], near_id),
        over_tensor(gx_near.at[0], gx_near_land.at[0], near_id),
        over_tensor(gx_far, gx_far_land, far_id),
    ]

    load_ffn = lambda: pltpu.make_async_copy(ffn_hbm, ffn_part, write_sem.at[1])
    load_x = lambda: pltpu.make_async_copy(x_hbm, x_ref, write_sem.at[2])

    @pl.when(head == 0)
    def _():
        load_ffn().start()
        load_x().start()
        others = [{"tensor": near_id}, {"tensor": far_id}]
        greet(others + [{"dp": in_pair(place, bit)[0]} for bit in bits])
        load_ffn().wait()
        run_step(ffn_plans, 0)
        out_near[0] = outg_ref[1]
        out_near[1] = outg_ref[3]
        out_steps[0]().start()
        small[0] = small_ref[...]
        tensor_small[0]().start()
        size = own_rows // CHUNKS
        for j, block in enumerate(blocks):
            for c in range(CHUNKS):
                where = slice(j * own_rows + c * size, j * own_rows + (c + 1) * size)
                pair = block[c, :size, :]
                ones = [pair[:, :HEAD_DIM], pair[:, HEAD_DIM:], side_by_side(block[c, size:, :])]
                for h, one in enumerate(ones):
                    grads[h, where, :] = jnp.concatenate([one, jnp.zeros_like(one)], axis=1)
        packed[...] = jnp.zeros_like(packed)
        wide[...] = jnp.zeros_like(wide)
        for h in range(heads):
            for c, scale in enumerate((0.125, 1.0, 1.0)):
                one = w_ref[c, h * HEAD_DIM : (h + 1) * HEAD_DIM, :] * scale
                wide[h, c * LANES : c * LANES + HEAD_DIM, :] = one

    queries = q_ref[0]
    slopes = grads[head]
    inner = -jnp.sum(slopes[:, :HEAD_DIM].astype(F32) * ctx_ref[0], axis=1, keepdims=True)
    slopes = slopes + in_lane((rows, LANES), 1, split_three(inner)).astype(BF16)
    keys_t[...] = k_ref[0].T

    def over_keys(first, last, query_grad):
        for start in range(first, last, key_block):
            span = slice(start, start + key_block)
            weights = jnp.exp(dot_cols(k_ref[0, span, :], queries))
            grad_weights = dot_cols(v_ref[0, span, :], slopes)
            grad_scores = (weights * grad_weights).astype(BF16)
            step = dot(keys_t[:, span], grad_scores)
            query_grad = step if query_grad is None else query_grad + step
            key_grad = dot(grad_scores, queries)[:, :HEAD_DIM]
            packed[span, LANES : LANES + HEAD_DIM] = key_grad.astype(BF16)
            value_grad = dot(weights.astype(BF16), slopes)[:, :HEAD_DIM]
            packed[span, 2 * LANES : 2 * LANES + HEAD_DIM] = value_grad.astype(BF16)
        return query_grad

    def at(which):
        return pl.when(head == which)

    quarter = rows // 4
    query_grad = over_keys(0, quarter, None)

    @at(1)
    def _():
        run_step(ffn_plans, 2)

    query_grad = over_keys(quarter, 2 * quarter, query_grad)

    @at(0)
    def _():
        load_x().wait()
        run_step(ffn_plans, 1)
        out_steps[0]().wait_recv()
        out_far[...] = (outg_ref[2].astype(F32) + out_near_land[1].astype(F32)).astype(BF16)
        out_steps[1]().start()
        tensor_small[0]().wait_recv()
        small[2] = small[0] + small[1]
        tensor_small[1]().start()

    @at(1)
    def _():
        run_step(early_plans, 1)

    @at(2)
    def _():
        run_step(ffn_plans, 4)
        run_step(early_plans, 3)
        run_step(middle_plans, 1)

    query_grad = over_keys(2 * quarter, rows, query_grad)
    packed[:, :HEAD_DIM] = query_grad[:HEAD_DIM].T.astype(BF16)
    sums = jnp.sum(packed[...].astype(F32), axis=0, keepdims=True)
    small[4 + head, 0:1, : 3 * LANES] = sums
    weight_grad = dot_rows(packed[...], x_ref[...])
    slot = jnp.where(head == 0, 0, head_cols + head * head_cols)
    for c, factor in enumerate((0.125, 1.0, 1.0)):
        target = pl.multiple_of(slot + c * HEAD_DIM, HEAD_DIM)
        late_in[pl.ds(target, HEAD_DIM), :] = (
            weight_grad[c * LANES : c * LANES + HEAD_DIM] * factor
        ).astype(BF16)

    @pl.when(head == 0)
    def _():
        out_steps[1]().wait_recv()
        late_in[head_cols : 2 * head_cols, :] = (
            outg_ref[0].astype(F32)
            + out_near_land[0].astype(F32)
            + out_far_land[...].astype(F32)
        ).astype(BF16)
        tensor_small[1]().wait_recv()
        run_step(early_plans, 0)

    @pl.when(head == 1)
    def _():
        run_step(middle_plans, 0)
        run_step(ffn_plans, 3)
        run_step(early_plans, 2)

    @pl.when(head == 2)
    def _():
        run_step(last_plans, 0)
        small_in[0, :8, :] = small[2] + small[3]
        small_in[0, UP_ROW : UP_ROW + 1, :] = small_ref[UP_ROW : UP_ROW + 1, :]
        small_in[0, 8:, :] = jnp.zeros((8, width), F32)
        for h in range(heads):
            small_in[0, 8 + h : 9 + h, : 3 * LANES] = small[4 + h, 0:1, : 3 * LANES]
        small_steps[0]().start()

    for j in (3, 2, 1, 0):
        step = dot(packed[part(j), :], wide[head])
        total[part(j), :] = jnp.where(head == 0, step, total[part(j), :] + step)
        if j % 2:

            @pl.when(head == heads - 1)
            def _(j=j):
                gx_near[j // 2] = total[part(j), :].astype(BF16)
                gx_steps[1 - j // 2]().start()

    @pl.when(head == heads - 1)
    def _():
        run_step(last_plans, 1)
        gx_steps[0]().wait_recv()
        gx_far[...] = (total[part(2), :] + gx_near_land[1].astype(F32)).astype(BF16)
        gx_steps[2]().start()
        gx_steps[1]().wait_recv()
        total[part(0), :] = total[part(0), :] + gx_near_land[0].astype(F32)
        gx_write = pltpu.make_async_copy(total.at[part(0)], gx_out, write_sem.at[0])
        gx_write.start()
        run_step(early_plans, 4)
        run_step(middle_plans, 2)
        for index in range(1, 2 * len(bits) + 1):
            if index > 1:
                run_step(last_plans, index)
            if index <= len(bits):
                small_steps[index - 1]().wait_recv()
                arrived = small_in[index - 1] + small_land[index - 1]
                if index < len(bits):
                    small_in[index] = arrived
                    small_steps[index]().start()
                else:
                    small_out[...] = arrived
            run_step(middle_plans, 2 + index)
            run_step(early_plans, 4 + index)
        for index in range(5, 2 * len(bits) + 1):
            run_step(ffn_plans, index)
        ffn_write = pltpu.make_async_copy(ffn, ffn_out, write_sem.at[1])
        ffn_write.start()
        late_write = pltpu.make_async_copy(late, late_out, write_sem.at[2])
        late_write.start()
        gx_steps[2]().wait_recv()
        far_write = pltpu.make_async_copy(gx_far_land, gxfar_out, write_sem.at[3])
        far_write.start()
        shared = small[2, LOSS_ROW : LOSS_ROW + 1, :] + small[3, LOSS_ROW : LOSS_ROW + 1, :]
        small_out[LOSS_ROW : LOSS_ROW + 1, :] = shared
        for copy in small_steps + tensor_small + out_steps + gx_steps:
            copy().wait_send()
        for copy in (gx_write, ffn_write, late_write, far_write):
            copy.wait()


def attend_backward(qkv, context, source, weight, blocks, ffn_grads, out_grads, small):
    rows, width = source.shape
    own_rows, head_cols = rows // len(blocks), weight.shape[1]
    cols = 3 * LANES
    heads = head_cols // HEAD_DIM
    levels = (lax.axis_size("dp") - 1).bit_length()
    ffn_rows, late_rows = 2 * ffn_grads.shape[0], (heads + 1) * head_cols
    landing = ffn_rows + late_rows + 8 * 48 * levels
    transfers = 2 * 4 * 2 * levels + levels + 7
    array = jax.ShapeDtypeStruct
    whole = lambda *shape: pl.BlockSpec(shape, lambda h: (0,) * len(shape))
    head_block = lambda *shape: pl.BlockSpec((1,) + shape, lambda h: (h, 0, 0))
    anywhere = pl.BlockSpec(memory_space=pl.ANY)
    return pl.pallas_call(
        functools.partial(backward_kernel, key_block=256),
        grid=(heads,),
        in_specs=[
            head_block(rows, LANES),
            head_block(rows, LANES),
            head_block(rows, LANES),
            head_block(rows, HEAD_DIM),
            anywhere,
            whole(*weight.shape),
        ]
        + [whole(*block.shape) for block in blocks]
        + [anywhere, whole(*out_grads.shape), whole(*small.shape)],
        out_specs=[
            anywhere,
            anywhere,
            whole(16, width),
            anywhere,
            anywhere,
        ],
        out_shape=[
            array((ffn_rows, width), BF16),
            array((late_rows, width), BF16),
            array((16, width), F32),
            array((own_rows, width), F32),
            array((own_rows, width), BF16),
        ],
        scratch_shapes=[
            pltpu.VMEM((heads, rows, LANES), BF16),
            pltpu.VMEM((heads, cols, width), BF16),
            pltpu.VMEM((rows, cols), BF16),
            pltpu.VMEM((LANES, rows), BF16),
            pltpu.VMEM((rows, width), F32),
            pltpu.VMEM((ffn_rows // 2, width), BF16),
            pltpu.VMEM((ffn_rows, width), BF16),
            pltpu.VMEM((late_rows, width), BF16),
            pltpu.VMEM((late_rows, width), BF16),
            pltpu.VMEM((4 + heads, 8, width), F32),
            pltpu.VMEM((levels, 16, width), F32),
            pltpu.VMEM((landing, width), BF16),
            pltpu.VMEM((levels, 16, width), F32),
            pltpu.VMEM((2, head_cols, width), BF16),
            pltpu.VMEM((2, head_cols, width), BF16),
            pltpu.VMEM((head_cols, width), BF16),
            pltpu.VMEM((head_cols, width), BF16),
            pltpu.VMEM((2, own_rows, width), BF16),
            pltpu.VMEM((2, own_rows, width), BF16),
            pltpu.VMEM((own_rows, width), BF16),
            pltpu.VMEM((own_rows, width), BF16),
            pltpu.VMEM((rows, width), BF16),
            pltpu.SemaphoreType.DMA((transfers,)),
            pltpu.SemaphoreType.DMA((transfers,)),
            pltpu.SemaphoreType.DMA((4,)),
        ],
        compiler_params=pltpu.CompilerParams(
            collective_id=4, has_side_effects=True, vmem_limit_bytes=62 * 2**20
        ),
        cost_estimate=pl.CostEstimate(
            flops=60 * heads * rows * rows * HEAD_DIM,
            bytes_accessed=2 * rows * heads * (cols + 7 * LANES),
            transcendentals=heads * rows * rows,
        ),
        name="attention_backward",
    )(*qkv, context, source, weight, *blocks, ffn_grads, out_grads, small)


def stacked(block):
    half = block.shape[0] // 2
    return jnp.concatenate([block[:half], block[half:]], axis=1)


def side_by_side(block):
    return jnp.concatenate([block[:, :HEAD_DIM], block[:, HEAD_DIM:]], axis=0)


(OUT_BIAS, GAIN_1, SHIFT_1, DOWN_BIAS, GAIN_2, SHIFT_2, UP_BIAS) = range(7)
T_VECTORS = 7
LOSS_ROW, UP_ROW = 6, 7


def middle_kernel(
    x_ref, ca0, ca1, ca2, ca3, tc_ref, ta0, ta1, ta2, ta3, outs0, outs1, outs2, outs3, w_up, s_down, vec,
    pack_own, pack_near, piece_a, piece_b, piece_c, next_a, sums_ref,
    out_ref, gh_ref, kept_ref, outg_ref, g0_ref, g1_ref, g2_ref, g3_ref, small_ref, piece_d, next_b, next_c, next_d,
    tc1, tc2, tcf, tc3, y_all, g_all, slope, hid, gu_all, t_out, first, normed, two, inv,
    part0, part2, send1, send2, send3, near0, near2, far0, gs, gr, packs, ffn_ref, ffn_land, w_outs, w_down,
    send_sem, recv_sem, pack_sem,
):
    near_id, far_id = neighbours()
    own_rows, width = x_ref.shape
    hidden = s_down.shape[0]
    head_cols = ca0.shape[1]
    size = own_rows // CHUNKS
    chunks = [slice(c * size, (c + 1) * size) for c in range(CHUNKS)]
    tiles = [slice(n, n + 256) for n in range(0, hidden, 256)]
    group = lambda j: slice(j * head_cols, (j + 1) * head_cols)
    outs = (outs0, outs1, outs2, outs3)
    w_out = lambda j: w_outs[j]
    tw_out = lambda j: outs[j][head_cols:, :]
    row = lambda index: vec[index : index + 1, :]

    place = lax.axis_index("dp")
    others = [{"tensor": near_id}, {"tensor": far_id}]
    others += [{"dp": in_pair(place, bit)[0]} for bit in dp_bits()[0][:2]]
    greet(others)

    count = [0]
    started = []

    def put(source, target, device, axis="tensor"):
        index = count[0]
        count[0] += 1
        copy = pltpu.make_async_remote_copy(
            src_ref=source,
            dst_ref=target,
            send_sem=send_sem.at[index],
            recv_sem=recv_sem.at[index],
            device_id={axis: device},
            device_id_type=pl.DeviceIdType.MESH,
        )
        copy.start()
        started.append(copy)
        return copy

    t_far = put(tc_ref.at[2], tc2, far_id)
    t_pass = put(tc_ref.at[3], tcf, far_id)
    t_near = put(tc_ref.at[1], tc1, near_id)
    next_id, level = in_pair(place, 2)
    cut = piece_a.shape[0]
    here = pl.ds(pl.multiple_of(level * cut, 16), cut)
    there = pl.ds(pl.multiple_of((1 - level) * cut, 16), cut)
    next_copies = [
        put(next_a, next_c, near_id),
        put(piece_b, next_b, next_id, "dp"),
        put(piece_b, piece_d, near_id),
    ]

    pack_refs = [pack_own.at[0], pack_own.at[1], pack_near.at[0], pack_near.at[1]]
    pack_refs += [(piece_a, next_a), (piece_c, next_c), (piece_b, next_b), (piece_d, next_d)]

    def load_pack(index):
        slot = index % 2
        source, target = pack_refs[index], packs.at[slot]
        if not isinstance(source, tuple):
            return [pltpu.make_async_copy(source, target, pack_sem.at[slot])]
        return [
            pltpu.make_async_copy(source[0], target.at[here], pack_sem.at[slot]),
            pltpu.make_async_copy(source[1], target.at[there], pack_sem.at[2 + slot]),
        ]

    def start_pack(index):
        for copy in load_pack(index):
            copy.start()

    start_pack(0)
    a_out = (sums_ref[0:1, :] * (1.0 / width)).astype(BF16)
    a_down = (sums_ref[1:2, :] * (1.0 / (lax.axis_size("tensor") * hidden))).astype(BF16)
    for j in range(4):
        w_outs[j] = outs[j][:head_cols, :] * a_out
    w_down[...] = s_down[...] * a_down
    small_ref[...] = jnp.zeros_like(small_ref)

    def add_small(index, values):
        small_ref[index : index + 1, :] += jnp.sum(values, axis=0, keepdims=True)

    def share(own_block, where):
        return (
            put(own_block.at[0, where], own_block.at[1, where], near_id),
            put(own_block.at[0, where], own_block.at[2, where], far_id),
        )

    y_sent = []
    for rows in chunks:
        attn = dot(ca0[rows, :], w_out(0)) + dot(ca1[rows, :], w_out(1))
        attn += dot(ca2[rows, :], w_out(2)) + dot(ca3[rows, :], w_out(3))
        y_one, y_normed, y_inv = norm_forward(
            x_ref[rows, :].astype(F32) + attn + row(OUT_BIAS), row(GAIN_1), row(SHIFT_1)
        )
        first[rows, :] = y_one
        normed[rows, :] = y_normed
        inv[rows, :] = jnp.broadcast_to(y_inv, (size, LANES))
        y_all[0, rows, :] = clip_act(y_one).astype(BF16)
        y_sent.append(share(y_all, rows))

    def forward_block(j, rows):
        total = None
        for cols in tiles:
            upward = dot(y_all[j, rows, :], w_up[:, cols]) + row(UP_BIAS)[:, cols]
            cdf, bell = normal_parts(upward)
            level = jnp.tanh(upward * cdf * (1.0 / CLIP_RANGE))
            act = (CLIP_RANGE * level).astype(BF16)
            hid[j, rows, cols] = act
            slope[j, rows, cols] = (1.0 - level * level) * (
                cdf + upward * bell * 0.3989422804014327
            )
            step = dot(act, w_down[cols, :])
            total = step if total is None else total + step
        return total

    def backward_block(j, rows):
        total = None
        for cols in tiles:
            grad = dot_cols(g_all[j, rows, :], w_down[cols, :])
            grad = (grad * slope[j, rows, cols]).astype(BF16)
            gu_all[j, rows, cols] = grad
            small_ref[UP_ROW : UP_ROW + 1, cols] += jnp.sum(
                grad.astype(F32), axis=0, keepdims=True
            )
            step = dot_cols(grad, w_up[:, cols])
            total = step if total is None else total + step
        return total

    def near_blocks(work, sent):
        copies = []
        for rows in chunks:
            part0[rows, :] = work(0, rows)
        for rows, (near, _) in zip(chunks, sent):
            near.wait_recv()
            send1[rows, :] = work(1, rows).astype(BF16)
            copies.append(put(send1.at[rows], near0.at[rows], near_id))
        return copies

    def far_blocks(block, work, sent, between=()):
        copies = []
        for c, (rows, (_, far)) in enumerate(zip(chunks, sent)):
            far.wait_recv()
            passed = put(block.at[2, rows], block.at[3, rows], near_id)
            part2[rows, :] = work(2, rows)
            passed.wait_recv()
            send3[rows, :] = work(3, rows).astype(BF16)
            met = put(send3.at[rows], near2.at[rows], near_id)
            met.wait_recv()
            send2[rows, :] = (part2[rows, :] + near2[rows, :].astype(F32)).astype(BF16)
            copies.append(put(send2.at[rows], far0.at[rows], far_id))
            if between:
                between[c]()
        return copies

    def summed(rows, near, far):
        near.wait_recv()
        far.wait_recv()
        return part0[rows, :] + near0[rows, :].astype(F32) + far0[rows, :].astype(F32)

    y_near = near_blocks(forward_block, y_sent)

    t_pass.wait_recv()
    t_last = put(tcf, tc3, near_id)
    t_near.wait_recv()
    t_far.wait_recv()
    t_row = lambda index: row(T_VECTORS + index)
    t_last.wait_recv()
    t_attn = None
    for j, (wide, last) in enumerate(zip((ta0, ta1, ta2, ta3), (tc_ref.at[0], tc1, tc2, tc3))):
        both = jnp.concatenate([wide[...], side_by_side(last[...])], axis=1)
        step = dot(both, tw_out(j))
        t_attn = step if t_attn is None else t_attn + step
    t_one, _, _ = norm_forward(x_ref[...].astype(F32) + t_attn + t_row(0), t_row(1), t_row(2))
    two[...] = t_one
    t_out[...] = t_one + t_row(3)
    half = hidden // 2
    t_in = t_one.astype(BF16)

    def teacher_packs(first, last):
        for index in range(first, last):
            slot = index % 2
            if index == 4:
                next_copies[0].wait_recv()
                next_copies[1].wait_recv()
                next_copies.append(put(next_b, next_d, near_id))
            if index == 6:
                next_copies[2].wait_recv()
                next_copies[3].wait_recv()
            if index + 1 < len(pack_refs):
                start_pack(index + 1)
            for copy in load_pack(index):
                copy.wait()
            upward = dot_cols(t_in, packs[slot, :half, :])
            upward = upward + packs[slot, hidden : hidden + 1, :half].astype(F32)
            act = (upward * normal_parts(upward)[0]).astype(BF16)
            t_out[...] += dot(act, packs[slot, half:hidden, :])

    middle_pack = len(pack_refs) // 2
    between = [
        functools.partial(teacher_packs, 0, middle_pack),
        functools.partial(teacher_packs, middle_pack, len(pack_refs)),
    ]
    y_far = far_blocks(y_all, forward_block, y_sent, between)
    t_out[...] = norm_forward(t_out[...], t_row(4), t_row(5))[0]

    g_sent = []
    earlier = list(started)
    started.clear()
    for rows, near, far in zip(chunks, y_near, y_far):
        ffn = summed(rows, near, far)
        out, n_two, inv_two = norm_forward(
            first[rows, :] + ffn + row(DOWN_BIAS), row(GAIN_2), row(SHIFT_2)
        )
        out_ref[rows, :] = out.astype(BF16)
        gap = out - t_out[rows, :]
        add_small(LOSS_ROW, gap * gap)
        add_small(GAIN_2, gap * n_two)
        add_small(SHIFT_2, gap)
        grad_two = norm_backward(gap, n_two, inv_two, row(GAIN_2))
        two[rows, :] = grad_two
        grad_ffn = grad_two.astype(BF16)
        add_small(DOWN_BIAS, grad_ffn.astype(F32))
        g_all[0, rows, :] = grad_ffn
        g_sent.append(share(g_all, rows))

    for copy in earlier:
        copy.wait_send()
    g_near = near_blocks(backward_block, g_sent)
    g_far = far_blocks(g_all, backward_block, g_sent)
    flat = lambda block: block[...].reshape(4 * own_rows, block.shape[2])

    def weight_gradients():
        ffn_ref[:width, :] = dot_rows(flat(y_all), flat(gu_all)).astype(BF16)
        ffn_ref[width:, :] = dot_rows(flat(hid), flat(g_all)).astype(BF16)
        sent, taken = [], 0
        for (low, count), order in zip(split_rows(0, width + hidden), dp_bits()):
            partner, digit = in_pair(place, order[0])
            count = count // 2
            give = ffn_ref.at[pl.ds(pl.multiple_of(low + (1 - digit) * count, 16), count)]
            keep = pl.multiple_of(low + digit * count, 16)
            land = ffn_land.at[taken : taken + count]
            sent.append((put(give, land, partner, "dp"), (keep, count)))
            taken += count
        return sent

    passes = []
    for c, (rows, near, far) in enumerate(zip(chunks, g_near, g_far)):
        y_one = first[rows, :]
        grad_one = two[rows, :] + summed(rows, near, far) * clip_slope(y_one)
        n_one = normed[rows, :]
        add_small(GAIN_1, grad_one * n_one)
        add_small(SHIFT_1, grad_one)
        grad_h = norm_backward(grad_one, n_one, inv[rows, :1], row(GAIN_1))
        gh_ref[rows, :] = grad_h
        grad_attn = grad_h.astype(BF16)
        add_small(OUT_BIAS, grad_attn.astype(F32))
        for j, ca in enumerate((ca0.at[rows], ca1.at[rows], ca2.at[rows], ca3.at[rows])):
            act = ca[...]
            level = act.astype(F32) * (1.0 / CLIP_RANGE)
            grad = dot_cols(grad_attn, w_out(j)) * (1.0 - level * level)
            grad = grad.astype(BF16)
            gs[j, c, :size, :] = grad[:, :LANES]
            gs[j, c, size:, :] = stacked(grad[:, LANES:])
            step = dot_rows(act, grad_attn)
            if c:
                step = step + part2[group(j), :]
            part2[group(j), :] = step
        passes.append(
            (
                put(gs.at[3, c], gr.at[3, c], far_id),
                put(gs.at[2, c], gr.at[1, c], far_id),
                put(gs.at[1, c], gr.at[0, c], near_id),
            )
        )
        if c == 0:
            halves = weight_gradients()
    g0_ref[...] = gs[0]
    for j in range(4):
        outg_ref[j] = part2[group(j), :].astype(BF16)
    lasts = []
    for c, (passing, _, _) in enumerate(passes):
        passing.wait_recv()
        lasts.append(put(gr.at[3, c], gr.at[2, c], near_id))
    for c, ((_, far, near), last) in enumerate(zip(passes, lasts)):
        near.wait_recv()
        g1_ref[c] = gr[0, c]
        far.wait_recv()
        g2_ref[c] = gr[1, c]
        last.wait_recv()
        g3_ref[c] = gr[2, c]
    taken = 0
    for copy, (keep, part_size) in halves:
        copy.wait_recv()
        land = slice(taken, taken + part_size)
        mine = ffn_ref[pl.ds(keep, part_size), :].astype(F32)
        kept_ref[land, :] = (mine + ffn_land[land, :].astype(F32)).astype(BF16)
        taken += part_size
    for copy in started:
        copy.wait_send()


def middle(x_own, cas, tcs, outs, w_up, s_down, vectors, packs, sums):
    own_rows, width = x_own.shape
    hidden = s_down.shape[0]
    head_cols = cas[0].shape[1]
    array = jax.ShapeDtypeStruct
    vmem = pl.BlockSpec(memory_space=pltpu.VMEM)
    transfers = 8 + 4 * 3 * CHUNKS + 4 * CHUNKS + 2
    packed = (CHUNKS, own_rows // CHUNKS * 3 // 2, LANES)
    four_outs = pltpu.VMEM((4, head_cols, width), BF16)
    square = lambda kind: pltpu.VMEM((own_rows, width), kind)
    four = lambda cols, kind: pltpu.VMEM((4, own_rows, cols), kind)
    return pl.pallas_call(
        middle_kernel,
        in_specs=[vmem] * 17 + [pl.BlockSpec(memory_space=pl.ANY)] * 6 + [vmem],
        out_specs=[vmem] * 9 + [pl.BlockSpec(memory_space=pl.ANY)] * 4,
        out_shape=[
            array((own_rows, width), BF16),
            array((own_rows, width), F32),
            array(((width + hidden) // 2, width), BF16),
            array((4, head_cols, width), BF16),
        ]
        + [array(packed, BF16)] * 4
        + [array((8, width), F32)]
        + [array(packs[2].shape, BF16)] * 4,
        scratch_shapes=[pltpu.VMEM(tcs[0].shape[1:], BF16)] * 4
        + [four(width, BF16), four(width, BF16), four(hidden, F32), four(hidden, BF16)]
        + [four(hidden, BF16)]
        + [square(F32)] * 4
        + [pltpu.VMEM((own_rows, LANES), F32)]
        + [square(F32), pltpu.VMEM((4 * max(own_rows // 4, head_cols), width), F32)]
        + [square(BF16)] * 6
        + [pltpu.VMEM((4,) + packed, BF16)] * 2
        + [
            pltpu.VMEM(packs[0].shape, BF16),
            pltpu.VMEM((width + hidden, width), BF16),
            pltpu.VMEM(((width + hidden) // 2, width), BF16),
            four_outs,
            pltpu.VMEM(s_down.shape, BF16),
            pltpu.SemaphoreType.DMA((transfers,)),
            pltpu.SemaphoreType.DMA((transfers,)),
            pltpu.SemaphoreType.DMA((4,)),
        ],
        compiler_params=pltpu.CompilerParams(
            collective_id=3, has_side_effects=True, vmem_limit_bytes=62 * 2**20
        ),
        cost_estimate=pl.CostEstimate(
            flops=120 * own_rows * width * hidden, bytes_accessed=2**25, transcendentals=2**22
        ),
        name="middle",
    )(x_own, *cas, *tcs, *outs, w_up, s_down, vectors, *packs, sums)


def finish_kernel(
    ffn_ref, late_ref, small_ref, gx_ref, gx_far_ref, gh_ref, x_ref, y_ref,
    up_ref, down_ref, qkv_ref, out_ref, input_ref, y_out, bias_ref, loss_ref, *vectors, tokens
):
    up_ref[...] = ffn_ref[0].astype(F32)
    down_ref[...] = ffn_ref[1].astype(F32)
    grad = gx_ref[...] + gx_far_ref[...].astype(F32)
    input_ref[...] = gh_ref[...] + grad * clip_slope(x_ref[...].astype(F32))
    y_out[...] = y_ref[...]

    @pl.when(pl.program_id(0) == 0)
    def _():
        cols = out_ref.shape[0]
        heads = cols // HEAD_DIM
        out_ref[...] = late_ref[cols : 2 * cols, :].astype(F32)
        for h in range(heads):
            first = 0 if h == 0 else cols + h * cols
            for c in range(3):
                rows = slice(first + c * HEAD_DIM, first + (c + 1) * HEAD_DIM)
                qkv_ref[c, h * HEAD_DIM : (h + 1) * HEAD_DIM, :] = late_ref[rows, :].astype(F32)
        for index, (lane, factor) in enumerate(((0, 0.125), (2 * LANES, 1.0))):
            parts = [small_ref[8 + h : 9 + h, lane : lane + HEAD_DIM] for h in range(heads)]
            bias_ref[index : index + 1, :] = jnp.concatenate(parts, axis=1) * factor
        for row, vector in zip((0, 1, 2, UP_ROW, 3, 4, 5), vectors):
            vector[...] = small_ref[row : row + 1, :].reshape(vector.shape)
        loss_ref[0] = jnp.sum(small_ref[LOSS_ROW : LOSS_ROW + 1, :]) * (1.0 / tokens)


def finish(ffn, late, small, gx, gx_far, grad_h, x_own, out_own, head_cols, tokens):
    own_rows, width = x_own.shape
    steps = 4
    array = jax.ShapeDtypeStruct
    whole = lambda *shape: pl.BlockSpec(shape, lambda i: (0,) * len(shape))
    by_rows = lambda rows: pl.BlockSpec((rows // steps, width), lambda i: (i, 0))
    hidden = ffn.shape[0] // 2
    return pl.pallas_call(
        functools.partial(finish_kernel, tokens=tokens),
        grid=(steps,),
        in_specs=[
            pl.BlockSpec((2, hidden // steps, width), lambda i: (0, i, 0)),
            whole(*late.shape),
            whole(*small.shape),
        ]
        + [by_rows(own_rows)] * 5,
        out_specs=[
            by_rows(hidden),
            by_rows(hidden),
            whole(3, head_cols, width),
            whole(head_cols, width),
            by_rows(own_rows),
            by_rows(own_rows),
            whole(2, head_cols),
            pl.BlockSpec(memory_space=pltpu.SMEM),
        ]
        + [whole(width)] * 7,
        out_shape=[
            array((hidden, width), F32),
            array((hidden, width), F32),
            array((3, head_cols, width), F32),
            array((head_cols, width), F32),
            array((own_rows, width), F32),
            array((own_rows, width), BF16),
            array((2, head_cols), F32),
            array((1,), F32),
        ]
        + [array((width,), F32)] * 7,
        compiler_params=pltpu.CompilerParams(vmem_limit_bytes=58 * 2**20),
        name="finish",
    )(ffn.reshape(2, hidden, width), late, small, gx, gx_far, grad_h, x_own, out_own)


def body(
    tokens,
    seg_lengths,
    parents,
    qkv_latent,
    qv_bias,
    out_latent,
    out_bias,
    norm1_gain,
    norm1_shift,
    up_latent,
    up_bias,
    down_latent,
    down_bias,
    norm2_gain,
    norm2_shift,
    teacher_qkv,
    teacher_qv_bias,
    teacher_out,
    teacher_out_bias,
    teacher_norm1_gain,
    teacher_norm1_shift,
    teacher_up,
    teacher_up_bias,
    teacher_down,
    teacher_down_bias,
    teacher_norm2_gain,
    teacher_norm2_shift,
):
    own_rows, model_width = tokens.shape
    group = lax.axis_size("tensor")
    me = lax.axis_index("tensor")
    all_rows = own_rows * group
    local_cols = qkv_latent.shape[2]
    blocks = [tokens, swap(tokens, 1), swap(tokens, 2)]
    qkv_latent, teacher_qkv = qkv_latent.transpose(1, 2, 0), teacher_qkv.transpose(1, 2, 0)
    latents = [qkv_latent, out_latent, teacher_out, up_latent, down_latent]
    latents += [teacher_up, teacher_down, teacher_up_bias]
    vectors = [out_bias, norm1_gain, norm1_shift, down_bias, norm2_gain, norm2_shift, up_bias]
    vectors += [teacher_out_bias, teacher_norm1_gain, teacher_norm1_shift]
    vectors += [teacher_down_bias, teacher_norm2_gain, teacher_norm2_shift]
    w_qkv, outs, w_up, s_down, pack, sums, vectors = prepare(latents, vectors)
    seg_lanes, blocked = segment_tables(seg_lengths[0], parents[0])
    base = jnp.stack([(me ^ j) * own_rows for j in range(group)]).astype(jnp.int32)

    tables = (seg_lanes, blocked)
    *qkv, context, x_in_all, ca_own, ca_near, ca_far, sums, pack_near, piece_a, outs1, outs2 = attend_forward(
        base, blocks, w_qkv, qv_bias, *tables, [pack, outs, sums], True
    )
    t_last, ta0, ca1, ca2, _, ca3, ta1, ta2, _, ta3, outs3, next_a, piece_b, piece_c = attend_forward(
        base, blocks, teacher_qkv, teacher_qv_bias, *tables,
        [ca_near, ca_far, outs2, piece_a], False,
    )
    cas, outs = [ca_own, ca1, ca2, ca3], [outs, outs1, outs2, outs3]
    packs = [pack, pack_near, piece_a, piece_b, piece_c, next_a]
    out_own, grad_h, ffn_grads, out_grads, g0, g1, g2, g3, small, *_ = middle(
        tokens, cas, [t_last, ta0, ta1, ta2, ta3], outs, w_up, s_down, vectors, packs, sums
    )
    ffn_grads, late, small, gx_own, gx_far = attend_backward(
        qkv, context, x_in_all, w_qkv, [g0, g1, g2, g3], ffn_grads, out_grads, small
    )
    up_grad, down_grad, qkv_grad, out_grad, input_grad, out_own, bias_grad, loss, *vectors = finish(
        ffn_grads, late, small, gx_own, gx_far, grad_h, tokens, out_own, local_cols,
        all_rows * model_width,
    )
    return (
        out_own,
        loss,
        input_grad,
        qkv_grad.transpose(2, 0, 1),
        bias_grad,
        out_grad,
        *vectors[:3],
        up_grad,
        vectors[3],
        down_grad,
        *vectors[4:],
    )


def solution(mesh):
    rows, cols = ("dp", "tensor"), "tensor"
    vec = P()
    params = (
        P(None, None, cols),
        P(None, cols),
        P(cols, None),
        vec,
        vec,
        vec,
        P(None, cols),
        P(cols),
        P(cols, None),
        vec,
        vec,
        vec,
    )
    in_specs = (P(rows, None), P("dp", None), P("dp", None)) + params + params
    out_specs = (P(rows, None), P("dp"), P(rows, None)) + params
    return jax.shard_map(body, mesh=mesh, in_specs=in_specs, out_specs=out_specs, check_vma=False)
```
